256 devices in a mesh: rows: 128 (over z, x, y), cols: 2 (over core).
Axes of the slice: x: 4, y: 4, z: 8, core: 2. Of those that a mesh axis runs over, the one named last changes fastest.
Arguments:
- vectors: float32 [64, 393216], P('cols', 'rows'), may hold values from -45 to 45
- directions: float32 [64, 393216], P('cols', 'rows'), may hold values from -6 to 6
- affinity: float32 [3072, 6, 128, 128], P('rows'), may hold values from 0.01 to 1, as said below
- pattern: int32 [3072, 6], P('rows'), may hold values from 0 to 3071, as said below
- rotation: float32 [192, 64], replicated, may hold values from -0.4375 to 0.4375
Outputs:
- new_vectors: float32 [64, 393216], P('cols', 'rows')
- new_directions: float32 [64, 393216], P('cols', 'rows')
- ritz_matrix: float32 [192, 192], replicated
The draws below stay inside these ranges and needn't reach their ends.
Inputs may be any that keep to these rules, and one draw needn't show every extreme that they name: Block row i has pattern[i, 0] = i; its 6 indices are distinct, block j appears in row i exactly when block i appears in row j, and each lies, modulo 3072, among the block rows of its own index of rows and of the two indices beside it (the first and last indices count as beside each other). The affinity matrix is symmetric as the steps state.
All inputs are finite; a program needn't handle non-finite values.
Results may differ from the reference program's by a relative error of at most 0.0015.
Values sent between devices are 32-bit elements; how exact they have to be, the bound alone decides.
No kernel may reach another device: no remote copies, remote signals or barrier semaphores. Data moves between devices by JAX's collectives and lax.ppermute only.
A program may use at most 64 MiB of HBM per device.

```python
import math
import jax
import jax.numpy as jnp
from jax import lax

K = 64
BLK = 128
NNZB = 6
BPD = 24
NBLK = 3072
NODES = 393216


def shared_pattern(key):
    first_key = jax.random.fold_in(key, 101)
    second_key = jax.random.fold_in(key, 102)
    third_key = jax.random.fold_in(key, 103)
    near = jax.random.randint(first_key, (), 2, BPD + 1, dtype=jnp.int32)
    step = jax.random.randint(second_key, (), 1, BPD - 1, dtype=jnp.int32)
    far = 2 + (near - 2 + step) % (BPD - 1)
    block_rows = jnp.arange(NBLK, dtype=jnp.int32)
    partner = jnp.bitwise_xor(block_rows, 1)
    columns = [block_rows, partner, (block_rows + near) % NBLK, (block_rows - near + NBLK) % NBLK, (block_rows + far) % NBLK, (block_rows - far + NBLK) % NBLK]
    table = jnp.stack(columns, axis=1).astype(jnp.int32)
    owners = NBLK // BPD
    owner_ids = jnp.arange(owners, dtype=jnp.int32)
    shuffles = jax.vmap(lambda owner: jax.random.permutation(jax.random.fold_in(third_key, owner), BPD).astype(jnp.int32))(owner_ids)
    relabel = (owner_ids[:, None] * BPD + shuffles).reshape(-1).astype(jnp.int32)
    undo = jnp.zeros((NBLK,), jnp.int32).at[relabel].set(block_rows)
    return relabel[table][undo].astype(jnp.int32)


def draw_pattern(key, part):
    table = shared_pattern(key)
    return table


def draw_affinity(key, part):
    table = shared_pattern(key)
    key = jax.random.fold_in(key, 13)
    block_rows = jnp.broadcast_to(jnp.arange(NBLK, dtype=jnp.int32)[:, None], (NBLK, NNZB)).reshape(-1)
    others = table.reshape(-1)
    smaller = jnp.minimum(block_rows, others)
    larger = jnp.maximum(block_rows, others)
    pair_id = smaller * NBLK + larger

    def one_block(pair, row, other):
        pair_key = jax.random.fold_in(key, pair)
        low = jnp.log(jnp.float32(0.01))
        draw = jnp.exp(jax.random.uniform(pair_key, (BLK, BLK), jnp.float32, low, 0.0))
        mirrored = jnp.where(row > other, draw.T, draw)
        return jnp.where(row == other, 0.5 * (draw + draw.T), mirrored)
    blocks = jax.vmap(one_block)(pair_id, block_rows, others)
    return blocks.reshape(NBLK, NNZB, BLK, BLK)


def draw_vectors(key, part):
    key = jax.random.fold_in(key, 17)
    freq_key = jax.random.fold_in(key, 1)
    phase_key = jax.random.fold_in(key, 2)
    weight_key = jax.random.fold_in(key, 3)
    noise_key = jax.random.fold_in(key, 4)
    position = jnp.arange(NODES, dtype=jnp.float32) / jnp.float32(NODES)
    freq = jax.random.randint(freq_key, (K, 1), 1, 3, dtype=jnp.int32).astype(jnp.float32)
    phase = jax.random.uniform(phase_key, (K, 1), jnp.float32, -math.pi, math.pi)
    weight = jax.random.uniform(weight_key, (K, 1), jnp.float32, 0.5, 1.5)
    noise = jax.random.truncated_normal(noise_key, -4.0, 4.0, (K, NODES), jnp.float32)
    amplitude = 1.0 + 3.0 * position
    smooth = 3.0 * (1.0 - position)
    wave = 1.4142135 * jnp.cos(2.0 * math.pi * freq * position[None, :] + phase)
    return amplitude[None, :] * (weight * smooth[None, :] * wave + noise)


def shard_levels(key, dims, cuts, smallest, top_value):
    def one(dim, parts):
        steps = jax.random.uniform(jax.random.fold_in(jax.random.fold_in(key, 6), dim), (parts,), jnp.float32, smallest / len(cuts), top_value / len(cuts))
        return jnp.repeat(jnp.exp(steps), dims[dim] // parts).reshape((-1,) + (1,) * (len(dims) - dim - 1))

    level = one(*cuts[0])
    for cut in cuts[1:]:
        level = level * one(*cut)
    return level


def bell_draw(own_key, dims, spread, reach, cuts=(), kind=jnp.bfloat16):
    entries = spread * jax.random.normal(own_key, dims, jnp.float32)
    if cuts:
        entries = entries * shard_levels(own_key, dims, cuts, -0.22, 0.18)
    return jnp.clip(entries, -reach, reach).astype(kind)


def setup_inputs(seed: int = 0) -> dict:
    key_of = jax.random.split(jax.random.key(seed), 6)
    vectors = draw_vectors(jax.random.fold_in(key_of[5], 71), 0)
    directions = bell_draw(key_of[1], (K, NODES), 1.0, 6.0, ((0, 2), (1, 128)), jnp.float32)
    affinity = draw_affinity(jax.random.fold_in(key_of[5], 71), 0)
    pattern = draw_pattern(jax.random.fold_in(key_of[5], 71), 0)
    rotation = bell_draw(key_of[4], (3 * K, K), (3 * K) ** -0.5, 0.4375, (), jnp.float32)
    return dict(vectors=vectors, directions=directions, affinity=affinity, pattern=pattern, rotation=rotation)


def apply_laplace(panel, affinity, pattern, scale):
    count = panel.shape[0]
    nblk = affinity.shape[0]
    scaled = (scale[None, :] * panel).reshape(count, nblk, BLK)
    picked = scaled[:, pattern]
    image = jnp.einsum('cikn,ikmn->cim', picked, affinity, precision=lax.Precision.HIGHEST)
    return panel - scale[None, :] * image.reshape(count, -1)

def reference(vectors, directions, affinity, pattern, rotation):
    scale = lax.rsqrt(lax.optimization_barrier(jnp.sum(affinity, axis=(1, 3))).reshape(-1))
    image_x = apply_laplace(vectors, affinity, pattern, scale)
    image_p = apply_laplace(directions, affinity, pattern, scale)
    quotient = lax.optimization_barrier(jnp.sum(vectors * image_x, axis=1)) / lax.optimization_barrier(jnp.sum(vectors * vectors, axis=1))
    residual = image_x - quotient[:, None] * vectors
    image_w = apply_laplace(residual, affinity, pattern, scale)
    panel = jnp.concatenate([residual, vectors, directions], axis=0)
    imaged = jnp.concatenate([image_w, image_x, image_p], axis=0)
    gram = jnp.dot(panel, panel.T, precision=lax.Precision.HIGHEST)
    raw = jnp.dot(panel, imaged.T, precision=lax.Precision.HIGHEST)
    lower = jnp.linalg.cholesky(gram)
    inverse = jax.scipy.linalg.solve_triangular(lower, jnp.eye(3 * K, dtype=jnp.float32), lower=True)
    ritz_matrix = jnp.dot(jnp.dot(inverse, raw, precision=lax.Precision.HIGHEST), inverse.T, precision=lax.Precision.HIGHEST)
    kept = jnp.concatenate([rotation[:K], jnp.zeros((K, K), jnp.float32), rotation[2 * K:]], axis=0)
    mixing = jnp.dot(inverse.T, rotation, precision=lax.Precision.HIGHEST)
    trailing = jnp.dot(inverse.T, kept, precision=lax.Precision.HIGHEST)
    factor = math.sqrt(NODES)
    new_vectors = factor * jnp.dot(mixing.T, panel, precision=lax.Precision.HIGHEST)
    new_directions = factor * jnp.dot(trailing.T, panel, precision=lax.Precision.HIGHEST)
    return (new_vectors, new_directions, ritz_matrix)
```

```python
import math

import jax
import jax.numpy as jnp
import numpy as np
from jax import lax
from jax.sharding import PartitionSpec as P

BLK = 128


def with_halo(x, sides, width):
    for axis, dim in sides:
        devices, length = (lax.axis_size(axis), x.shape[dim])
        up = [(i, (i + 1) % devices) for i in range(devices)]
        down = [(j, i) for i, j in up]
        last = lax.slice_in_dim(x, length - width, length, axis=dim)
        initial = lax.slice_in_dim(x, 0, width, axis=dim)
        before = lax.ppermute(last, axis, up)
        after = lax.ppermute(initial, axis, down)
        x = jnp.concatenate([before, x, after], axis=dim)
    return x


def exact_dot(left, right):
    return jnp.dot(left, right, precision=lax.Precision.HIGHEST)


def block_image(extended, panel, affinity, pattern, scale):
    count = panel.shape[0]
    local_blocks = affinity.shape[0]
    all_blocks = local_blocks * lax.axis_size("rows")
    first_block = (lax.axis_index("rows") - 1) * local_blocks
    local_index = (pattern - first_block + all_blocks) % all_blocks
    blocks = extended.reshape(count, 3 * local_blocks, BLK)
    picked = jnp.take(blocks, local_index, axis=1)
    image = jnp.einsum("cikn,ikmn->cim", picked, affinity, precision=lax.Precision.HIGHEST)
    return panel - scale[None, :] * image.reshape(count, -1)


def plane_groups():
    return [[z * 16 + i for i in range(16)] for z in range(8)]


def column_groups():
    return [[z * 16 + i for z in range(8)] for i in range(16)]


def exchange(x, groups):
    return lax.all_to_all(x, "rows", 0, 0, axis_index_groups=groups)


def sum_small(x):
    everyone = lax.all_to_all(jnp.broadcast_to(x[None], (128,) + x.shape), "rows", 0, 0)
    return jnp.sum(everyone, axis=0)


def sum_large(x):
    plane, column = plane_groups(), column_groups()
    part = jnp.sum(exchange(x, plane), axis=0)
    part = jnp.sum(exchange(jnp.broadcast_to(part[None], (8,) + part.shape), column), axis=0)
    return exchange(jnp.broadcast_to(part[None], (16,) + part.shape), plane)


def canonical_order(parts, width):
    total = width * parts
    listed = [
        panel_id * total + owner * width + column
        for owner in range(parts)
        for panel_id in range(3)
        for column in range(width)
    ]
    return np.array(listed, dtype=np.int32)


def local(vectors, directions, affinity, pattern, rotation):
    width = vectors.shape[0]
    rows_dev = vectors.shape[1]
    parts = lax.axis_size("cols")
    owner = lax.axis_index("cols")
    total = width * parts
    nodes = rows_dev * lax.axis_size("rows")
    scale = lax.rsqrt(jnp.sum(affinity, axis=(1, 3)).reshape(-1))
    paired = jnp.concatenate([vectors, directions], axis=0)
    spread = with_halo(scale[None, :] * paired, (("rows", 1),), rows_dev)
    paired_image = block_image(spread, paired, affinity, pattern, scale)
    image_x = paired_image[:width]
    image_p = paired_image[width:]
    sums = sum_small(
        jnp.concatenate([jnp.sum(vectors * image_x, axis=1), jnp.sum(vectors * vectors, axis=1)]).reshape(1, 2 * width)
    ).reshape(2, width)
    quotient = sums[0] / sums[1]
    second = image_x - quotient[:, None] * vectors
    beyond = with_halo(scale[None, :] * second, (("rows", 1),), rows_dev)
    second_image = block_image(beyond, second, affinity, pattern, scale)
    local_panel = jnp.concatenate([second, vectors, directions], axis=0)
    local_image = jnp.concatenate([second_image, image_x, image_p], axis=0)
    whole_panel, whole_image = (
        lax.all_gather(local_panel, "cols", axis=0, tiled=True),
        lax.all_gather(local_image, "cols", axis=0, tiled=True),
    )
    half_gram = exact_dot(local_panel, whole_panel.T)
    half_raw = exact_dot(local_panel, whole_image.T)
    both = jnp.concatenate([half_gram, half_raw], axis=0).reshape(16, 12, 6 * width)
    both = sum_large(both).reshape(6 * width, 6 * width)
    summed_gram, summed_raw = both[: 3 * width], both[3 * width :]
    gram_g, raw_g = (
        lax.all_gather(summed_gram, "cols", axis=0, tiled=True),
        lax.all_gather(summed_raw, "cols", axis=0, tiled=True),
    )
    order = canonical_order(parts, width)
    position = np.argsort(order).astype(np.int32)
    gram = gram_g[position][:, position]
    raw = raw_g[position][:, position]
    identity = jnp.eye(3 * total, dtype=jnp.float32)
    lower = jnp.linalg.cholesky(gram)
    inverse = jax.scipy.linalg.solve_triangular(lower, identity, lower=True)
    ritz_matrix = exact_dot(exact_dot(inverse, raw), inverse.T)
    kept = jnp.concatenate(
        [rotation[:total], jnp.zeros((total, total), jnp.float32), rotation[2 * total :]], axis=0
    )
    mixing = exact_dot(inverse.T, rotation)
    trailing = exact_dot(inverse.T, kept)
    combined = jnp.concatenate([mixing, trailing], axis=1)
    gathered_rows = combined[order]
    own_vectors = lax.dynamic_slice_in_dim(gathered_rows, owner * width, width, 1)
    own_directions = lax.dynamic_slice_in_dim(gathered_rows, total + owner * width, width, 1)
    selected = jnp.concatenate([own_vectors, own_directions], axis=1)
    result = math.sqrt(nodes) * exact_dot(selected.T, whole_panel)
    return (result[:width], result[width:], ritz_matrix)


def solution(mesh):
    in_specs = (
        P("cols", "rows"),
        P("cols", "rows"),
        P("rows", None, None, None),
        P("rows", None),
        P(),
    )
    out_specs = (P("cols", "rows"), P("cols", "rows"), P())
    return jax.shard_map(local, mesh=mesh, in_specs=in_specs, out_specs=out_specs, check_vma=False)
```

```python
import functools
import math

import jax
import jax.numpy as jnp
from jax import lax
from jax.experimental import pallas as pl
from jax.experimental.pallas import tpu as pltpu
from jax.sharding import PartitionSpec as P

BLK = 128
F32 = jnp.float32
BF16 = jnp.bfloat16
ROWS_PER_STEP = 4
VMEM_LIMIT = 60 * 2**20
PIVOTS = 16
EXACT = lax.Precision.HIGHEST


def halves(v):
    high = v.astype(BF16)
    return high, (v - high.astype(F32)).astype(BF16)


def ring(devices, step):
    return [(i, (i + step) % devices) for i in range(devices)]


def plane_groups():
    return [[z * 16 + i for i in range(16)] for z in range(8)]


def column_groups():
    return [[z * 16 + i for z in range(8)] for i in range(16)]


def exchange(x, groups):
    return lax.all_to_all(x, "rows", 0, 0, axis_index_groups=groups)


def repeated(x, count):
    return jnp.broadcast_to(x[None], (count,) + x.shape)


def sum_large(x):
    plane, column = plane_groups(), column_groups()
    part = jnp.sum(exchange(x, plane), axis=0)
    part = jnp.sum(exchange(repeated(part, 8), column), axis=0)
    return exchange(repeated(part, 16), plane)


def prepare_kernel(a_ref, split_ref, scale_ref):
    step = pl.program_id(0)
    for r in range(ROWS_PER_STEP):
        total = a_ref[r, 0]
        for k in range(6):
            a = a_ref[r, k]
            if k:
                total = total + a
            high, low = halves(a)
            split_ref[r, 0:BLK, k * BLK : (k + 1) * BLK] = high
            split_ref[r, BLK : 2 * BLK, k * BLK : (k + 1) * BLK] = low
        degree = jnp.sum(total.T, axis=0, keepdims=True)
        scale_ref[pl.ds(step * ROWS_PER_STEP + r, 1), :] = lax.rsqrt(degree)


def prepare(affinity):
    n = affinity.shape[0]
    return pl.pallas_call(
        prepare_kernel,
        grid=(n // ROWS_PER_STEP,),
        in_specs=[pl.BlockSpec((ROWS_PER_STEP, 6, BLK, BLK), lambda i: (i, 0, 0, 0))],
        out_specs=[
            pl.BlockSpec((ROWS_PER_STEP, 2 * BLK, 6 * BLK), lambda i: (i, 0, 0)),
            pl.BlockSpec((n, BLK), lambda i: (0, 0)),
        ],
        out_shape=[
            jax.ShapeDtypeStruct((n, 2 * BLK, 6 * BLK), BF16),
            jax.ShapeDtypeStruct((n, BLK), F32),
        ],
        compiler_params=pltpu.CompilerParams(vmem_limit_bytes=VMEM_LIMIT),
        cost_estimate=pl.CostEstimate(flops=10**7, bytes_accessed=19 * 10**6, transcendentals=3072),
        name="prepare",
    )(affinity)


def block_of(ref, i):
    return ref[:, pl.ds(pl.multiple_of(i * BLK, BLK), BLK)]


def local_place(index, first, total):
    place = index - first
    place = jnp.where(place < 0, place + total, place)
    return jnp.where(place >= total, place - total, place)


def gathered(info, pat, turned, i):
    places = [local_place(pat[i, k], info[1], info[2]) for k in range(6)]
    return jnp.concatenate([turned[place] for place in places], axis=0)


def first_kernel(info, pat, a_ref, x_ref, xb_ref, xa_ref, s_ref, sb_ref, sa_ref, y_ref, sums_ref, turned, acc):
    step = pl.program_id(0)
    count = s_ref.shape[0]

    @pl.when(step == 0)
    def _():
        acc[...] = jnp.zeros_like(acc)
        for part, (v_ref, t_ref) in enumerate(((xb_ref, sb_ref), (x_ref, s_ref), (xa_ref, sa_ref))):

            @pl.loop(0, count)
            def _(j):
                v = block_of(v_ref, j) * t_ref[pl.ds(j, 1), :]
                high = v.astype(BF16).astype(F32)
                stack = jnp.concatenate([high, v - high, jnp.zeros((64, BLK), F32)], axis=0)
                turned[part * count + j] = stack.T.astype(BF16)

    for r in range(ROWS_PER_STEP):
        i = step * ROWS_PER_STEP + r
        weights = gathered(info, pat, turned, i)
        product = jnp.dot(a_ref[r], weights, preferred_element_type=F32)
        image = (product[:BLK] + product[BLK:]).T
        x = block_of(x_ref, i)
        y = x - s_ref[pl.ds(i, 1), :] * (image[0:32] + image[32:64])
        y_ref[:, pl.ds(pl.multiple_of(i * BLK, BLK), BLK)] = y
        acc[0:32, :] += x * y
        acc[32:64, :] += x * x

    @pl.when(step == pl.num_programs(0) - 1)
    def _():
        stack = jnp.concatenate([acc[...], jnp.zeros((64, BLK), F32)], axis=0)
        sums_ref[...] = jnp.sum(stack.T, axis=0, keepdims=True)


def whole(shape):
    return pl.BlockSpec(shape, lambda i, *_: (0,) * len(shape))


def first_image(info, pattern, split, x, xb, xa, s, sb, sa):
    n = s.shape[0]
    return pl.pallas_call(
        first_kernel,
        grid_spec=pltpu.PrefetchScalarGridSpec(
            num_scalar_prefetch=2,
            grid=(n // ROWS_PER_STEP,),
            in_specs=[pl.BlockSpec((ROWS_PER_STEP, 2 * BLK, 6 * BLK), lambda i, *_: (i, 0, 0))]
            + [whole(x.shape)] * 3
            + [whole(s.shape)] * 3,
            out_specs=[whole(x.shape), whole((1, BLK))],
            scratch_shapes=[pltpu.VMEM((3 * n, BLK, BLK), BF16), pltpu.VMEM((64, BLK), F32)],
        ),
        out_shape=[jax.ShapeDtypeStruct(x.shape, F32), jax.ShapeDtypeStruct((1, BLK), F32)],
        compiler_params=pltpu.CompilerParams(vmem_limit_bytes=VMEM_LIMIT),
        cost_estimate=pl.CostEstimate(flops=4 * 10**9, bytes_accessed=11 * 10**6, transcendentals=0),
        name="first_image",
    )(info, pattern, split, x, xb, xa, s, sb, sa)


def second_kernel(
    info, pat, a_ref, sums_ref, y_ref, yb_ref, ya_ref, p_ref, pb_ref, pa_ref, s_ref, sb_ref, sa_ref,
    x_ref, xo_ref, yo_ref, po_ref, high_ref, low_ref, out_ref, turned, quotients, left_high, left_low, acc,
):
    step = pl.program_id(0)
    count = s_ref.shape[0]
    core = info[0]
    own = pl.multiple_of(core * 32, 32)
    other = pl.multiple_of((1 - core) * 32, 32)

    @pl.when(step == 0)
    def _():
        acc[...] = jnp.zeros_like(acc)
        sums = jnp.sum(sums_ref[...], axis=0, keepdims=True)
        column = jnp.broadcast_to(sums, (BLK, BLK)).T
        quotients[0:32] = column[0:32] / column[32:64]
        quotients[32:64] = column[64:96] / column[96:128]
        triples = ((yb_ref, pb_ref, sb_ref), (y_ref, p_ref, s_ref), (ya_ref, pa_ref, sa_ref))
        for part, (v_ref, w_ref, t_ref) in enumerate(triples):

            @pl.loop(0, count)
            def _(j):
                t = t_ref[pl.ds(j, 1), :]
                v = block_of(v_ref, j) * t
                w = block_of(w_ref, j) * t
                v_high = v.astype(BF16).astype(F32)
                w_high = w.astype(BF16).astype(F32)
                stack = jnp.concatenate([v_high, v - v_high, w_high, w - w_high], axis=0)
                turned[part * count + j] = stack.T.astype(BF16)

    q_own = quotients[pl.ds(own, 32), :]
    q_other = quotients[pl.ds(other, 32), :]
    for r in range(ROWS_PER_STEP):
        i = step * ROWS_PER_STEP + r
        lanes = slice(r * BLK, (r + 1) * BLK)
        weights = gathered(info, pat, turned, i)
        product = jnp.dot(a_ref[r], weights, preferred_element_type=F32)
        image = (product[:BLK] + product[BLK:]).T
        s = s_ref[pl.ds(i, 1), :]
        x, y, p = block_of(x_ref, i), block_of(y_ref, i), block_of(p_ref, i)
        z = y - s * (image[0:32] + image[32:64])
        p_image = p - s * (image[64:96] + image[96:128])
        residual = y - q_own * x
        for at, v in enumerate((residual, x, p, z - q_own * y, y, p_image)):
            high, low = halves(v)
            left_high[32 * at : 32 * at + 32, lanes] = high
            left_low[32 * at : 32 * at + 32, lanes] = low
            if at < 3:
                high_ref[pl.ds(64 * at + own, 32), lanes] = high
                low_ref[pl.ds(64 * at + own, 32), lanes] = low
        xo = block_of(xo_ref, i)
        for at, v in enumerate((block_of(yo_ref, i) - q_other * xo, xo, block_of(po_ref, i))):
            high, low = halves(v)
            high_ref[pl.ds(64 * at + other, 32), lanes] = high
            low_ref[pl.ds(64 * at + other, 32), lanes] = low

    left = jnp.concatenate([left_high[...], left_low[...]], axis=0)
    dims = (((1,), (1,)), ((), ()))
    acc[...] += lax.dot_general(left, high_ref[...], dims, preferred_element_type=F32) + lax.dot_general(
        left, low_ref[...], dims, preferred_element_type=F32
    )

    @pl.when(step == pl.num_programs(0) - 1)
    def _():
        total = acc[0:192] + acc[192:384]
        out_ref[0:192, :] = total[:, 0:BLK]
        out_ref[192:384, :] = jnp.concatenate([total[:, BLK:192], jnp.zeros((192, 64), F32)], axis=1)


def second_image(info, pattern, split, sums, y, yb, ya, p, pb, pa, s, sb, sa, x, xo, yo, po):
    n = s.shape[0]
    chunk = ROWS_PER_STEP * BLK
    return pl.pallas_call(
        second_kernel,
        grid_spec=pltpu.PrefetchScalarGridSpec(
            num_scalar_prefetch=2,
            grid=(n // ROWS_PER_STEP,),
            in_specs=[pl.BlockSpec((ROWS_PER_STEP, 2 * BLK, 6 * BLK), lambda i, *_: (i, 0, 0)), whole(sums.shape)]
            + [whole(x.shape)] * 6
            + [whole(s.shape)] * 3
            + [whole(x.shape)] * 4,
            out_specs=[pl.BlockSpec((192, chunk), lambda i, *_: (0, i))] * 2 + [whole((384, BLK))],
            scratch_shapes=[
                pltpu.VMEM((3 * n, BLK, BLK), BF16),
                pltpu.VMEM((64, BLK), F32),
                pltpu.VMEM((192, chunk), BF16),
                pltpu.VMEM((192, chunk), BF16),
                pltpu.VMEM((384, 192), F32),
            ],
        ),
        out_shape=[jax.ShapeDtypeStruct((192, x.shape[1]), BF16)] * 2 + [jax.ShapeDtypeStruct((384, BLK), F32)],
        compiler_params=pltpu.CompilerParams(vmem_limit_bytes=VMEM_LIMIT),
        cost_estimate=pl.CostEstimate(flops=8 * 10**9, bytes_accessed=18 * 10**6, transcendentals=0),
        name="second_image",
    )(info, pattern, split, sums, y, yb, ya, p, pb, pa, s, sb, sa, x, xo, yo, po)


def picked_row(groups, at):
    return jnp.broadcast_to(groups[at // 8][at % 8 : at % 8 + 1, :], (8, BLK))


def inverse_factor(block):
    lane = lax.broadcasted_iota(jnp.int32, (8, BLK), 1)
    sub = lax.broadcasted_iota(jnp.int32, (8, BLK), 0)
    a = []
    for g in range(4):
        unit = jnp.where(lane - 32 == sub + 8 * g, 1.0, 0.0)
        a.append(jnp.where(lane < 32, block[8 * g : 8 * g + 8, :], unit))
    for start in range(0, 32, PIVOTS):
        columns = [
            [jnp.broadcast_to(a[g][:, start + k : start + k + 1], (8, BLK)) if g >= start // 8 else None for g in range(4)]
            for k in range(PIVOTS)
        ]
        for k in range(PIVOTS):
            at = start + k
            own = at // 8
            pivot = 1.0 / picked_row(columns[k], at)
            factor = [columns[k][g] * pivot if g >= own else None for g in range(4)]
            factor[own] = jnp.where(sub > at % 8, factor[own], 0.0)
            for other in columns[k + 1 :]:
                e = picked_row(other, at)
                for g in range(own, 4):
                    other[g] = other[g] - factor[g] * e
            row = picked_row(a, at)
            for g in range(own, 4):
                a[g] = a[g] - factor[g] * row
    scaled = []
    for g in range(4):
        diagonal = jnp.sum(jnp.where(lane == sub + 8 * g, a[g], 0.0), axis=1, keepdims=True)
        scaled.append(a[g] * lax.rsqrt(diagonal))
    return jnp.concatenate(scaled, axis=0)[:, 32:64]


def exact(left, right, dims):
    return lax.dot_general(left, right, (dims, ((), ())), precision=EXACT, preferred_element_type=F32)


def inverse_cholesky(work, inverse):
    lane = lax.broadcasted_iota(jnp.int32, (32, 192), 1)
    sub = lax.broadcasted_iota(jnp.int32, (32, 192), 0)
    for at in range(0, 192, 32):
        rows = work[at : at + 32, :]
        if at < BLK:
            piece = rows[:, 0:BLK]
        else:
            piece = jnp.concatenate([rows[:, BLK:192], jnp.zeros((32, 64), F32)], axis=1)
        if at % BLK:
            piece = pltpu.roll(piece, BLK - at % BLK, 1)
        small = inverse_factor(piece)
        unit = jnp.where(lane - at == sub, 1.0, 0.0)
        rows = jnp.where((lane >= at) & (lane < at + 32), unit, rows)
        new = exact(small, rows, ((1,), (0,)))
        inverse[at : at + 32, :] = jnp.where(lane < at + 32, new, 0.0)
        if at < 160:
            update = exact(new, new, ((0,), (0,)))
            wide = lax.broadcasted_iota(jnp.int32, (160 - at, 192), 1)
            old = jnp.where((wide >= at) & (wide < at + 32), 0.0, work[at + 32 : 192, :])
            work[at + 32 : 192, :] = old - update[at + 32 : 192, :]


def final_kernel(
    info, mine_ref, theirs_ref, chosen_ref, high_ref, low_ref, vectors_ref, directions_ref, ritz_ref, work, raw, inverse, *, factor
):
    first = info[0] == 0
    for at in range(6):
        low_row = 32 * (at // 2)
        own = (at % 2 == 0) == first
        for base, target in ((0, work), (96, raw)):
            rows = slice(base + low_row, base + low_row + 32)
            lower_rows = slice(192 + base + low_row, 192 + base + low_row + 32)
            target[32 * at : 32 * at + 32, 0:BLK] = jnp.where(own, mine_ref[rows, :], theirs_ref[rows, :])
            tail = jnp.where(own, mine_ref[lower_rows, :], theirs_ref[lower_rows, :])
            target[32 * at : 32 * at + 32, BLK:192] = tail[:, 0:64]
    inverse_cholesky(work, inverse)
    whole_inverse = inverse[...]
    half = exact(whole_inverse, raw[...], ((1,), (1,)))
    ritz_ref[...] = exact(half, whole_inverse, ((1,), (1,)))
    mix = factor * exact(chosen_ref[...], whole_inverse, ((1,), (0,)))
    left = jnp.concatenate(halves(mix), axis=0)
    for at in range(0, high_ref.shape[1], 512):
        lanes = slice(at, at + 512)
        product = jnp.dot(left, high_ref[:, lanes], preferred_element_type=F32)
        product = product + jnp.dot(left, low_ref[:, lanes], preferred_element_type=F32)
        product = product[0:64] + product[64:128]
        vectors_ref[:, lanes] = product[0:32]
        directions_ref[:, lanes] = product[32:64]


def final(info, mine, theirs, chosen, high, low, factor):
    return pl.pallas_call(
        functools.partial(final_kernel, factor=factor),
        in_specs=[pl.BlockSpec(memory_space=pltpu.SMEM)] + [pl.BlockSpec(memory_space=pltpu.VMEM)] * 5,
        out_shape=[jax.ShapeDtypeStruct((32, high.shape[1]), F32)] * 2 + [jax.ShapeDtypeStruct((192, 192), F32)],
        scratch_shapes=[pltpu.VMEM((192, 192), F32)] * 3,
        compiler_params=pltpu.CompilerParams(vmem_limit_bytes=VMEM_LIMIT),
        cost_estimate=pl.CostEstimate(flops=4 * 10**8, bytes_accessed=4 * 10**6, transcendentals=0),
        name="final",
    )(info, mine, theirs, chosen, high, low)


def other_core(x):
    return lax.ppermute(x, "cols", [(0, 1), (1, 0)])


def local(vectors, directions, affinity, pattern, rotation):
    width, rows_dev = vectors.shape
    devices = lax.axis_size("rows")
    core = lax.axis_index("cols")
    total = 2 * width
    nodes = rows_dev * devices
    local_blocks = affinity.shape[0]
    all_blocks = local_blocks * devices
    first_block = (lax.axis_index("rows") - 1) * local_blocks
    info = jnp.stack([core, first_block, jnp.int32(all_blocks)]).astype(jnp.int32)
    up, down = ring(devices, 1), ring(devices, -1)

    x_before = lax.ppermute(vectors, "rows", up)
    x_after = lax.ppermute(vectors, "rows", down)
    split, scale = prepare(affinity)
    s_before = lax.ppermute(scale, "rows", up)
    s_after = lax.ppermute(scale, "rows", down)
    p_early, _ = lax.optimization_barrier((directions, scale))
    p_before = lax.ppermute(p_early, "rows", up)
    p_after = lax.ppermute(p_early, "rows", down)
    x_other = other_core(vectors)
    p_other = other_core(directions)
    y, sums = first_image(info, pattern, split, vectors, x_before, x_after, scale, s_before, s_after)
    y_before = lax.ppermute(y, "rows", up)
    y_after = lax.ppermute(y, "rows", down)
    y_other = other_core(y)
    half = sums[:, 0:64]
    blank = jnp.zeros_like(half)
    row = jnp.where(core == 0, jnp.concatenate([half, blank], axis=1), jnp.concatenate([blank, half], axis=1))
    all_sums = lax.all_to_all(repeated(row, 2 * devices), ("rows", "cols"), 0, 0).reshape(2 * devices, BLK)
    high, low, part = second_image(
        info, pattern, split, all_sums, y, y_before, y_after, directions, p_before, p_after,
        scale, s_before, s_after, vectors, x_other, y_other, p_other,
    )
    summed = sum_large(part.reshape(16, 24, BLK)).reshape(384, BLK)
    theirs = other_core(summed)
    mine = lambda m: lax.dynamic_slice_in_dim(m, core * width, width, 1)
    kept = jnp.concatenate([rotation[:total], jnp.zeros((total, total), F32), rotation[2 * total :]], axis=0)
    chosen = jnp.concatenate([mine(rotation), mine(kept)], axis=1).T
    new_vectors, new_directions, ritz_matrix = final(info, summed, theirs, chosen, high, low, math.sqrt(nodes))
    return new_vectors, new_directions, ritz_matrix


def solution(mesh):
    in_specs = (P("cols", "rows"), P("cols", "rows"), P("rows", None, None, None), P("rows", None), P())
    out_specs = (P("cols", "rows"), P("cols", "rows"), P())
    return jax.shard_map(local, mesh=mesh, in_specs=in_specs, out_specs=out_specs, check_vma=False)
```

```python
import functools
import math

import jax
import jax.numpy as jnp
from jax import lax
from jax.experimental import pallas as pl
from jax.experimental.pallas import tpu as pltpu
from jax.sharding import PartitionSpec as P

BLK = 128
F32 = jnp.float32
BF16 = jnp.bfloat16
UNROLL = 24
GROUP = 6
CHUNK = 8
VMEM_LIMIT = 60 * 2**20
PIVOTS = 16
EXACT = lax.Precision.HIGHEST


def halves(v):
    high = v.astype(BF16)
    return high, (v - high.astype(F32)).astype(BF16)


def ring(devices, step):
    return [(i, (i + step) % devices) for i in range(devices)]


def row_of(z, x, y):
    return z * 16 + x * 4 + y


def plane_groups():
    return [[row_of(z, x, y) for x in range(4) for y in range(4)] for z in range(8)]


def column_groups():
    return [[row_of(z, x, y) for z in range(8)] for x in range(4) for y in range(4)]


def sheet_groups():
    return [[row_of(z, x, y) for z in range(8) for x in range(4)] for y in range(4)]


def line_groups():
    return [[row_of(z, x, y) for y in range(4)] for z in range(8) for x in range(4)]


def with_cores(groups):
    return [[2 * i + core for core in range(2) for i in group] for group in groups]


def exchange(x, groups):
    return lax.all_to_all(x, "rows", 0, 0, axis_index_groups=groups)


def exchange_cores(x, groups):
    return lax.all_to_all(x, ("rows", "cols"), 0, 0, axis_index_groups=with_cores(groups))


def repeated(x, count):
    return jnp.broadcast_to(x[None], (count,) + x.shape)


def sum_large(x):
    part = jnp.sum(exchange(x, plane_groups()), axis=0)
    part = jnp.sum(exchange(repeated(part, 8), column_groups()), axis=0)
    return exchange_cores(repeated(part, 32), plane_groups())


def prepare_kernel(a_hbm, split_hbm, scale_ref, a_ref, split_ref, arrived, sent):
    count = a_ref.shape[0]
    arrivals = [pltpu.make_async_copy(a_hbm.at[i], a_ref.at[i], arrived.at[i]) for i in range(count)]
    sends = [pltpu.make_async_copy(split_ref.at[i], split_hbm.at[i], sent.at[i]) for i in range(count)]
    for copy in arrivals:
        copy.start()
    for i in range(count):
        if i % GROUP == 0:
            for copy in arrivals[i : i + GROUP]:
                copy.wait()
        total = a_ref[i, 0]
        for k in range(6):
            a = a_ref[i, k]
            if k:
                total = total + a
            high, low = halves(a)
            split_ref[i, 0:BLK, k * BLK : (k + 1) * BLK] = high
            split_ref[i, BLK : 2 * BLK, k * BLK : (k + 1) * BLK] = low
        scale_ref[i : i + 1, :] = lax.rsqrt(jnp.sum(total.T, axis=0, keepdims=True))
        if i % GROUP == GROUP - 1:
            for copy in sends[i + 1 - GROUP : i + 1]:
                copy.start()
    for copy in sends:
        copy.wait()


def prepare(affinity):
    n = affinity.shape[0]
    split = (n, 2 * BLK, 6 * BLK)
    return pl.pallas_call(
        prepare_kernel,
        in_specs=[pl.BlockSpec(memory_space=pl.ANY)],
        out_specs=[pl.BlockSpec(memory_space=pl.ANY), pl.BlockSpec(memory_space=pltpu.VMEM)],
        out_shape=[jax.ShapeDtypeStruct(split, BF16), jax.ShapeDtypeStruct((n, BLK), F32)],
        scratch_shapes=[
            pltpu.VMEM((n, 6, BLK, BLK), F32),
            pltpu.VMEM(split, BF16),
            pltpu.SemaphoreType.DMA((n,)),
            pltpu.SemaphoreType.DMA((n,)),
        ],
        compiler_params=pltpu.CompilerParams(vmem_limit_bytes=VMEM_LIMIT),
        cost_estimate=pl.CostEstimate(flops=10**7, bytes_accessed=19 * 10**6, transcendentals=3072),
        name="prepare",
    )(affinity)


def block_of(ref, i):
    return ref[:, pl.ds(pl.multiple_of(i * BLK, BLK), BLK)]


def local_place(index, first, total):
    place = index - first
    place = jnp.where(place < 0, place + total, place)
    return jnp.where(place >= total, place - total, place)


def gathered(info, pat, turned, i):
    places = [local_place(pat[i, k], info[1], info[2]) for k in range(6)]
    return jnp.concatenate([turned[place] for place in places], axis=0)


def loads(a_hbm, split_ref, arrived):
    copies = [pltpu.make_async_copy(a_hbm.at[i], split_ref.at[i], arrived.at[i]) for i in range(a_hbm.shape[0])]
    for copy in copies:
        copy.start()
    return copies


def turn(turned, place, v):
    turned[place] = v.T.astype(BF16)


def first_kernel(
    info, pat, a_hbm, x_ref, xb_ref, xa_ref, p_ref, s_ref, sb_ref, sa_ref, yp_ref, sums_ref, split_ref, turned, arrived
):
    count = s_ref.shape[0]
    copies = loads(a_hbm, split_ref, arrived)
    for part, (v_ref, t_ref) in enumerate(((xb_ref, sb_ref), (x_ref, s_ref), (xa_ref, sa_ref))):

        @pl.loop(0, count, unroll=UNROLL)
        def _(j):
            v = block_of(v_ref, j) * t_ref[pl.ds(j, 1), :]
            high = v.astype(BF16).astype(F32)
            turn(turned, part * count + j, jnp.concatenate([high, v - high, jnp.zeros((64, BLK), F32)], axis=0))

    yp_ref[32:64, :] = p_ref[...]
    xy = jnp.zeros((32, BLK), F32)
    xx = jnp.zeros((32, BLK), F32)
    for i in range(count):
        lanes = slice(i * BLK, (i + 1) * BLK)
        if i % GROUP == 0:
            for copy in copies[i : i + GROUP]:
                copy.wait()
        weights = gathered(info, pat, turned, i)
        product = jnp.dot(split_ref[i], weights, preferred_element_type=F32)
        image = (product[:BLK] + product[BLK:]).T
        x = x_ref[:, lanes]
        y = x - s_ref[i : i + 1, :] * (image[0:32] + image[32:64])
        yp_ref[0:32, lanes] = y
        xy += x * y
        xx += x * x
    stack = jnp.concatenate([xy, xx, jnp.zeros((64, BLK), F32)], axis=0)
    sums_ref[...] = jnp.sum(stack.T, axis=0, keepdims=True)


def memory(*spaces):
    return [pl.BlockSpec(memory_space=space) for space in spaces]


def first_image(info, pattern, split, x, xb, xa, p, s, sb, sa):
    n = s.shape[0]
    return pl.pallas_call(
        first_kernel,
        in_specs=memory(pltpu.SMEM, pltpu.SMEM, pl.ANY, *[pltpu.VMEM] * 7),
        out_shape=[jax.ShapeDtypeStruct((64, x.shape[1]), F32), jax.ShapeDtypeStruct((1, BLK), F32)],
        scratch_shapes=[
            pltpu.VMEM(split.shape, BF16),
            pltpu.VMEM((3 * n, BLK, BLK), BF16),
            pltpu.SemaphoreType.DMA((n,)),
        ],
        compiler_params=pltpu.CompilerParams(vmem_limit_bytes=VMEM_LIMIT),
        cost_estimate=pl.CostEstimate(flops=4 * 10**9, bytes_accessed=11 * 10**6, transcendentals=0),
        name="first_image",
    )(info, pattern, split, x, xb, xa, p, s, sb, sa)


def second_kernel(
    info, pat, a_hbm, sums_ref, yp_ref, before_ref, after_ref, s_ref, sb_ref, sa_ref, x_ref, xo_ref, ypo_ref,
    high_ref, low_ref, out_ref, split_ref, turned, quotients, left_ref, acc, arrived,
):
    count = s_ref.shape[0]
    core = info[0]
    own = pl.multiple_of(core * 32, 32)
    other = pl.multiple_of((1 - core) * 32, 32)
    copies = loads(a_hbm, split_ref, arrived)

    sums = jnp.sum(sums_ref[...], axis=0, keepdims=True)
    column = jnp.broadcast_to(sums, (BLK, BLK)).T
    quotients[0:32] = column[0:32] / column[32:64]
    quotients[32:64] = column[64:96] / column[96:128]
    q_own = quotients[pl.ds(own, 32), :]
    q_other = quotients[pl.ds(other, 32), :]
    for part, (v_ref, t_ref) in enumerate(((before_ref, sb_ref), (yp_ref, s_ref), (after_ref, sa_ref))):

        @pl.loop(0, count, unroll=UNROLL)
        def _(j):
            v = block_of(v_ref, j) * t_ref[pl.ds(j, 1), :]
            high = v.astype(BF16).astype(F32)
            turn(turned, part * count + j, jnp.concatenate([high, v - high], axis=0))

    for i in range(count):
        lanes = slice(i * BLK, (i + 1) * BLK)
        place = slice(i % CHUNK * BLK, (i % CHUNK + 1) * BLK)
        if i % GROUP == 0:
            for copy in copies[i : i + GROUP]:
                copy.wait()
        weights = gathered(info, pat, turned, i)
        product = jnp.dot(split_ref[i], weights, preferred_element_type=F32)
        image = (product[:BLK] + product[BLK:]).T
        image = yp_ref[:, lanes] - s_ref[i : i + 1, :] * (image[0:64] + image[64:128])
        x, y, p = x_ref[:, lanes], yp_ref[0:32, lanes], yp_ref[32:64, lanes]
        for at, v in enumerate((y - q_own * x, x, p, image[0:32] - q_own * y, y, image[32:64])):
            high, low = halves(v)
            left_ref[32 * at : 32 * at + 32, place] = high
            left_ref[192 + 32 * at : 224 + 32 * at, place] = low
            if at < 3:
                high_ref[pl.ds(64 * at + own, 32), lanes] = high
                low_ref[pl.ds(64 * at + own, 32), lanes] = low
        xo = xo_ref[:, lanes]
        for at, v in enumerate((ypo_ref[0:32, lanes] - q_other * xo, xo, ypo_ref[32:64, lanes])):
            high, low = halves(v)
            high_ref[pl.ds(64 * at + other, 32), lanes] = high
            low_ref[pl.ds(64 * at + other, 32), lanes] = low
        if i % CHUNK == CHUNK - 1:
            span = slice((i + 1 - CHUNK) * BLK, (i + 1) * BLK)
            dims = (((1,), (1,)), ((), ()))
            left = left_ref[...]
            part = lax.dot_general(left, high_ref[:, span], dims, preferred_element_type=F32)
            part = part + lax.dot_general(left, low_ref[:, span], dims, preferred_element_type=F32)
            acc[...] = part if i < CHUNK else acc[...] + part

    total = acc[0:192] + acc[192:384]
    out_ref[0:192, :] = total[:, 0:BLK]
    out_ref[192:384, :] = jnp.concatenate([total[:, BLK:192], jnp.zeros((192, 64), F32)], axis=1)


def second_image(info, pattern, split, sums, yp, before, after, s, sb, sa, x, xo, ypo):
    n = s.shape[0]
    return pl.pallas_call(
        second_kernel,
        in_specs=memory(pltpu.SMEM, pltpu.SMEM, pl.ANY, *[pltpu.VMEM] * 10),
        out_shape=[jax.ShapeDtypeStruct((192, x.shape[1]), BF16)] * 2 + [jax.ShapeDtypeStruct((384, BLK), F32)],
        scratch_shapes=[
            pltpu.VMEM(split.shape, BF16),
            pltpu.VMEM((3 * n, BLK, BLK), BF16),
            pltpu.VMEM((64, BLK), F32),
            pltpu.VMEM((384, CHUNK * BLK), BF16),
            pltpu.VMEM((384, 192), F32),
            pltpu.SemaphoreType.DMA((n,)),
        ],
        compiler_params=pltpu.CompilerParams(vmem_limit_bytes=VMEM_LIMIT),
        cost_estimate=pl.CostEstimate(flops=8 * 10**9, bytes_accessed=18 * 10**6, transcendentals=0),
        name="second_image",
    )(info, pattern, split, sums, yp, before, after, s, sb, sa, x, xo, ypo)


def picked_row(groups, at):
    return jnp.broadcast_to(groups[at // 8][at % 8 : at % 8 + 1, :], (8, BLK))


def inverse_factor(block):
    lane = lax.broadcasted_iota(jnp.int32, (8, BLK), 1)
    sub = lax.broadcasted_iota(jnp.int32, (8, BLK), 0)
    a = []
    for g in range(4):
        unit = jnp.where(lane - 32 == sub + 8 * g, 1.0, 0.0)
        a.append(jnp.where(lane < 32, block[8 * g : 8 * g + 8, :], unit))
    for start in range(0, 32, PIVOTS):
        columns = [
            [jnp.broadcast_to(a[g][:, start + k : start + k + 1], (8, BLK)) if g >= start // 8 else None for g in range(4)]
            for k in range(PIVOTS)
        ]
        for k in range(PIVOTS):
            at = start + k
            own = at // 8
            pivot = 1.0 / picked_row(columns[k], at)
            factor = [columns[k][g] * pivot if g >= own else None for g in range(4)]
            factor[own] = jnp.where(sub > at % 8, factor[own], 0.0)
            for other in columns[k + 1 :]:
                e = picked_row(other, at)
                for g in range(own, 4):
                    other[g] = other[g] - factor[g] * e
            row = picked_row(a, at)
            for g in range(own, 4):
                a[g] = a[g] - factor[g] * row
    scaled = []
    for g in range(4):
        diagonal = jnp.sum(jnp.where(lane == sub + 8 * g, a[g], 0.0), axis=1, keepdims=True)
        scaled.append(a[g] * lax.rsqrt(diagonal))
    return jnp.concatenate(scaled, axis=0)[:, 32:64]


def exact(left, right, dims):
    return lax.dot_general(left, right, (dims, ((), ())), precision=EXACT, preferred_element_type=F32)


def inverse_cholesky(work, inverse):
    lane = lax.broadcasted_iota(jnp.int32, (32, 192), 1)
    sub = lax.broadcasted_iota(jnp.int32, (32, 192), 0)
    for at in range(0, 192, 32):
        rows = work[at : at + 32, :]
        if at < BLK:
            piece = rows[:, 0:BLK]
        else:
            piece = jnp.concatenate([rows[:, BLK:192], jnp.zeros((32, 64), F32)], axis=1)
        if at % BLK:
            piece = pltpu.roll(piece, BLK - at % BLK, 1)
        small = inverse_factor(piece)
        unit = jnp.where(lane - at == sub, 1.0, 0.0)
        rows = jnp.where((lane >= at) & (lane < at + 32), unit, rows)
        new = exact(small, rows, ((1,), (0,)))
        inverse[at : at + 32, :] = jnp.where(lane < at + 32, new, 0.0)
        if at < 160:
            update = exact(new, new, ((0,), (0,)))
            wide = lax.broadcasted_iota(jnp.int32, (160 - at, 192), 1)
            old = jnp.where((wide >= at) & (wide < at + 32), 0.0, work[at + 32 : 192, :])
            work[at + 32 : 192, :] = old - update[at + 32 : 192, :]


def final_kernel(
    both_ref, chosen_ref, high_ref, low_ref, vectors_ref, directions_ref, ritz_ref, work, raw, inverse, *, factor
):
    for at in range(6):
        for base, target in ((0, work), (96, raw)):
            row = 384 * (at % 2) + base + 32 * (at // 2)
            target[32 * at : 32 * at + 32, 0:BLK] = both_ref[row : row + 32, :]
            target[32 * at : 32 * at + 32, BLK:192] = both_ref[row + 192 : row + 224, 0:64]
    inverse_cholesky(work, inverse)
    whole_inverse = inverse[...]
    half = exact(whole_inverse, raw[...], ((1,), (1,)))
    ritz_ref[...] = exact(half, whole_inverse, ((1,), (1,)))
    mix = factor * exact(chosen_ref[...], whole_inverse, ((1,), (0,)))
    left = jnp.concatenate(halves(mix), axis=0)
    for at in range(0, high_ref.shape[1], 512):
        lanes = slice(at, at + 512)
        product = jnp.dot(left, high_ref[:, lanes], preferred_element_type=F32)
        product = product + jnp.dot(left, low_ref[:, lanes], preferred_element_type=F32)
        product = product[0:64] + product[64:128]
        vectors_ref[:, lanes] = product[0:32]
        directions_ref[:, lanes] = product[32:64]


def final(both, chosen, high, low, factor):
    return pl.pallas_call(
        functools.partial(final_kernel, factor=factor),
        in_specs=memory(*[pltpu.VMEM] * 4),
        out_shape=[jax.ShapeDtypeStruct((32, high.shape[1]), F32)] * 2 + [jax.ShapeDtypeStruct((192, 192), F32)],
        scratch_shapes=[pltpu.VMEM((192, 192), F32)] * 3,
        compiler_params=pltpu.CompilerParams(vmem_limit_bytes=VMEM_LIMIT),
        cost_estimate=pl.CostEstimate(flops=4 * 10**8, bytes_accessed=4 * 10**6, transcendentals=0),
        name="final",
    )(both, chosen, high, low)


def other_core(x):
    return lax.ppermute(x, "cols", [(0, 1), (1, 0)])


def local(vectors, directions, affinity, pattern, rotation):
    width, rows_dev = vectors.shape
    devices = lax.axis_size("rows")
    core = lax.axis_index("cols")
    total = 2 * width
    nodes = rows_dev * devices
    local_blocks = affinity.shape[0]
    all_blocks = local_blocks * devices
    first_block = (lax.axis_index("rows") - 1) * local_blocks
    info = jnp.stack([core, first_block, jnp.int32(all_blocks)]).astype(jnp.int32)
    up, down = ring(devices, 1), ring(devices, -1)

    x_before = lax.ppermute(vectors, "rows", up)
    x_after = lax.ppermute(vectors, "rows", down)
    split, scale = prepare(affinity)
    s_before = lax.ppermute(scale, "rows", up)
    s_after = lax.ppermute(scale, "rows", down)
    x_other = other_core(vectors)
    yp, sums = first_image(info, pattern, split, vectors, x_before, x_after, directions, scale, s_before, s_after)
    yp_before = lax.ppermute(yp, "rows", up)
    yp_after = lax.ppermute(yp, "rows", down)
    yp_other = other_core(yp)
    sums = jnp.sum(exchange(repeated(sums, 32), sheet_groups()), axis=0)
    half = sums[:, 0:64]
    blank = jnp.zeros_like(half)
    row = jnp.where(core == 0, jnp.concatenate([half, blank], axis=1), jnp.concatenate([blank, half], axis=1))
    sums = exchange_cores(repeated(row, 8), line_groups()).reshape(8, BLK)
    high, low, part = second_image(
        info, pattern, split, sums, yp, yp_before, yp_after, scale, s_before, s_after, vectors, x_other, yp_other
    )
    both = sum_large(part.reshape(16, 24, BLK)).reshape(768, BLK)
    mine = lambda m: lax.dynamic_slice_in_dim(m, core * width, width, 1)
    kept = jnp.concatenate([rotation[:total], jnp.zeros((total, total), F32), rotation[2 * total :]], axis=0)
    chosen = jnp.concatenate([mine(rotation), mine(kept)], axis=1).T
    new_vectors, new_directions, ritz_matrix = final(both, chosen, high, low, math.sqrt(nodes))
    return new_vectors, new_directions, ritz_matrix


def solution(mesh):
    in_specs = (P("cols", "rows"), P("cols", "rows"), P("rows", None, None, None), P("rows", None), P())
    out_specs = (P("cols", "rows"), P("cols", "rows"), P())
    return jax.shard_map(local, mesh=mesh, in_specs=in_specs, out_specs=out_specs, check_vma=False)
```

```python
import functools
import math

import jax
import jax.numpy as jnp
from jax import lax
from jax.experimental import pallas as pl
from jax.experimental.pallas import tpu as pltpu
from jax.sharding import PartitionSpec as P

BLK = 128
F32 = jnp.float32
BF16 = jnp.bfloat16
UNROLL = 24
GROUP = 6
CHUNK = 8
VMEM_LIMIT = 60 * 2**20
PIVOTS = 16
EXACT = lax.Precision.HIGHEST


def halves(v):
    high = v.astype(BF16)
    return high, (v - high.astype(F32)).astype(BF16)


def ring(devices, step):
    return [(i, (i + step) % devices) for i in range(devices)]


def row_of(z, x, y):
    return z * 16 + x * 4 + y


def plane_groups():
    return [[row_of(z, x, y) for x in range(4) for y in range(4)] for z in range(8)]


def column_groups():
    return [[row_of(z, x, y) for z in range(8)] for x in range(4) for y in range(4)]


def with_cores(groups):
    return [[2 * i + core for core in range(2) for i in group] for group in groups]


def exchange(x, groups):
    return lax.all_to_all(x, "rows", 0, 0, axis_index_groups=groups)


def exchange_cores(x, groups):
    return lax.all_to_all(x, ("rows", "cols"), 0, 0, axis_index_groups=with_cores(groups))


def repeated(x, count):
    return jnp.broadcast_to(x[None], (count,) + x.shape)


def sum_large(x):
    part = jnp.sum(exchange(x, plane_groups()), axis=0)
    part = jnp.sum(exchange(repeated(part, 8), column_groups()), axis=0)
    return exchange_cores(repeated(part, 32), plane_groups())


def loads(a_hbm, a_ref, arrived):
    copies = [pltpu.make_async_copy(a_hbm.at[i], a_ref.at[i], arrived.at[i]) for i in range(a_hbm.shape[0])]
    for copy in copies:
        copy.start()
    return copies


def wait_group(copies, i):
    if i % GROUP == 0:
        for copy in copies[i : i + GROUP]:
            copy.wait()


def memory(*spaces):
    return [pl.BlockSpec(memory_space=space) for space in spaces]


def degree_kernel(a_hbm, x_ref, scale_ref, xs_ref, a_ref, arrived):
    copies = loads(a_hbm, a_ref, arrived)
    for i in range(a_ref.shape[0]):
        wait_group(copies, i)
        total = a_ref[i, 0]
        for k in range(1, 6):
            total = total + a_ref[i, k]
        scale = lax.rsqrt(jnp.sum(total.T, axis=0, keepdims=True))
        scale_ref[i : i + 1, :] = scale
        lanes = slice(i * BLK, (i + 1) * BLK)
        xs_ref[:, lanes] = x_ref[:, lanes] * scale


def degrees(affinity, x):
    n = affinity.shape[0]
    return pl.pallas_call(
        degree_kernel,
        in_specs=memory(pl.ANY, pltpu.VMEM),
        out_shape=[jax.ShapeDtypeStruct((n, BLK), F32), jax.ShapeDtypeStruct(x.shape, F32)],
        scratch_shapes=[pltpu.VMEM(affinity.shape, F32), pltpu.SemaphoreType.DMA((n,))],
        compiler_params=pltpu.CompilerParams(vmem_limit_bytes=VMEM_LIMIT),
        cost_estimate=pl.CostEstimate(flops=10**7, bytes_accessed=10**7, transcendentals=3072),
        name="degrees",
    )(affinity, x)


def split_kernel(a_hbm, scale_hbm, split_hbm, a_ref, split_ref, arrived, sent):
    count = a_ref.shape[0]
    copies = loads(a_hbm, a_ref, arrived)
    sends = [pltpu.make_async_copy(split_ref.at[i], split_hbm.at[i], sent.at[i]) for i in range(count)]
    for i in range(count):
        wait_group(copies, i)
        for k in range(6):
            high, low = halves(a_ref[i, k])
            split_ref[i, 0:BLK, k * BLK : (k + 1) * BLK] = high
            split_ref[i, BLK : 2 * BLK, k * BLK : (k + 1) * BLK] = low
        if i % GROUP == GROUP - 1:
            for copy in sends[i + 1 - GROUP : i + 1]:
                copy.start()
    for copy in sends:
        copy.wait()


def split_affinity(affinity, scale):
    n = affinity.shape[0]
    split = (n, 2 * BLK, 6 * BLK)
    return pl.pallas_call(
        split_kernel,
        in_specs=memory(pl.ANY, pl.ANY),
        out_specs=pl.BlockSpec(memory_space=pl.ANY),
        out_shape=jax.ShapeDtypeStruct(split, BF16),
        scratch_shapes=[
            pltpu.VMEM((n, 6, BLK, BLK), F32),
            pltpu.VMEM(split, BF16),
            pltpu.SemaphoreType.DMA((n,)),
            pltpu.SemaphoreType.DMA((n,)),
        ],
        compiler_params=pltpu.CompilerParams(vmem_limit_bytes=VMEM_LIMIT),
        cost_estimate=pl.CostEstimate(flops=10**7, bytes_accessed=19 * 10**6, transcendentals=0),
        name="split",
    )(affinity, scale)


def block_of(ref, i):
    return ref[:, pl.ds(pl.multiple_of(i * BLK, BLK), BLK)]


def local_place(index, first, total):
    place = index - first
    place = jnp.where(place < 0, place + total, place)
    return jnp.where(place >= total, place - total, place)


def gathered(info, pat, turned, i):
    places = [local_place(pat[i, k], info[1], info[2]) for k in range(6)]
    return jnp.concatenate([turned[place] for place in places], axis=0)


def turn_all(turned, refs, count):
    for part, v_ref in enumerate(refs):

        @pl.loop(0, count, unroll=UNROLL)
        def _(j):
            v = block_of(v_ref, j)
            high = v.astype(BF16).astype(F32)
            stack = [high, v - high]
            if v.shape[0] == 32:
                stack.append(jnp.zeros((64, BLK), F32))
            turned[part * count + j] = jnp.concatenate(stack, axis=0).T.astype(BF16)


def first_kernel(
    info, pat, a_hbm, x_ref, xs_ref, before_ref, after_ref, p_ref, s_ref, y_ref, scaled_ref, sums_ref, split_ref, turned, arrived
):
    count = s_ref.shape[0]
    copies = loads(a_hbm, split_ref, arrived)
    turn_all(turned, (before_ref, xs_ref, after_ref), count)
    xy = jnp.zeros((32, BLK), F32)
    xx = jnp.zeros((32, BLK), F32)
    for i in range(count):
        lanes = slice(i * BLK, (i + 1) * BLK)
        wait_group(copies, i)
        weights = gathered(info, pat, turned, i)
        product = jnp.dot(split_ref[i], weights, preferred_element_type=F32)
        image = (product[:BLK] + product[BLK:]).T
        x, s = x_ref[:, lanes], s_ref[i : i + 1, :]
        y = x - s * (image[0:32] + image[32:64])
        y_ref[:, lanes] = y
        scaled_ref[0:32, lanes] = s * y
        scaled_ref[32:64, lanes] = s * p_ref[:, lanes]
        xy += x * y
        xx += x * x
    stack = jnp.concatenate([xy, xx, jnp.zeros((64, BLK), F32)], axis=0)
    sums_ref[...] = jnp.sum(stack.T, axis=0, keepdims=True)


def first_image(info, pattern, split, x, xs, before, after, p, s):
    n = s.shape[0]
    return pl.pallas_call(
        first_kernel,
        in_specs=memory(pltpu.SMEM, pltpu.SMEM, pl.ANY, *[pltpu.VMEM] * 6),
        out_shape=[
            jax.ShapeDtypeStruct(x.shape, F32),
            jax.ShapeDtypeStruct((64, x.shape[1]), F32),
            jax.ShapeDtypeStruct((1, BLK), F32),
        ],
        scratch_shapes=[
            pltpu.VMEM(split.shape, BF16),
            pltpu.VMEM((3 * n, BLK, BLK), BF16),
            pltpu.SemaphoreType.DMA((n,)),
        ],
        compiler_params=pltpu.CompilerParams(vmem_limit_bytes=VMEM_LIMIT),
        cost_estimate=pl.CostEstimate(flops=4 * 10**9, bytes_accessed=11 * 10**6, transcendentals=0),
        name="first_image",
    )(info, pattern, split, x, xs, before, after, p, s)


def second_kernel(
    info, pat, a_hbm, sums_ref, scaled_ref, before_ref, after_ref, s_ref, x_ref, y_ref, p_ref, xo_ref, yo_ref, po_ref,
    high_ref, low_ref, out_ref, split_ref, turned, quotients, left_ref, acc, arrived,
):
    count = s_ref.shape[0]
    core = info[0]
    own = pl.multiple_of(core * 32, 32)
    other = pl.multiple_of((1 - core) * 32, 32)
    copies = loads(a_hbm, split_ref, arrived)

    sums = jnp.sum(sums_ref[...], axis=0, keepdims=True)
    column = jnp.broadcast_to(sums, (BLK, BLK)).T
    quotients[0:32] = column[0:32] / column[32:64]
    quotients[32:64] = column[64:96] / column[96:128]
    q_own = quotients[pl.ds(own, 32), :]
    q_other = quotients[pl.ds(other, 32), :]
    turn_all(turned, (before_ref, scaled_ref, after_ref), count)
    for i in range(count):
        lanes = slice(i * BLK, (i + 1) * BLK)
        place = slice(i % CHUNK * BLK, (i % CHUNK + 1) * BLK)
        wait_group(copies, i)
        weights = gathered(info, pat, turned, i)
        product = jnp.dot(split_ref[i], weights, preferred_element_type=F32)
        image = (product[:BLK] + product[BLK:]).T
        x, y, p, s = x_ref[:, lanes], y_ref[:, lanes], p_ref[:, lanes], s_ref[i : i + 1, :]
        z = y - s * (image[0:32] + image[64:96])
        p_image = p - s * (image[32:64] + image[96:128])
        for at, v in enumerate((y - q_own * x, x, p, z - q_own * y, y, p_image)):
            high, low = halves(v)
            left_ref[32 * at : 32 * at + 32, place] = high
            left_ref[192 + 32 * at : 224 + 32 * at, place] = low
            if at < 3:
                high_ref[pl.ds(64 * at + own, 32), lanes] = high
                low_ref[pl.ds(64 * at + own, 32), lanes] = low
        xo = xo_ref[:, lanes]
        for at, v in enumerate((yo_ref[:, lanes] - q_other * xo, xo, po_ref[:, lanes])):
            high, low = halves(v)
            high_ref[pl.ds(64 * at + other, 32), lanes] = high
            low_ref[pl.ds(64 * at + other, 32), lanes] = low
        if i % CHUNK == CHUNK - 1:
            span = slice((i + 1 - CHUNK) * BLK, (i + 1) * BLK)
            dims = (((1,), (1,)), ((), ()))
            left = left_ref[...]
            part = lax.dot_general(left, high_ref[:, span], dims, preferred_element_type=F32)
            part = part + lax.dot_general(left, low_ref[:, span], dims, preferred_element_type=F32)
            acc[...] = part if i < CHUNK else acc[...] + part

    total = acc[0:192] + acc[192:384]
    out_ref[0:192, :] = total[:, 0:BLK]
    out_ref[192:384, :] = jnp.concatenate([total[:, BLK:192], jnp.zeros((192, 64), F32)], axis=1)


def second_image(info, pattern, split, sums, scaled, before, after, s, x, y, p, xo, yo, po):
    n = s.shape[0]
    return pl.pallas_call(
        second_kernel,
        in_specs=memory(pltpu.SMEM, pltpu.SMEM, pl.ANY, *[pltpu.VMEM] * 11),
        out_shape=[jax.ShapeDtypeStruct((192, x.shape[1]), BF16)] * 2 + [jax.ShapeDtypeStruct((384, BLK), F32)],
        scratch_shapes=[
            pltpu.VMEM(split.shape, BF16),
            pltpu.VMEM((3 * n, BLK, BLK), BF16),
            pltpu.VMEM((64, BLK), F32),
            pltpu.VMEM((384, CHUNK * BLK), BF16),
            pltpu.VMEM((384, 192), F32),
            pltpu.SemaphoreType.DMA((n,)),
        ],
        compiler_params=pltpu.CompilerParams(vmem_limit_bytes=VMEM_LIMIT),
        cost_estimate=pl.CostEstimate(flops=8 * 10**9, bytes_accessed=18 * 10**6, transcendentals=0),
        name="second_image",
    )(info, pattern, split, sums, scaled, before, after, s, x, y, p, xo, yo, po)


def picked_row(groups, at):
    return jnp.broadcast_to(groups[at // 8][at % 8 : at % 8 + 1, :], (8, BLK))


def inverse_factor(block):
    lane = lax.broadcasted_iota(jnp.int32, (8, BLK), 1)
    sub = lax.broadcasted_iota(jnp.int32, (8, BLK), 0)
    a = []
    for g in range(4):
        unit = jnp.where(lane - 32 == sub + 8 * g, 1.0, 0.0)
        a.append(jnp.where(lane < 32, block[8 * g : 8 * g + 8, :], unit))
    for start in range(0, 32, PIVOTS):
        columns = [
            [jnp.broadcast_to(a[g][:, start + k : start + k + 1], (8, BLK)) if g >= start // 8 else None for g in range(4)]
            for k in range(PIVOTS)
        ]
        for k in range(PIVOTS):
            at = start + k
            own = at // 8
            pivot = 1.0 / picked_row(columns[k], at)
            factor = [columns[k][g] * pivot if g >= own else None for g in range(4)]
            factor[own] = jnp.where(sub > at % 8, factor[own], 0.0)
            for other in columns[k + 1 :]:
                e = picked_row(other, at)
                for g in range(own, 4):
                    other[g] = other[g] - factor[g] * e
            row = picked_row(a, at)
            for g in range(own, 4):
                a[g] = a[g] - factor[g] * row
    scaled = []
    for g in range(4):
        diagonal = jnp.sum(jnp.where(lane == sub + 8 * g, a[g], 0.0), axis=1, keepdims=True)
        scaled.append(a[g] * lax.rsqrt(diagonal))
    return jnp.concatenate(scaled, axis=0)[:, 32:64]


def exact(left, right, dims):
    return lax.dot_general(left, right, (dims, ((), ())), precision=EXACT, preferred_element_type=F32)


def inverse_cholesky(work, inverse):
    lane = lax.broadcasted_iota(jnp.int32, (32, 192), 1)
    sub = lax.broadcasted_iota(jnp.int32, (32, 192), 0)
    for at in range(0, 192, 32):
        rows = work[at : at + 32, :]
        if at < BLK:
            piece = rows[:, 0:BLK]
        else:
            piece = jnp.concatenate([rows[:, BLK:192], jnp.zeros((32, 64), F32)], axis=1)
        if at % BLK:
            piece = pltpu.roll(piece, BLK - at % BLK, 1)
        small = inverse_factor(piece)
        unit = jnp.where(lane - at == sub, 1.0, 0.0)
        rows = jnp.where((lane >= at) & (lane < at + 32), unit, rows)
        new = exact(small, rows, ((1,), (0,)))
        inverse[at : at + 32, :] = jnp.where(lane < at + 32, new, 0.0)
        if at < 160:
            update = exact(new, new, ((0,), (0,)))
            wide = lax.broadcasted_iota(jnp.int32, (160 - at, 192), 1)
            old = jnp.where((wide >= at) & (wide < at + 32), 0.0, work[at + 32 : 192, :])
            work[at + 32 : 192, :] = old - update[at + 32 : 192, :]


def final_kernel(
    both_ref, chosen_ref, high_ref, low_ref, vectors_ref, directions_ref, ritz_ref, work, raw, inverse, *, factor
):
    for at in range(6):
        for base, target in ((0, work), (96, raw)):
            row = 384 * (at % 2) + base + 32 * (at // 2)
            target[32 * at : 32 * at + 32, 0:BLK] = both_ref[row : row + 32, :]
            target[32 * at : 32 * at + 32, BLK:192] = both_ref[row + 192 : row + 224, 0:64]
    inverse_cholesky(work, inverse)
    whole_inverse = inverse[...]
    half = exact(whole_inverse, raw[...], ((1,), (1,)))
    ritz_ref[...] = exact(half, whole_inverse, ((1,), (1,)))
    mix = factor * exact(chosen_ref[...], whole_inverse, ((1,), (0,)))
    left = jnp.concatenate(halves(mix), axis=0)
    for at in range(0, high_ref.shape[1], 512):
        lanes = slice(at, at + 512)
        product = jnp.dot(left, high_ref[:, lanes], preferred_element_type=F32)
        product = product + jnp.dot(left, low_ref[:, lanes], preferred_element_type=F32)
        product = product[0:64] + product[64:128]
        vectors_ref[:, lanes] = product[0:32]
        directions_ref[:, lanes] = product[32:64]


def final(both, chosen, high, low, factor):
    return pl.pallas_call(
        functools.partial(final_kernel, factor=factor),
        in_specs=memory(*[pltpu.VMEM] * 4),
        out_shape=[jax.ShapeDtypeStruct((32, high.shape[1]), F32)] * 2 + [jax.ShapeDtypeStruct((192, 192), F32)],
        scratch_shapes=[pltpu.VMEM((192, 192), F32)] * 3,
        compiler_params=pltpu.CompilerParams(vmem_limit_bytes=VMEM_LIMIT),
        cost_estimate=pl.CostEstimate(flops=4 * 10**8, bytes_accessed=4 * 10**6, transcendentals=0),
        name="final",
    )(both, chosen, high, low)


def other_core(x):
    return lax.ppermute(x, "cols", [(0, 1), (1, 0)])


def local(vectors, directions, affinity, pattern, rotation):
    width, rows_dev = vectors.shape
    devices = lax.axis_size("rows")
    core = lax.axis_index("cols")
    total = 2 * width
    nodes = rows_dev * devices
    local_blocks = affinity.shape[0]
    all_blocks = local_blocks * devices
    first_block = (lax.axis_index("rows") - 1) * local_blocks
    info = jnp.stack([core, first_block, jnp.int32(all_blocks)]).astype(jnp.int32)
    up, down = ring(devices, 1), ring(devices, -1)

    scale, xs = degrees(affinity, vectors)
    xs_before = lax.ppermute(xs, "rows", up)
    xs_after = lax.ppermute(xs, "rows", down)
    split = split_affinity(affinity, scale)
    x_other = other_core(vectors)
    p_other = other_core(directions)
    y, scaled, sums = first_image(info, pattern, split, vectors, xs, xs_before, xs_after, directions, scale)
    scaled_before = lax.ppermute(scaled, "rows", up)
    scaled_after = lax.ppermute(scaled, "rows", down)
    y_other = other_core(y)
    half = sums[:, 0:64]
    blank = jnp.zeros_like(half)
    row = jnp.where(core == 0, jnp.concatenate([half, blank], axis=1), jnp.concatenate([blank, half], axis=1))
    sums = lax.all_to_all(repeated(row, 2 * devices), ("rows", "cols"), 0, 0).reshape(2 * devices, BLK)
    high, low, part = second_image(
        info, pattern, split, sums, scaled, scaled_before, scaled_after, scale, vectors, y, directions, x_other, y_other, p_other
    )
    both = sum_large(part.reshape(16, 24, BLK)).reshape(768, BLK)
    mine = lambda m: lax.dynamic_slice_in_dim(m, core * width, width, 1)
    kept = jnp.concatenate([rotation[:total], jnp.zeros((total, total), F32), rotation[2 * total :]], axis=0)
    chosen = jnp.concatenate([mine(rotation), mine(kept)], axis=1).T
    new_vectors, new_directions, ritz_matrix = final(both, chosen, high, low, math.sqrt(nodes))
    return new_vectors, new_directions, ritz_matrix


def solution(mesh):
    in_specs = (P("cols", "rows"), P("cols", "rows"), P("rows", None, None, None), P("rows", None), P())
    out_specs = (P("cols", "rows"), P("cols", "rows"), P())
    return jax.shard_map(local, mesh=mesh, in_specs=in_specs, out_specs=out_specs, check_vma=False)
```

```python
import functools
import math

import jax
import jax.numpy as jnp
from jax import lax
from jax.experimental import pallas as pl
from jax.experimental.pallas import tpu as pltpu
from jax.sharding import PartitionSpec as P

BLK = 128
F32 = jnp.float32
BF16 = jnp.bfloat16
UNROLL = 24
GROUP = 6
CHUNK = 8
VMEM_LIMIT = 60 * 2**20
PIVOTS = 16
EXACT = lax.Precision.HIGHEST


def halves(v):
    high = v.astype(BF16)
    return high, (v - high.astype(F32)).astype(BF16)


def swaps(devices, first):
    return [pair for i in range(first, devices, 2) for pair in ((i, (i + 1) % devices), ((i + 1) % devices, i))]


def from_neighbours(x):
    devices = lax.axis_size("rows")
    return [lax.ppermute(x, "rows", swaps(devices, first)) for first in (1, 0)]


def row_of(z, x, y):
    return z * 16 + x * 4 + y


def plane_groups():
    return [[row_of(z, x, y) for x in range(4) for y in range(4)] for z in range(8)]


def column_groups():
    return [[row_of(z, x, y) for z in range(8)] for x in range(4) for y in range(4)]


def with_cores(groups):
    return [[2 * i + core for core in range(2) for i in group] for group in groups]


def exchange(x, groups):
    return lax.all_to_all(x, "rows", 0, 0, axis_index_groups=groups)


def exchange_cores(x, groups):
    return lax.all_to_all(x, ("rows", "cols"), 0, 0, axis_index_groups=with_cores(groups))


def repeated(x, count):
    return jnp.broadcast_to(x[None], (count,) + x.shape)


def sum_large(x):
    part = jnp.sum(exchange(x, plane_groups()), axis=0)
    part = jnp.sum(exchange(repeated(part, 8), column_groups()), axis=0)
    return exchange_cores(repeated(part, 32), plane_groups())


def loads(a_hbm, a_ref, arrived):
    copies = [pltpu.make_async_copy(a_hbm.at[i], a_ref.at[i], arrived.at[i]) for i in range(a_hbm.shape[0])]
    for copy in copies:
        copy.start()
    return copies


def wait_group(copies, i):
    if i % GROUP == 0:
        for copy in copies[i : i + GROUP]:
            copy.wait()


def memory(*spaces):
    return [pl.BlockSpec(memory_space=space) for space in spaces]


def degree_kernel(a_hbm, x_ref, scale_ref, xs_ref, a_ref, arrived):
    copies = loads(a_hbm, a_ref, arrived)
    for i in range(a_ref.shape[0]):
        wait_group(copies, i)
        total = a_ref[i, 0]
        for k in range(1, 6):
            total = total + a_ref[i, k]
        scale = lax.rsqrt(jnp.sum(total.T, axis=0, keepdims=True))
        scale_ref[i : i + 1, :] = scale
        lanes = slice(i * BLK, (i + 1) * BLK)
        xs_ref[:, lanes] = x_ref[:, lanes] * scale


def degrees(affinity, x):
    n = affinity.shape[0]
    return pl.pallas_call(
        degree_kernel,
        in_specs=memory(pl.ANY, pltpu.VMEM),
        out_shape=[jax.ShapeDtypeStruct((n, BLK), F32), jax.ShapeDtypeStruct(x.shape, F32)],
        scratch_shapes=[pltpu.VMEM(affinity.shape, F32), pltpu.SemaphoreType.DMA((n,))],
        compiler_params=pltpu.CompilerParams(vmem_limit_bytes=VMEM_LIMIT),
        cost_estimate=pl.CostEstimate(flops=10**7, bytes_accessed=10**7, transcendentals=3072),
        name="degrees",
    )(affinity, x)


def split_kernel(a_hbm, scale_hbm, split_hbm, a_ref, split_ref, arrived, sent):
    count = a_ref.shape[0]
    copies = loads(a_hbm, a_ref, arrived)
    sends = [pltpu.make_async_copy(split_ref.at[i], split_hbm.at[i], sent.at[i]) for i in range(count)]
    for i in range(count):
        wait_group(copies, i)
        for k in range(6):
            high, low = halves(a_ref[i, k])
            split_ref[i, 0:BLK, k * BLK : (k + 1) * BLK] = high
            split_ref[i, BLK : 2 * BLK, k * BLK : (k + 1) * BLK] = low
        if i % GROUP == GROUP - 1:
            for copy in sends[i + 1 - GROUP : i + 1]:
                copy.start()
    for copy in sends:
        copy.wait()


def split_affinity(affinity, scale):
    n = affinity.shape[0]
    split = (n, 2 * BLK, 6 * BLK)
    return pl.pallas_call(
        split_kernel,
        in_specs=memory(pl.ANY, pl.ANY),
        out_specs=pl.BlockSpec(memory_space=pl.ANY),
        out_shape=jax.ShapeDtypeStruct(split, BF16),
        scratch_shapes=[
            pltpu.VMEM((n, 6, BLK, BLK), F32),
            pltpu.VMEM(split, BF16),
            pltpu.SemaphoreType.DMA((n,)),
            pltpu.SemaphoreType.DMA((n,)),
        ],
        compiler_params=pltpu.CompilerParams(vmem_limit_bytes=VMEM_LIMIT),
        cost_estimate=pl.CostEstimate(flops=10**7, bytes_accessed=19 * 10**6, transcendentals=0),
        name="split",
    )(affinity, scale)


def block_of(ref, i):
    return ref[:, pl.ds(pl.multiple_of(i * BLK, BLK), BLK)]


def local_place(index, first, total):
    place = index - first
    place = jnp.where(place < 0, place + total, place)
    return jnp.where(place >= total, place - total, place)


def gathered(info, pat, turned, i):
    places = [local_place(pat[i, k], info[1], info[2]) for k in range(6)]
    return jnp.concatenate([turned[place] for place in places], axis=0)


def turn_all(turned, odd, refs, count):
    for part, v_ref in zip((2 * odd, 1, 2 - 2 * odd), refs):

        @pl.loop(0, count, unroll=UNROLL)
        def _(j):
            v = block_of(v_ref, j)
            high = v.astype(BF16).astype(F32)
            stack = [high, v - high]
            if v.shape[0] == 32:
                stack.append(jnp.zeros((64, BLK), F32))
            turned[part * count + j] = jnp.concatenate(stack, axis=0).T.astype(BF16)


def first_kernel(
    info, pat, a_hbm, x_ref, xs_ref, across_odd_ref, across_even_ref, p_ref, s_ref, y_ref, scaled_ref, sums_ref, split_ref, turned, arrived
):
    count = s_ref.shape[0]
    copies = loads(a_hbm, split_ref, arrived)
    turn_all(turned, info[3], (across_odd_ref, xs_ref, across_even_ref), count)
    xy = jnp.zeros((32, BLK), F32)
    xx = jnp.zeros((32, BLK), F32)
    for i in range(count):
        lanes = slice(i * BLK, (i + 1) * BLK)
        wait_group(copies, i)
        weights = gathered(info, pat, turned, i)
        product = jnp.dot(split_ref[i], weights, preferred_element_type=F32)
        image = (product[:BLK] + product[BLK:]).T
        x, s = x_ref[:, lanes], s_ref[i : i + 1, :]
        y = x - s * (image[0:32] + image[32:64])
        y_ref[:, lanes] = y
        scaled_ref[0:32, lanes] = s * y
        scaled_ref[32:64, lanes] = s * p_ref[:, lanes]
        xy += x * y
        xx += x * x
    stack = jnp.concatenate([xy, xx, jnp.zeros((64, BLK), F32)], axis=0)
    sums_ref[...] = jnp.sum(stack.T, axis=0, keepdims=True)


def first_image(info, pattern, split, x, xs, across_odd, across_even, p, s):
    n = s.shape[0]
    return pl.pallas_call(
        first_kernel,
        in_specs=memory(pltpu.SMEM, pltpu.SMEM, pl.ANY, *[pltpu.VMEM] * 6),
        out_shape=[
            jax.ShapeDtypeStruct(x.shape, F32),
            jax.ShapeDtypeStruct((64, x.shape[1]), F32),
            jax.ShapeDtypeStruct((1, BLK), F32),
        ],
        scratch_shapes=[
            pltpu.VMEM(split.shape, BF16),
            pltpu.VMEM((3 * n, BLK, BLK), BF16),
            pltpu.SemaphoreType.DMA((n,)),
        ],
        compiler_params=pltpu.CompilerParams(vmem_limit_bytes=VMEM_LIMIT),
        cost_estimate=pl.CostEstimate(flops=4 * 10**9, bytes_accessed=11 * 10**6, transcendentals=0),
        name="first_image",
    )(info, pattern, split, x, xs, across_odd, across_even, p, s)


def second_kernel(
    info, pat, a_hbm, sums_ref, scaled_ref, across_odd_ref, across_even_ref, s_ref, x_ref, y_ref, p_ref, xo_ref, yo_ref, po_ref,
    high_ref, low_ref, out_ref, split_ref, turned, quotients, left_ref, acc, arrived,
):
    count = s_ref.shape[0]
    core = info[0]
    own = pl.multiple_of(core * 32, 32)
    other = pl.multiple_of((1 - core) * 32, 32)
    copies = loads(a_hbm, split_ref, arrived)

    sums = jnp.sum(sums_ref[...], axis=0, keepdims=True)
    column = jnp.broadcast_to(sums, (BLK, BLK)).T
    quotients[0:32] = column[0:32] / column[32:64]
    quotients[32:64] = column[64:96] / column[96:128]
    q_own = quotients[pl.ds(own, 32), :]
    q_other = quotients[pl.ds(other, 32), :]
    turn_all(turned, info[3], (across_odd_ref, scaled_ref, across_even_ref), count)
    for i in range(count):
        lanes = slice(i * BLK, (i + 1) * BLK)
        place = slice(i % CHUNK * BLK, (i % CHUNK + 1) * BLK)
        wait_group(copies, i)
        weights = gathered(info, pat, turned, i)
        product = jnp.dot(split_ref[i], weights, preferred_element_type=F32)
        image = (product[:BLK] + product[BLK:]).T
        x, y, p, s = x_ref[:, lanes], y_ref[:, lanes], p_ref[:, lanes], s_ref[i : i + 1, :]
        z = y - s * (image[0:32] + image[64:96])
        p_image = p - s * (image[32:64] + image[96:128])
        for at, v in enumerate((y - q_own * x, x, p, z - q_own * y, y, p_image)):
            high, low = halves(v)
            left_ref[32 * at : 32 * at + 32, place] = high
            left_ref[192 + 32 * at : 224 + 32 * at, place] = low
            if at < 3:
                high_ref[pl.ds(64 * at + own, 32), lanes] = high
                low_ref[pl.ds(64 * at + own, 32), lanes] = low
        xo = xo_ref[:, lanes]
        for at, v in enumerate((yo_ref[:, lanes] - q_other * xo, xo, po_ref[:, lanes])):
            high, low = halves(v)
            high_ref[pl.ds(64 * at + other, 32), lanes] = high
            low_ref[pl.ds(64 * at + other, 32), lanes] = low
        if i % CHUNK == CHUNK - 1:
            span = slice((i + 1 - CHUNK) * BLK, (i + 1) * BLK)
            dims = (((1,), (1,)), ((), ()))
            left = left_ref[...]
            part = lax.dot_general(left, high_ref[:, span], dims, preferred_element_type=F32)
            part = part + lax.dot_general(left, low_ref[:, span], dims, preferred_element_type=F32)
            acc[...] = part if i < CHUNK else acc[...] + part

    total = acc[0:192] + acc[192:384]
    out_ref[0:192, :] = total[:, 0:BLK]
    out_ref[192:384, :] = jnp.concatenate([total[:, BLK:192], jnp.zeros((192, 64), F32)], axis=1)


def second_image(info, pattern, split, sums, scaled, across_odd, across_even, s, x, y, p, xo, yo, po):
    n = s.shape[0]
    return pl.pallas_call(
        second_kernel,
        in_specs=memory(pltpu.SMEM, pltpu.SMEM, pl.ANY, *[pltpu.VMEM] * 11),
        out_shape=[jax.ShapeDtypeStruct((192, x.shape[1]), BF16)] * 2 + [jax.ShapeDtypeStruct((384, BLK), F32)],
        scratch_shapes=[
            pltpu.VMEM(split.shape, BF16),
            pltpu.VMEM((3 * n, BLK, BLK), BF16),
            pltpu.VMEM((64, BLK), F32),
            pltpu.VMEM((384, CHUNK * BLK), BF16),
            pltpu.VMEM((384, 192), F32),
            pltpu.SemaphoreType.DMA((n,)),
        ],
        compiler_params=pltpu.CompilerParams(vmem_limit_bytes=VMEM_LIMIT),
        cost_estimate=pl.CostEstimate(flops=8 * 10**9, bytes_accessed=18 * 10**6, transcendentals=0),
        name="second_image",
    )(info, pattern, split, sums, scaled, across_odd, across_even, s, x, y, p, xo, yo, po)


def picked_row(groups, at):
    return jnp.broadcast_to(groups[at // 8][at % 8 : at % 8 + 1, :], (8, BLK))


def inverse_factor(block):
    lane = lax.broadcasted_iota(jnp.int32, (8, BLK), 1)
    sub = lax.broadcasted_iota(jnp.int32, (8, BLK), 0)
    a = []
    for g in range(4):
        unit = jnp.where(lane - 32 == sub + 8 * g, 1.0, 0.0)
        a.append(jnp.where(lane < 32, block[8 * g : 8 * g + 8, :], unit))
    for start in range(0, 32, PIVOTS):
        columns = [
            [jnp.broadcast_to(a[g][:, start + k : start + k + 1], (8, BLK)) if g >= start // 8 else None for g in range(4)]
            for k in range(PIVOTS)
        ]
        for k in range(PIVOTS):
            at = start + k
            own = at // 8
            pivot = 1.0 / picked_row(columns[k], at)
            factor = [columns[k][g] * pivot if g >= own else None for g in range(4)]
            factor[own] = jnp.where(sub > at % 8, factor[own], 0.0)
            for other in columns[k + 1 :]:
                e = picked_row(other, at)
                for g in range(own, 4):
                    other[g] = other[g] - factor[g] * e
            row = picked_row(a, at)
            for g in range(own, 4):
                a[g] = a[g] - factor[g] * row
    scaled = []
    for g in range(4):
        diagonal = jnp.sum(jnp.where(lane == sub + 8 * g, a[g], 0.0), axis=1, keepdims=True)
        scaled.append(a[g] * lax.rsqrt(diagonal))
    return jnp.concatenate(scaled, axis=0)[:, 32:64]


def exact(left, right, dims):
    return lax.dot_general(left, right, (dims, ((), ())), precision=EXACT, preferred_element_type=F32)


def inverse_cholesky(work, inverse):
    lane = lax.broadcasted_iota(jnp.int32, (32, 192), 1)
    sub = lax.broadcasted_iota(jnp.int32, (32, 192), 0)
    for at in range(0, 192, 32):
        rows = work[at : at + 32, :]
        if at < BLK:
            piece = rows[:, 0:BLK]
        else:
            piece = jnp.concatenate([rows[:, BLK:192], jnp.zeros((32, 64), F32)], axis=1)
        if at % BLK:
            piece = pltpu.roll(piece, BLK - at % BLK, 1)
        small = inverse_factor(piece)
        unit = jnp.where(lane - at == sub, 1.0, 0.0)
        rows = jnp.where((lane >= at) & (lane < at + 32), unit, rows)
        new = exact(small, rows, ((1,), (0,)))
        inverse[at : at + 32, :] = jnp.where(lane < at + 32, new, 0.0)
        if at < 160:
            update = exact(new, new, ((0,), (0,)))
            wide = lax.broadcasted_iota(jnp.int32, (160 - at, 192), 1)
            old = jnp.where((wide >= at) & (wide < at + 32), 0.0, work[at + 32 : 192, :])
            work[at + 32 : 192, :] = old - update[at + 32 : 192, :]


def final_kernel(
    both_ref, chosen_ref, high_ref, low_ref, vectors_ref, directions_ref, ritz_ref, work, raw, inverse, *, factor
):
    for at in range(6):
        for base, target in ((0, work), (96, raw)):
            row = 384 * (at % 2) + base + 32 * (at // 2)
            target[32 * at : 32 * at + 32, 0:BLK] = both_ref[row : row + 32, :]
            target[32 * at : 32 * at + 32, BLK:192] = both_ref[row + 192 : row + 224, 0:64]
    inverse_cholesky(work, inverse)
    whole_inverse = inverse[...]
    half = exact(whole_inverse, raw[...], ((1,), (1,)))
    ritz_ref[...] = exact(half, whole_inverse, ((1,), (1,)))
    mix = factor * exact(chosen_ref[...], whole_inverse, ((1,), (0,)))
    left = jnp.concatenate(halves(mix), axis=0)
    for at in range(0, high_ref.shape[1], 512):
        lanes = slice(at, at + 512)
        product = jnp.dot(left, high_ref[:, lanes], preferred_element_type=F32)
        product = product + jnp.dot(left, low_ref[:, lanes], preferred_element_type=F32)
        product = product[0:64] + product[64:128]
        vectors_ref[:, lanes] = product[0:32]
        directions_ref[:, lanes] = product[32:64]


def final(both, chosen, high, low, factor):
    return pl.pallas_call(
        functools.partial(final_kernel, factor=factor),
        in_specs=memory(*[pltpu.VMEM] * 4),
        out_shape=[jax.ShapeDtypeStruct((32, high.shape[1]), F32)] * 2 + [jax.ShapeDtypeStruct((192, 192), F32)],
        scratch_shapes=[pltpu.VMEM((192, 192), F32)] * 3,
        compiler_params=pltpu.CompilerParams(vmem_limit_bytes=VMEM_LIMIT),
        cost_estimate=pl.CostEstimate(flops=4 * 10**8, bytes_accessed=4 * 10**6, transcendentals=0),
        name="final",
    )(both, chosen, high, low)


def other_core(x):
    return lax.ppermute(x, "cols", [(0, 1), (1, 0)])


def local(vectors, directions, affinity, pattern, rotation):
    width, rows_dev = vectors.shape
    devices = lax.axis_size("rows")
    core = lax.axis_index("cols")
    total = 2 * width
    nodes = rows_dev * devices
    local_blocks = affinity.shape[0]
    all_blocks = local_blocks * devices
    place = lax.axis_index("rows")
    first_block = (place - 1) * local_blocks
    info = jnp.stack([core, first_block, jnp.int32(all_blocks), place % 2]).astype(jnp.int32)
    scale, xs = degrees(affinity, vectors)
    xs_odd, xs_even = from_neighbours(xs)
    split = split_affinity(affinity, scale)
    x_other = other_core(vectors)
    p_other = other_core(directions)
    y, scaled, sums = first_image(info, pattern, split, vectors, xs, xs_odd, xs_even, directions, scale)
    scaled_odd, scaled_even = from_neighbours(scaled)
    y_other = other_core(y)
    half = sums[:, 0:64]
    blank = jnp.zeros_like(half)
    row = jnp.where(core == 0, jnp.concatenate([half, blank], axis=1), jnp.concatenate([blank, half], axis=1))
    sums = lax.all_to_all(repeated(row, 2 * devices), ("rows", "cols"), 0, 0).reshape(2 * devices, BLK)
    high, low, part = second_image(
        info, pattern, split, sums, scaled, scaled_odd, scaled_even, scale, vectors, y, directions, x_other, y_other, p_other
    )
    both = sum_large(part.reshape(16, 24, BLK)).reshape(768, BLK)
    mine = lambda m: lax.dynamic_slice_in_dim(m, core * width, width, 1)
    kept = jnp.concatenate([rotation[:total], jnp.zeros((total, total), F32), rotation[2 * total :]], axis=0)
    chosen = jnp.concatenate([mine(rotation), mine(kept)], axis=1).T
    new_vectors, new_directions, ritz_matrix = final(both, chosen, high, low, math.sqrt(nodes))
    return new_vectors, new_directions, ritz_matrix


def solution(mesh):
    in_specs = (P("cols", "rows"), P("cols", "rows"), P("rows", None, None, None), P("rows", None), P())
    out_specs = (P("cols", "rows"), P("cols", "rows"), P())
    return jax.shard_map(local, mesh=mesh, in_specs=in_specs, out_specs=out_specs, check_vma=False)
```

```python
import functools
import math

import jax
import jax.numpy as jnp
from jax import lax
from jax.experimental import pallas as pl
from jax.experimental.pallas import tpu as pltpu
from jax.sharding import PartitionSpec as P

BLK = 128
F32 = jnp.float32
BF16 = jnp.bfloat16
UNROLL = 24
GROUP = 6
CHUNK = 4
VMEM_LIMIT = 60 * 2**20
PIVOTS = 16
EXACT = lax.Precision.HIGHEST


def halves(v):
    high = v.astype(BF16)
    return high, (v - high.astype(F32)).astype(BF16)


def swaps(devices, first):
    return [pair for i in range(first, devices, 2) for pair in ((i, (i + 1) % devices), ((i + 1) % devices, i))]


def from_neighbours(x):
    devices = lax.axis_size("rows")
    return [lax.ppermute(x, "rows", swaps(devices, first)) for first in (1, 0)]


def row_of(z, x, y):
    return z * 16 + x * 4 + y


def plane_groups():
    return [[row_of(z, x, y) for x in range(4) for y in range(4)] for z in range(8)]


def column_groups():
    return [[row_of(z, x, y) for z in range(8)] for x in range(4) for y in range(4)]


def with_cores(groups):
    return [[2 * i + core for core in range(2) for i in group] for group in groups]


def exchange(x, groups):
    return lax.all_to_all(x, "rows", 0, 0, axis_index_groups=groups)


def exchange_cores(x, groups):
    return lax.all_to_all(x, ("rows", "cols"), 0, 0, axis_index_groups=with_cores(groups))


def repeated(x, count):
    return jnp.broadcast_to(x[None], (count,) + x.shape)


def sum_large(x):
    part = jnp.sum(exchange(x, plane_groups()), axis=0)
    part = jnp.sum(exchange(repeated(part, 8), column_groups()), axis=0)
    return exchange_cores(repeated(part, 32), plane_groups())


def loads(a_hbm, a_ref, arrived):
    copies = [pltpu.make_async_copy(a_hbm.at[i], a_ref.at[i], arrived.at[i]) for i in range(a_hbm.shape[0])]
    for copy in copies:
        copy.start()
    return copies


def wait_group(copies, i):
    if i % GROUP == 0:
        for copy in copies[i : i + GROUP]:
            copy.wait()


def memory(*spaces):
    return [pl.BlockSpec(memory_space=space) for space in spaces]


def degree_kernel(a_hbm, x_ref, scale_ref, xs_ref, a_ref, arrived):
    copies = loads(a_hbm, a_ref, arrived)
    for i in range(a_ref.shape[0]):
        wait_group(copies, i)
        total = a_ref[i, 0]
        for k in range(1, 6):
            total = total + a_ref[i, k]
        scale = lax.rsqrt(jnp.sum(total.T, axis=0, keepdims=True))
        scale_ref[i : i + 1, :] = scale
        lanes = slice(i * BLK, (i + 1) * BLK)
        xs_ref[:, lanes] = x_ref[:, lanes] * scale


def degrees(affinity, x):
    n = affinity.shape[0]
    return pl.pallas_call(
        degree_kernel,
        in_specs=memory(pl.ANY, pltpu.VMEM),
        out_shape=[jax.ShapeDtypeStruct((n, BLK), F32), jax.ShapeDtypeStruct(x.shape, F32)],
        scratch_shapes=[pltpu.VMEM(affinity.shape, F32), pltpu.SemaphoreType.DMA((n,))],
        compiler_params=pltpu.CompilerParams(vmem_limit_bytes=VMEM_LIMIT),
        cost_estimate=pl.CostEstimate(flops=10**7, bytes_accessed=10**7, transcendentals=3072),
        name="degrees",
    )(affinity, x)


def split_kernel(a_hbm, scale_ref, p_ref, split_hbm, ps_ref, a_ref, split_ref, arrived, sent):
    count = a_ref.shape[0]
    copies = loads(a_hbm, a_ref, arrived)
    sends = [pltpu.make_async_copy(split_ref.at[i], split_hbm.at[i], sent.at[i]) for i in range(count)]
    for i in range(count):
        lanes = slice(i * BLK, (i + 1) * BLK)
        ps_ref[:, lanes] = p_ref[:, lanes] * scale_ref[i : i + 1, :]
    for i in range(count):
        wait_group(copies, i)
        for k in range(6):
            high, low = halves(a_ref[i, k])
            split_ref[i, 0:BLK, k * BLK : (k + 1) * BLK] = high
            split_ref[i, BLK : 2 * BLK, k * BLK : (k + 1) * BLK] = low
        if i % GROUP == GROUP - 1:
            for copy in sends[i + 1 - GROUP : i + 1]:
                copy.start()
    for copy in sends:
        copy.wait()


def split_affinity(affinity, scale, p):
    n = affinity.shape[0]
    split = (n, 2 * BLK, 6 * BLK)
    return pl.pallas_call(
        split_kernel,
        in_specs=memory(pl.ANY, pltpu.VMEM, pltpu.VMEM),
        out_specs=memory(pl.ANY, pltpu.VMEM),
        out_shape=[jax.ShapeDtypeStruct(split, BF16), jax.ShapeDtypeStruct(p.shape, F32)],
        scratch_shapes=[
            pltpu.VMEM((n, 6, BLK, BLK), F32),
            pltpu.VMEM(split, BF16),
            pltpu.SemaphoreType.DMA((n,)),
            pltpu.SemaphoreType.DMA((n,)),
        ],
        compiler_params=pltpu.CompilerParams(vmem_limit_bytes=VMEM_LIMIT),
        cost_estimate=pl.CostEstimate(flops=10**7, bytes_accessed=19 * 10**6, transcendentals=0),
        name="split",
    )(affinity, scale, p)


def block_of(ref, i):
    return ref[:, pl.ds(pl.multiple_of(i * BLK, BLK), BLK)]


def local_place(index, first, total):
    place = index - first
    place = jnp.where(place < 0, place + total, place)
    return jnp.where(place >= total, place - total, place)


def gathered(info, pat, turned, i):
    places = [local_place(pat[i, k], info[1], info[2]) for k in range(6)]
    return jnp.concatenate([turned[place] for place in places], axis=0)


def turn_all(turned, odd, triples, count):
    for part, refs in zip((2 * odd, 1, 2 - 2 * odd), triples):

        @pl.loop(0, count, unroll=UNROLL)
        def _(j):
            stack = []
            for v_ref in refs:
                v = block_of(v_ref, j)
                high = v.astype(BF16).astype(F32)
                stack += [high, v - high]
            if len(refs) == 1:
                stack.append(jnp.zeros((64, BLK), F32))
            turned[part * count + j] = jnp.concatenate(stack, axis=0).T.astype(BF16)


def first_kernel(
    info, pat, a_hbm, x_ref, xs_ref, across_odd_ref, across_even_ref, s_ref, y_ref, ys_ref, sums_ref, split_ref, turned, arrived
):
    count = s_ref.shape[0]
    copies = loads(a_hbm, split_ref, arrived)
    turn_all(turned, info[3], ((across_odd_ref,), (xs_ref,), (across_even_ref,)), count)
    xy = jnp.zeros((32, BLK), F32)
    xx = jnp.zeros((32, BLK), F32)
    for i in range(count):
        lanes = slice(i * BLK, (i + 1) * BLK)
        wait_group(copies, i)
        weights = gathered(info, pat, turned, i)
        product = jnp.dot(split_ref[i], weights, preferred_element_type=F32)
        image = (product[:BLK] + product[BLK:]).T
        x, s = x_ref[:, lanes], s_ref[i : i + 1, :]
        y = x - s * (image[0:32] + image[32:64])
        y_ref[:, lanes] = y
        ys_ref[:, lanes] = s * y
        xy += x * y
        xx += x * x
    stack = jnp.concatenate([xy, xx, jnp.zeros((64, BLK), F32)], axis=0)
    sums_ref[...] = jnp.sum(stack.T, axis=0, keepdims=True)


def first_image(info, pattern, split, x, xs, across_odd, across_even, s):
    n = s.shape[0]
    return pl.pallas_call(
        first_kernel,
        in_specs=memory(pltpu.SMEM, pltpu.SMEM, pl.ANY, *[pltpu.VMEM] * 5),
        out_shape=[
            jax.ShapeDtypeStruct(x.shape, F32),
            jax.ShapeDtypeStruct(x.shape, F32),
            jax.ShapeDtypeStruct((1, BLK), F32),
        ],
        scratch_shapes=[
            pltpu.VMEM(split.shape, BF16),
            pltpu.VMEM((3 * n, BLK, BLK), BF16),
            pltpu.SemaphoreType.DMA((n,)),
        ],
        compiler_params=pltpu.CompilerParams(vmem_limit_bytes=VMEM_LIMIT),
        cost_estimate=pl.CostEstimate(flops=4 * 10**9, bytes_accessed=11 * 10**6, transcendentals=0),
        name="first_image",
    )(info, pattern, split, x, xs, across_odd, across_even, s)


def second_kernel(
    info, pat, a_hbm, ys_ref, ys_odd_ref, ys_even_ref, ps_ref, ps_odd_ref, ps_even_ref, s_ref, y_ref, p_ref,
    z_ref, image_ref, split_ref, turned, arrived,
):
    count = s_ref.shape[0]
    copies = loads(a_hbm, split_ref, arrived)
    turn_all(turned, info[3], ((ys_odd_ref, ps_odd_ref), (ys_ref, ps_ref), (ys_even_ref, ps_even_ref)), count)
    for i in range(count):
        lanes = slice(i * BLK, (i + 1) * BLK)
        wait_group(copies, i)
        weights = gathered(info, pat, turned, i)
        product = jnp.dot(split_ref[i], weights, preferred_element_type=F32)
        image = (product[:BLK] + product[BLK:]).T
        s = s_ref[i : i + 1, :]
        z_ref[:, lanes] = y_ref[:, lanes] - s * (image[0:32] + image[32:64])
        image_ref[:, lanes] = p_ref[:, lanes] - s * (image[64:96] + image[96:128])


def second_image(info, pattern, split, ys, ys_odd, ys_even, ps, ps_odd, ps_even, s, y, p):
    n = s.shape[0]
    return pl.pallas_call(
        second_kernel,
        in_specs=memory(pltpu.SMEM, pltpu.SMEM, pl.ANY, *[pltpu.VMEM] * 9),
        out_shape=[jax.ShapeDtypeStruct(y.shape, F32)] * 2,
        scratch_shapes=[
            pltpu.VMEM(split.shape, BF16),
            pltpu.VMEM((3 * n, BLK, BLK), BF16),
            pltpu.SemaphoreType.DMA((n,)),
        ],
        compiler_params=pltpu.CompilerParams(vmem_limit_bytes=VMEM_LIMIT),
        cost_estimate=pl.CostEstimate(flops=4 * 10**9, bytes_accessed=14 * 10**6, transcendentals=0),
        name="second_image",
    )(info, pattern, split, ys, ys_odd, ys_even, ps, ps_odd, ps_even, s, y, p)


def products_kernel(
    info, sums_ref, x_ref, y_ref, p_ref, xo_ref, yo_ref, po_ref, z_ref, image_ref, high_ref, low_ref, out_ref, quotients, left_ref, acc
):
    core = info[0]
    own = pl.multiple_of(core * 32, 32)
    other = pl.multiple_of((1 - core) * 32, 32)
    sums = jnp.sum(sums_ref[...], axis=0, keepdims=True)
    column = jnp.broadcast_to(sums, (BLK, BLK)).T
    quotients[0:32] = column[0:32] / column[32:64]
    quotients[32:64] = column[64:96] / column[96:128]
    q_own = quotients[pl.ds(own, 32), :]
    q_other = quotients[pl.ds(other, 32), :]
    for i in range(x_ref.shape[1] // BLK):
        lanes = slice(i * BLK, (i + 1) * BLK)
        place = slice(i % CHUNK * BLK, (i % CHUNK + 1) * BLK)
        x, y = x_ref[:, lanes], y_ref[:, lanes]
        rows = (y - q_own * x, x, p_ref[:, lanes], z_ref[:, lanes] - q_own * y, y, image_ref[:, lanes])
        for at, v in enumerate(rows):
            high, low = halves(v)
            left_ref[32 * at : 32 * at + 32, place] = high
            left_ref[192 + 32 * at : 224 + 32 * at, place] = low
            if at < 3:
                high_ref[pl.ds(64 * at + own, 32), lanes] = high
                low_ref[pl.ds(64 * at + own, 32), lanes] = low
        xo = xo_ref[:, lanes]
        for at, v in enumerate((yo_ref[:, lanes] - q_other * xo, xo, po_ref[:, lanes])):
            high, low = halves(v)
            high_ref[pl.ds(64 * at + other, 32), lanes] = high
            low_ref[pl.ds(64 * at + other, 32), lanes] = low
        if i % CHUNK == CHUNK - 1:
            span = slice((i + 1 - CHUNK) * BLK, (i + 1) * BLK)
            dims = (((1,), (1,)), ((), ()))
            left = left_ref[...]
            part = lax.dot_general(left, high_ref[:, span], dims, preferred_element_type=F32)
            part = part + lax.dot_general(left, low_ref[:, span], dims, preferred_element_type=F32)
            acc[...] = part if i < CHUNK else acc[...] + part

    total = acc[0:192] + acc[192:384]
    out_ref[0:192, :] = total[:, 0:BLK]
    out_ref[192:384, :] = jnp.concatenate([total[:, BLK:192], jnp.zeros((192, 64), F32)], axis=1)


def products(info, sums, x, y, p, xo, yo, po, z, image):
    return pl.pallas_call(
        products_kernel,
        in_specs=memory(pltpu.SMEM, *[pltpu.VMEM] * 9),
        out_shape=[jax.ShapeDtypeStruct((192, x.shape[1]), BF16)] * 2 + [jax.ShapeDtypeStruct((384, BLK), F32)],
        scratch_shapes=[
            pltpu.VMEM((64, BLK), F32),
            pltpu.VMEM((384, CHUNK * BLK), BF16),
            pltpu.VMEM((384, 192), F32),
        ],
        compiler_params=pltpu.CompilerParams(vmem_limit_bytes=VMEM_LIMIT),
        cost_estimate=pl.CostEstimate(flops=2 * 10**9, bytes_accessed=6 * 10**6, transcendentals=0),
        name="products",
    )(info, sums, x, y, p, xo, yo, po, z, image)


def picked_row(groups, at):
    return jnp.broadcast_to(groups[at // 8][at % 8 : at % 8 + 1, :], (8, BLK))


def inverse_factor(block):
    lane = lax.broadcasted_iota(jnp.int32, (8, BLK), 1)
    sub = lax.broadcasted_iota(jnp.int32, (8, BLK), 0)
    a = []
    for g in range(4):
        unit = jnp.where(lane - 32 == sub + 8 * g, 1.0, 0.0)
        a.append(jnp.where(lane < 32, block[8 * g : 8 * g + 8, :], unit))
    for start in range(0, 32, PIVOTS):
        columns = [
            [jnp.broadcast_to(a[g][:, start + k : start + k + 1], (8, BLK)) if g >= start // 8 else None for g in range(4)]
            for k in range(PIVOTS)
        ]
        for k in range(PIVOTS):
            at = start + k
            own = at // 8
            pivot = 1.0 / picked_row(columns[k], at)
            factor = [columns[k][g] * pivot if g >= own else None for g in range(4)]
            factor[own] = jnp.where(sub > at % 8, factor[own], 0.0)
            for other in columns[k + 1 :]:
                e = picked_row(other, at)
                for g in range(own, 4):
                    other[g] = other[g] - factor[g] * e
            row = picked_row(a, at)
            for g in range(own, 4):
                a[g] = a[g] - factor[g] * row
    scaled = []
    for g in range(4):
        diagonal = jnp.sum(jnp.where(lane == sub + 8 * g, a[g], 0.0), axis=1, keepdims=True)
        scaled.append(a[g] * lax.rsqrt(diagonal))
    return jnp.concatenate(scaled, axis=0)[:, 32:64]


def exact(left, right, dims):
    return lax.dot_general(left, right, (dims, ((), ())), precision=EXACT, preferred_element_type=F32)


def inverse_cholesky(work, inverse):
    lane = lax.broadcasted_iota(jnp.int32, (32, 192), 1)
    sub = lax.broadcasted_iota(jnp.int32, (32, 192), 0)
    for at in range(0, 192, 32):
        rows = work[at : at + 32, :]
        if at < BLK:
            piece = rows[:, 0:BLK]
        else:
            piece = jnp.concatenate([rows[:, BLK:192], jnp.zeros((32, 64), F32)], axis=1)
        if at % BLK:
            piece = pltpu.roll(piece, BLK - at % BLK, 1)
        small = inverse_factor(piece)
        unit = jnp.where(lane - at == sub, 1.0, 0.0)
        rows = jnp.where((lane >= at) & (lane < at + 32), unit, rows)
        new = exact(small, rows, ((1,), (0,)))
        inverse[at : at + 32, :] = jnp.where(lane < at + 32, new, 0.0)
        if at < 160:
            update = exact(new, new, ((0,), (0,)))
            wide = lax.broadcasted_iota(jnp.int32, (160 - at, 192), 1)
            old = jnp.where((wide >= at) & (wide < at + 32), 0.0, work[at + 32 : 192, :])
            work[at + 32 : 192, :] = old - update[at + 32 : 192, :]


def final_kernel(
    both_ref, chosen_ref, high_ref, low_ref, vectors_ref, directions_ref, ritz_ref, work, raw, inverse, *, factor
):
    for at in range(6):
        for base, target in ((0, work), (96, raw)):
            row = 384 * (at % 2) + base + 32 * (at // 2)
            target[32 * at : 32 * at + 32, 0:BLK] = both_ref[row : row + 32, :]
            target[32 * at : 32 * at + 32, BLK:192] = both_ref[row + 192 : row + 224, 0:64]
    inverse_cholesky(work, inverse)
    whole_inverse = inverse[...]
    half = exact(whole_inverse, raw[...], ((1,), (1,)))
    ritz_ref[...] = exact(half, whole_inverse, ((1,), (1,)))
    mix = factor * exact(chosen_ref[...], whole_inverse, ((1,), (0,)))
    left = jnp.concatenate(halves(mix), axis=0)
    for at in range(0, high_ref.shape[1], 512):
        lanes = slice(at, at + 512)
        product = jnp.dot(left, high_ref[:, lanes], preferred_element_type=F32)
        product = product + jnp.dot(left, low_ref[:, lanes], preferred_element_type=F32)
        product = product[0:64] + product[64:128]
        vectors_ref[:, lanes] = product[0:32]
        directions_ref[:, lanes] = product[32:64]


def final(both, chosen, high, low, factor):
    return pl.pallas_call(
        functools.partial(final_kernel, factor=factor),
        in_specs=memory(*[pltpu.VMEM] * 4),
        out_shape=[jax.ShapeDtypeStruct((32, high.shape[1]), F32)] * 2 + [jax.ShapeDtypeStruct((192, 192), F32)],
        scratch_shapes=[pltpu.VMEM((192, 192), F32)] * 3,
        compiler_params=pltpu.CompilerParams(vmem_limit_bytes=VMEM_LIMIT),
        cost_estimate=pl.CostEstimate(flops=4 * 10**8, bytes_accessed=4 * 10**6, transcendentals=0),
        name="final",
    )(both, chosen, high, low)


def other_core(x):
    return lax.ppermute(x, "cols", [(0, 1), (1, 0)])


def local(vectors, directions, affinity, pattern, rotation):
    width, rows_dev = vectors.shape
    devices = lax.axis_size("rows")
    core = lax.axis_index("cols")
    total = 2 * width
    nodes = rows_dev * devices
    local_blocks = affinity.shape[0]
    all_blocks = local_blocks * devices
    place = lax.axis_index("rows")
    first_block = (place - 1) * local_blocks
    info = jnp.stack([core, first_block, jnp.int32(all_blocks), place % 2]).astype(jnp.int32)
    scale, xs = degrees(affinity, vectors)
    xs_odd, xs_even = from_neighbours(xs)
    split, ps = split_affinity(affinity, scale, directions)
    ps_odd, ps_even = from_neighbours(ps)
    x_other = other_core(vectors)
    p_other = other_core(directions)
    y, ys, sums = first_image(info, pattern, split, vectors, xs, xs_odd, xs_even, scale)
    ys_odd, ys_even = from_neighbours(ys)
    y_other = other_core(y)
    half = sums[:, 0:64]
    blank = jnp.zeros_like(half)
    row = jnp.where(core == 0, jnp.concatenate([half, blank], axis=1), jnp.concatenate([blank, half], axis=1))
    sums = lax.all_to_all(repeated(row, 2 * devices), ("rows", "cols"), 0, 0).reshape(2 * devices, BLK)
    z, image = second_image(info, pattern, split, ys, ys_odd, ys_even, ps, ps_odd, ps_even, scale, y, directions)
    high, low, part = products(info, sums, vectors, y, directions, x_other, y_other, p_other, z, image)
    both = sum_large(part.reshape(16, 24, BLK)).reshape(768, BLK)
    mine = lambda m: lax.dynamic_slice_in_dim(m, core * width, width, 1)
    kept = jnp.concatenate([rotation[:total], jnp.zeros((total, total), F32), rotation[2 * total :]], axis=0)
    chosen = jnp.concatenate([mine(rotation), mine(kept)], axis=1).T
    new_vectors, new_directions, ritz_matrix = final(both, chosen, high, low, math.sqrt(nodes))
    return new_vectors, new_directions, ritz_matrix


def solution(mesh):
    in_specs = (P("cols", "rows"), P("cols", "rows"), P("rows", None, None, None), P("rows", None), P())
    out_specs = (P("cols", "rows"), P("cols", "rows"), P())
    return jax.shard_map(local, mesh=mesh, in_specs=in_specs, out_specs=out_specs, check_vma=False)
```

```python
import functools
import math

import jax
import jax.numpy as jnp
from jax import lax
from jax.experimental import pallas as pl
from jax.experimental.pallas import tpu as pltpu
from jax.sharding import PartitionSpec as P

BLK = 128
F32 = jnp.float32
BF16 = jnp.bfloat16
UNROLL = 24
GROUP = 6
WIDE_GROUP = 12
PIECE = 64
CHUNK = 4
VMEM_LIMIT = 60 * 2**20
PIVOTS = 16
EXACT = lax.Precision.HIGHEST


def halves(v):
    high = v.astype(BF16)
    return high, (v - high.astype(F32)).astype(BF16)


def swaps(devices, first):
    return [pair for i in range(first, devices, 2) for pair in ((i, (i + 1) % devices), ((i + 1) % devices, i))]


def from_neighbours(x):
    devices = lax.axis_size("rows")
    return [lax.ppermute(x, "rows", swaps(devices, first)) for first in (1, 0)]


def row_of(z, x, y):
    return z * 16 + x * 4 + y


def plane_groups():
    return [[row_of(z, x, y) for x in range(4) for y in range(4)] for z in range(8)]


def column_groups():
    return [[row_of(z, x, y) for z in range(8)] for x in range(4) for y in range(4)]


def with_cores(groups):
    return [[2 * i + core for core in range(2) for i in group] for group in groups]


def exchange(x, groups):
    return lax.all_to_all(x, "rows", 0, 0, axis_index_groups=groups)


def exchange_cores(x, groups):
    return lax.all_to_all(x, ("rows", "cols"), 0, 0, axis_index_groups=with_cores(groups))


def repeated(x, count):
    return jnp.broadcast_to(x[None], (count,) + x.shape)


def sum_large(x):
    part = jnp.sum(exchange(x, plane_groups()), axis=0)
    part = jnp.sum(exchange(repeated(part, 8), column_groups()), axis=0)
    return exchange_cores(repeated(part, 32), plane_groups())


def loads(a_hbm, a_ref, arrived):
    copies = [pltpu.make_async_copy(a_hbm.at[i], a_ref.at[i], arrived.at[i]) for i in range(a_hbm.shape[0])]
    for copy in copies:
        copy.start()
    return copies


def wait_group(copies, i, group):
    if i % group == 0:
        for copy in copies[i : i + group]:
            copy.wait()


def memory(*spaces):
    return [pl.BlockSpec(memory_space=space) for space in spaces]


def degree_kernel(a_hbm, x_hbm, scale_ref, xs_hbm, a_ref, x_ref, xs_ref, arrived, x_arrived, sent):
    count = a_ref.shape[0]
    copies = loads(a_hbm, a_ref, arrived)
    x_copy = pltpu.make_async_copy(x_hbm, x_ref, x_arrived)
    x_copy.start()
    sends = []
    for i in range(count):
        wait_group(copies, i, GROUP)
        if i == 0:
            x_copy.wait()
        total = a_ref[i, 0]
        for k in range(1, 6):
            total = total + a_ref[i, k]
        scale = lax.rsqrt(jnp.sum(total.T, axis=0, keepdims=True))
        scale_ref[i : i + 1, :] = scale
        lanes = slice(i * BLK, (i + 1) * BLK)
        xs_ref[:, lanes] = x_ref[:, lanes] * scale
        if i % GROUP == GROUP - 1:
            span = pl.ds((i + 1 - GROUP) * BLK, GROUP * BLK)
            sends.append(pltpu.make_async_copy(xs_ref.at[:, span], xs_hbm.at[:, span], sent.at[i // GROUP]))
            sends[-1].start()
    for copy in sends:
        copy.wait()


def degrees(affinity, x):
    n = affinity.shape[0]
    return pl.pallas_call(
        degree_kernel,
        in_specs=memory(pl.ANY, pl.ANY),
        out_specs=memory(pltpu.VMEM, pl.ANY),
        out_shape=[jax.ShapeDtypeStruct((n, BLK), F32), jax.ShapeDtypeStruct(x.shape, F32)],
        scratch_shapes=[
            pltpu.VMEM(affinity.shape, F32),
            pltpu.VMEM(x.shape, F32),
            pltpu.VMEM(x.shape, F32),
            pltpu.SemaphoreType.DMA((n,)),
            pltpu.SemaphoreType.DMA,
            pltpu.SemaphoreType.DMA((n // GROUP,)),
        ],
        compiler_params=pltpu.CompilerParams(vmem_limit_bytes=VMEM_LIMIT),
        cost_estimate=pl.CostEstimate(flops=10**7, bytes_accessed=10**7, transcendentals=3072),
        name="degrees",
    )(affinity, x)


def split_kernel(a_hbm, scale_ref, p_ref, split_hbm, ps_ref, a_ref, split_ref, arrived, sent):
    count = a_ref.shape[0]
    copies = loads(a_hbm, a_ref, arrived)
    sends = [pltpu.make_async_copy(split_ref.at[i], split_hbm.at[i], sent.at[i]) for i in range(count)]
    for i in range(count):
        lanes = slice(i * BLK, (i + 1) * BLK)
        ps_ref[:, lanes] = p_ref[:, lanes] * scale_ref[i : i + 1, :]
    for i in range(count):
        wait_group(copies, i, WIDE_GROUP)
        for k in range(6):
            high, low = halves(a_ref[i, k])
            split_ref[i, 0:BLK, k * BLK : (k + 1) * BLK] = high
            split_ref[i, BLK : 2 * BLK, k * BLK : (k + 1) * BLK] = low
        if i % WIDE_GROUP == WIDE_GROUP - 1:
            for copy in sends[i + 1 - WIDE_GROUP : i + 1]:
                copy.start()
    for copy in sends:
        copy.wait()


def split_affinity(affinity, scale, p):
    n = affinity.shape[0]
    split = (n, 2 * BLK, 6 * BLK)
    return pl.pallas_call(
        split_kernel,
        in_specs=memory(pl.ANY, pltpu.VMEM, pltpu.VMEM),
        out_specs=memory(pl.ANY, pltpu.VMEM),
        out_shape=[jax.ShapeDtypeStruct(split, BF16), jax.ShapeDtypeStruct(p.shape, F32)],
        scratch_shapes=[
            pltpu.VMEM((n, 6, BLK, BLK), F32),
            pltpu.VMEM(split, BF16),
            pltpu.SemaphoreType.DMA((n,)),
            pltpu.SemaphoreType.DMA((n,)),
        ],
        compiler_params=pltpu.CompilerParams(vmem_limit_bytes=VMEM_LIMIT),
        cost_estimate=pl.CostEstimate(flops=10**7, bytes_accessed=19 * 10**6, transcendentals=0),
        name="split",
    )(affinity, scale, p)


def block_of(ref, i):
    return ref[:, pl.ds(pl.multiple_of(i * BLK, BLK), BLK)]


def local_place(index, first, total):
    place = index - first
    place = jnp.where(place < 0, place + total, place)
    return jnp.where(place >= total, place - total, place)


def gathered(info, pat, turned, i):
    places = [local_place(pat[k, i], info[1], info[2]) for k in range(6)]
    return jnp.concatenate([turned[place] for place in places], axis=0)


def turn_all(turned, odd, triples, count):
    for part, refs in zip((2 * odd, 1, 2 - 2 * odd), triples):

        @pl.loop(0, count, unroll=UNROLL)
        def _(j):
            stack = []
            for v_ref in refs:
                v = block_of(v_ref, j)
                high = v.astype(BF16).astype(F32)
                stack += [high, v - high]
            if len(refs) == 1:
                stack.append(jnp.zeros((64, BLK), F32))
            turned[part * count + j] = jnp.concatenate(stack, axis=0).T.astype(BF16)


def first_kernel(
    info, pat, a_hbm, x_ref, xs_ref, across_odd_ref, across_even_ref, s_ref, y_ref, ys_ref, sums_ref, split_ref, turned, arrived
):
    count = s_ref.shape[0]
    copies = loads(a_hbm, split_ref, arrived)
    turn_all(turned, info[3], ((across_odd_ref,), (xs_ref,), (across_even_ref,)), count)
    xy = jnp.zeros((32, BLK), F32)
    xx = jnp.zeros((32, BLK), F32)
    for i in range(count):
        lanes = slice(i * BLK, (i + 1) * BLK)
        wait_group(copies, i, GROUP)
        weights = gathered(info, pat, turned, i)
        product = jnp.dot(split_ref[i], weights, preferred_element_type=F32)
        image = (product[:BLK] + product[BLK:]).T
        x, s = x_ref[:, lanes], s_ref[i : i + 1, :]
        y = x - s * (image[0:32] + image[32:64])
        y_ref[:, lanes] = y
        ys_ref[:, lanes] = s * y
        xy += x * y
        xx += x * x
    stack = jnp.concatenate([xy, xx, jnp.zeros((64, BLK), F32)], axis=0)
    sums_ref[...] = jnp.sum(stack.T, axis=0, keepdims=True)


def first_image(info, pattern, split, x, xs, across_odd, across_even, s):
    n = s.shape[0]
    return pl.pallas_call(
        first_kernel,
        in_specs=memory(pltpu.SMEM, pltpu.SMEM, pl.ANY, *[pltpu.VMEM] * 5),
        out_shape=[
            jax.ShapeDtypeStruct(x.shape, F32),
            jax.ShapeDtypeStruct(x.shape, F32),
            jax.ShapeDtypeStruct((1, BLK), F32),
        ],
        scratch_shapes=[
            pltpu.VMEM(split.shape, BF16),
            pltpu.VMEM((3 * n, BLK, BLK), BF16),
            pltpu.SemaphoreType.DMA((n,)),
        ],
        compiler_params=pltpu.CompilerParams(vmem_limit_bytes=VMEM_LIMIT),
        cost_estimate=pl.CostEstimate(flops=4 * 10**9, bytes_accessed=11 * 10**6, transcendentals=0),
        name="first_image",
    )(info, pattern, split, x, xs, across_odd, across_even, s)


def second_kernel(
    info, pat, a_hbm, ys_ref, ys_odd_ref, ys_even_ref, ps_ref, ps_odd_ref, ps_even_ref, s_ref, y_ref, p_ref,
    z_ref, image_ref, split_ref, turned, arrived,
):
    count = s_ref.shape[0]
    copies = loads(a_hbm, split_ref, arrived)
    turn_all(turned, info[3], ((ys_odd_ref, ps_odd_ref), (ys_ref, ps_ref), (ys_even_ref, ps_even_ref)), count)
    for i in range(count):
        lanes = slice(i * BLK, (i + 1) * BLK)
        wait_group(copies, i, GROUP)
        weights = gathered(info, pat, turned, i)
        product = jnp.dot(split_ref[i], weights, preferred_element_type=F32)
        image = (product[:BLK] + product[BLK:]).T
        s = s_ref[i : i + 1, :]
        z_ref[:, lanes] = y_ref[:, lanes] - s * (image[0:32] + image[32:64])
        image_ref[:, lanes] = p_ref[:, lanes] - s * (image[64:96] + image[96:128])


def second_image(info, pattern, split, ys, ys_odd, ys_even, ps, ps_odd, ps_even, s, y, p):
    n = s.shape[0]
    return pl.pallas_call(
        second_kernel,
        in_specs=memory(pltpu.SMEM, pltpu.SMEM, pl.ANY, *[pltpu.VMEM] * 9),
        out_shape=[jax.ShapeDtypeStruct(y.shape, F32)] * 2,
        scratch_shapes=[
            pltpu.VMEM(split.shape, BF16),
            pltpu.VMEM((3 * n, BLK, BLK), BF16),
            pltpu.SemaphoreType.DMA((n,)),
        ],
        compiler_params=pltpu.CompilerParams(vmem_limit_bytes=VMEM_LIMIT),
        cost_estimate=pl.CostEstimate(flops=4 * 10**9, bytes_accessed=14 * 10**6, transcendentals=0),
        name="second_image",
    )(info, pattern, split, ys, ys_odd, ys_even, ps, ps_odd, ps_even, s, y, p)


def products_kernel(
    info, sums_ref, x_ref, y_ref, p_ref, xo_ref, yo_ref, po_ref, z_ref, image_ref, high_ref, low_ref, out_ref, quotients, left_ref, acc
):
    core = info[0]
    own = pl.multiple_of(core * 32, 32)
    other = pl.multiple_of((1 - core) * 32, 32)
    sums = jnp.sum(sums_ref[...], axis=0, keepdims=True)
    column = jnp.broadcast_to(sums, (BLK, BLK)).T
    quotients[0:32] = column[0:32] / column[32:64]
    quotients[32:64] = column[64:96] / column[96:128]
    q_own = quotients[pl.ds(own, 32), :]
    q_other = quotients[pl.ds(other, 32), :]
    for i in range(x_ref.shape[1] // BLK):
        lanes = slice(i * BLK, (i + 1) * BLK)
        place = slice(i % CHUNK * BLK, (i % CHUNK + 1) * BLK)
        x, y = x_ref[:, lanes], y_ref[:, lanes]
        rows = (y - q_own * x, x, p_ref[:, lanes], z_ref[:, lanes] - q_own * y, y, image_ref[:, lanes])
        for at, v in enumerate(rows):
            high, low = halves(v)
            left_ref[32 * at : 32 * at + 32, place] = high
            left_ref[192 + 32 * at : 224 + 32 * at, place] = low
            if at < 3:
                high_ref[pl.ds(64 * at + own, 32), lanes] = high
                low_ref[pl.ds(64 * at + own, 32), lanes] = low
        xo = xo_ref[:, lanes]
        for at, v in enumerate((yo_ref[:, lanes] - q_other * xo, xo, po_ref[:, lanes])):
            high, low = halves(v)
            high_ref[pl.ds(64 * at + other, 32), lanes] = high
            low_ref[pl.ds(64 * at + other, 32), lanes] = low
        if i % CHUNK == CHUNK - 1:
            span = slice((i + 1 - CHUNK) * BLK, (i + 1) * BLK)
            dims = (((1,), (1,)), ((), ()))
            left = left_ref[...]
            part = lax.dot_general(left, high_ref[:, span], dims, preferred_element_type=F32)
            part = part + lax.dot_general(left, low_ref[:, span], dims, preferred_element_type=F32)
            acc[...] = part if i < CHUNK else acc[...] + part

    total = acc[0:192] + acc[192:384]
    out_ref[0:192, :] = total[:, 0:BLK]
    out_ref[192:384, :] = jnp.concatenate([total[:, BLK:192], jnp.zeros((192, 64), F32)], axis=1)


def products(info, sums, x, y, p, xo, yo, po, z, image):
    return pl.pallas_call(
        products_kernel,
        in_specs=memory(pltpu.SMEM, *[pltpu.VMEM] * 9),
        out_shape=[jax.ShapeDtypeStruct((192, x.shape[1]), BF16)] * 2 + [jax.ShapeDtypeStruct((384, BLK), F32)],
        scratch_shapes=[
            pltpu.VMEM((64, BLK), F32),
            pltpu.VMEM((384, CHUNK * BLK), BF16),
            pltpu.VMEM((384, 192), F32),
        ],
        compiler_params=pltpu.CompilerParams(vmem_limit_bytes=VMEM_LIMIT),
        cost_estimate=pl.CostEstimate(flops=2 * 10**9, bytes_accessed=6 * 10**6, transcendentals=0),
        name="products",
    )(info, sums, x, y, p, xo, yo, po, z, image)


def picked_row(groups, at):
    return jnp.broadcast_to(groups[at // 8][at % 8 : at % 8 + 1, :], (8, BLK))


def inverse_factor(block):
    lane = lax.broadcasted_iota(jnp.int32, (8, BLK), 1)
    sub = lax.broadcasted_iota(jnp.int32, (8, BLK), 0)
    tall = PIECE // 8
    a = []
    for g in range(tall):
        unit = jnp.where(lane - PIECE == sub + 8 * g, 1.0, 0.0)
        a.append(jnp.where(lane < PIECE, block[8 * g : 8 * g + 8, :], unit))
    for start in range(0, PIECE, PIVOTS):
        columns = [
            [jnp.broadcast_to(a[g][:, start + k : start + k + 1], (8, BLK)) if g >= start // 8 else None for g in range(tall)]
            for k in range(PIVOTS)
        ]
        for k in range(PIVOTS):
            at = start + k
            own = at // 8
            pivot = 1.0 / picked_row(columns[k], at)
            factor = [columns[k][g] * pivot if g >= own else None for g in range(tall)]
            factor[own] = jnp.where(sub > at % 8, factor[own], 0.0)
            for other in columns[k + 1 :]:
                e = picked_row(other, at)
                for g in range(own, tall):
                    other[g] = other[g] - factor[g] * e
            row = picked_row(a, at)
            for g in range(own, tall):
                a[g] = a[g] - factor[g] * row
    scaled = []
    for g in range(tall):
        diagonal = jnp.sum(jnp.where(lane == sub + 8 * g, a[g], 0.0), axis=1, keepdims=True)
        scaled.append(a[g] * lax.rsqrt(diagonal))
    return jnp.concatenate(scaled, axis=0)[:, PIECE : 2 * PIECE]


def exact(left, right, dims):
    return lax.dot_general(left, right, (dims, ((), ())), precision=EXACT, preferred_element_type=F32)


def inverse_cholesky(work, inverse):
    lane = lax.broadcasted_iota(jnp.int32, (PIECE, 192), 1)
    sub = lax.broadcasted_iota(jnp.int32, (PIECE, 192), 0)
    for at in range(0, 192, PIECE):
        rows = work[at : at + PIECE, :]
        if at < BLK:
            piece = rows[:, 0:BLK]
        else:
            piece = jnp.concatenate([rows[:, BLK:192], jnp.zeros((PIECE, 64), F32)], axis=1)
        if at % BLK:
            piece = pltpu.roll(piece, BLK - at % BLK, 1)
        small = inverse_factor(piece)
        unit = jnp.where(lane - at == sub, 1.0, 0.0)
        rows = jnp.where((lane >= at) & (lane < at + PIECE), unit, rows)
        new = exact(small, rows, ((1,), (0,)))
        inverse[at : at + PIECE, :] = jnp.where(lane < at + PIECE, new, 0.0)
        if at + PIECE < 192:
            update = exact(new, new, ((0,), (0,)))
            wide = lax.broadcasted_iota(jnp.int32, (192 - PIECE - at, 192), 1)
            old = jnp.where((wide >= at) & (wide < at + PIECE), 0.0, work[at + PIECE : 192, :])
            work[at + PIECE : 192, :] = old - update[at + PIECE : 192, :]


def final_kernel(
    both_ref, chosen_ref, high_hbm, low_hbm, vectors_ref, directions_ref, ritz_ref, high_ref, low_ref, work, raw, inverse, arrived, *, factor
):
    copies = [
        pltpu.make_async_copy(high_hbm, high_ref, arrived.at[0]),
        pltpu.make_async_copy(low_hbm, low_ref, arrived.at[1]),
    ]
    for copy in copies:
        copy.start()
    for at in range(6):
        for base, target in ((0, work), (96, raw)):
            row = 384 * (at % 2) + base + 32 * (at // 2)
            target[32 * at : 32 * at + 32, 0:BLK] = both_ref[row : row + 32, :]
            target[32 * at : 32 * at + 32, BLK:192] = both_ref[row + 192 : row + 224, 0:64]
    inverse_cholesky(work, inverse)
    whole_inverse = inverse[...]
    half = exact(whole_inverse, raw[...], ((1,), (1,)))
    ritz_ref[...] = exact(half, whole_inverse, ((1,), (1,)))
    mix = factor * exact(chosen_ref[...], whole_inverse, ((1,), (0,)))
    left = jnp.concatenate(halves(mix), axis=0)
    for copy in copies:
        copy.wait()
    for at in range(0, high_ref.shape[1], 512):
        lanes = slice(at, at + 512)
        product = jnp.dot(left, high_ref[:, lanes], preferred_element_type=F32)
        product = product + jnp.dot(left, low_ref[:, lanes], preferred_element_type=F32)
        product = product[0:64] + product[64:128]
        vectors_ref[:, lanes] = product[0:32]
        directions_ref[:, lanes] = product[32:64]


def final(both, chosen, high, low, factor):
    return pl.pallas_call(
        functools.partial(final_kernel, factor=factor),
        in_specs=memory(pltpu.VMEM, pltpu.VMEM, pl.ANY, pl.ANY),
        out_shape=[jax.ShapeDtypeStruct((32, high.shape[1]), F32)] * 2 + [jax.ShapeDtypeStruct((192, 192), F32)],
        scratch_shapes=[pltpu.VMEM(high.shape, BF16)] * 2 + [pltpu.VMEM((192, 192), F32)] * 3 + [pltpu.SemaphoreType.DMA((2,))],
        compiler_params=pltpu.CompilerParams(vmem_limit_bytes=VMEM_LIMIT),
        cost_estimate=pl.CostEstimate(flops=4 * 10**8, bytes_accessed=4 * 10**6, transcendentals=0),
        name="final",
    )(both, chosen, high, low)


def other_core(x):
    return lax.ppermute(x, "cols", [(0, 1), (1, 0)])


def local(vectors, directions, affinity, pattern, rotation):
    width, rows_dev = vectors.shape
    devices = lax.axis_size("rows")
    core = lax.axis_index("cols")
    total = 2 * width
    nodes = rows_dev * devices
    local_blocks = affinity.shape[0]
    all_blocks = local_blocks * devices
    place = lax.axis_index("rows")
    first_block = (place - 1) * local_blocks
    info = jnp.stack([core, first_block, jnp.int32(all_blocks), place % 2]).astype(jnp.int32)
    columns = pattern.T
    scale, xs = degrees(affinity, vectors)
    xs_odd, xs_even = from_neighbours(xs)
    split, ps = split_affinity(affinity, scale, directions)
    ps_odd, ps_even = from_neighbours(ps)
    x_other = other_core(vectors)
    p_other = other_core(directions)
    y, ys, sums = first_image(info, columns, split, vectors, xs, xs_odd, xs_even, scale)
    ys_odd, ys_even = from_neighbours(ys)
    y_other = other_core(y)
    half = sums[:, 0:64]
    blank = jnp.zeros_like(half)
    row = jnp.where(core == 0, jnp.concatenate([half, blank], axis=1), jnp.concatenate([blank, half], axis=1))
    sums = lax.all_to_all(repeated(row, 2 * devices), ("rows", "cols"), 0, 0).reshape(2 * devices, BLK)
    z, image = second_image(info, columns, split, ys, ys_odd, ys_even, ps, ps_odd, ps_even, scale, y, directions)
    high, low, part = products(info, sums, vectors, y, directions, x_other, y_other, p_other, z, image)
    both = sum_large(part.reshape(16, 24, BLK)).reshape(768, BLK)
    mine = lambda m: lax.dynamic_slice_in_dim(m, core * width, width, 1)
    kept = jnp.concatenate([rotation[:total], jnp.zeros((total, total), F32), rotation[2 * total :]], axis=0)
    chosen = jnp.concatenate([mine(rotation), mine(kept)], axis=1).T
    new_vectors, new_directions, ritz_matrix = final(both, chosen, high, low, math.sqrt(nodes))
    return new_vectors, new_directions, ritz_matrix


def solution(mesh):
    in_specs = (P("cols", "rows"), P("cols", "rows"), P("rows", None, None, None), P("rows", None), P())
    out_specs = (P("cols", "rows"), P("cols", "rows"), P())
    return jax.shard_map(local, mesh=mesh, in_specs=in_specs, out_specs=out_specs, check_vma=False)
```

```python
import functools
import math

import jax
import jax.numpy as jnp
from jax import lax
from jax.experimental import pallas as pl
from jax.experimental.pallas import tpu as pltpu
from jax.sharding import PartitionSpec as P

BLK = 128
F32 = jnp.float32
BF16 = jnp.bfloat16
UNROLL = 24
GROUP = 6
WIDE_GROUP = 12
PIECE = 64
CHUNK = 4
VMEM_LIMIT = 60 * 2**20
PIVOTS = 16
EXACT = lax.Precision.HIGHEST


def halves(v):
    high = v.astype(BF16)
    return high, (v - high.astype(F32)).astype(BF16)


def swaps(devices, first):
    return [pair for i in range(first, devices, 2) for pair in ((i, (i + 1) % devices), ((i + 1) % devices, i))]


def from_neighbours(x):
    devices = lax.axis_size("rows")
    return [lax.ppermute(x, "rows", swaps(devices, first)) for first in (1, 0)]


def row_of(z, x, y):
    return z * 16 + x * 4 + y


def plane_groups():
    return [[row_of(z, x, y) for x in range(4) for y in range(4)] for z in range(8)]


def column_groups():
    return [[row_of(z, x, y) for z in range(8)] for x in range(4) for y in range(4)]


def exchange(x, groups):
    return lax.all_to_all(x, "rows", 0, 0, axis_index_groups=groups)


def repeated(x, count):
    return jnp.broadcast_to(x[None], (count,) + x.shape)


def sum_large(x):
    part = jnp.sum(exchange(x, plane_groups()), axis=0)
    part = jnp.sum(exchange(repeated(part, 8), column_groups()), axis=0)
    return exchange(repeated(part, 16), plane_groups())


def loads(a_hbm, a_ref, arrived):
    copies = [pltpu.make_async_copy(a_hbm.at[i], a_ref.at[i], arrived.at[i]) for i in range(a_hbm.shape[0])]
    for copy in copies:
        copy.start()
    return copies


def wait_group(copies, i, group):
    if i % group == 0:
        for copy in copies[i : i + group]:
            copy.wait()


def memory(*spaces):
    return [pl.BlockSpec(memory_space=space) for space in spaces]


def degree_kernel(a_hbm, x_ref, scale_ref, xs_ref, a_ref, arrived):
    copies = loads(a_hbm, a_ref, arrived)
    for i in range(a_ref.shape[0]):
        wait_group(copies, i, GROUP)
        total = a_ref[i, 0]
        for k in range(1, 6):
            total = total + a_ref[i, k]
        scale = lax.rsqrt(jnp.sum(total.T, axis=0, keepdims=True))
        scale_ref[i : i + 1, :] = scale
        lanes = slice(i * BLK, (i + 1) * BLK)
        xs_ref[:, lanes] = x_ref[:, lanes] * scale


def degrees(affinity, x):
    n = affinity.shape[0]
    return pl.pallas_call(
        degree_kernel,
        in_specs=memory(pl.ANY, pltpu.VMEM),
        out_shape=[jax.ShapeDtypeStruct((n, BLK), F32), jax.ShapeDtypeStruct(x.shape, F32)],
        scratch_shapes=[pltpu.VMEM(affinity.shape, F32), pltpu.SemaphoreType.DMA((n,))],
        compiler_params=pltpu.CompilerParams(vmem_limit_bytes=VMEM_LIMIT),
        cost_estimate=pl.CostEstimate(flops=10**7, bytes_accessed=10**7, transcendentals=3072),
        name="degrees",
    )(affinity, x)


def split_kernel(a_hbm, scale_ref, p_ref, split_hbm, ps_ref, a_ref, split_ref, arrived, sent):
    count = a_ref.shape[0]
    copies = loads(a_hbm, a_ref, arrived)
    sends = [pltpu.make_async_copy(split_ref.at[i], split_hbm.at[i], sent.at[i]) for i in range(count)]
    for i in range(count):
        lanes = slice(i * BLK, (i + 1) * BLK)
        ps_ref[:, lanes] = p_ref[:, lanes] * scale_ref[i : i + 1, :]
    for i in range(count):
        wait_group(copies, i, WIDE_GROUP)
        for k in range(6):
            high, low = halves(a_ref[i, k])
            split_ref[i, 0:BLK, k * BLK : (k + 1) * BLK] = high
            split_ref[i, BLK : 2 * BLK, k * BLK : (k + 1) * BLK] = low
        if i % WIDE_GROUP == WIDE_GROUP - 1:
            for copy in sends[i + 1 - WIDE_GROUP : i + 1]:
                copy.start()
    for copy in sends:
        copy.wait()


def split_affinity(affinity, scale, p):
    n = affinity.shape[0]
    split = (n, 2 * BLK, 6 * BLK)
    return pl.pallas_call(
        split_kernel,
        in_specs=memory(pl.ANY, pltpu.VMEM, pltpu.VMEM),
        out_specs=memory(pl.ANY, pltpu.VMEM),
        out_shape=[jax.ShapeDtypeStruct(split, BF16), jax.ShapeDtypeStruct(p.shape, F32)],
        scratch_shapes=[
            pltpu.VMEM((n, 6, BLK, BLK), F32),
            pltpu.VMEM(split, BF16),
            pltpu.SemaphoreType.DMA((n,)),
            pltpu.SemaphoreType.DMA((n,)),
        ],
        compiler_params=pltpu.CompilerParams(vmem_limit_bytes=VMEM_LIMIT),
        cost_estimate=pl.CostEstimate(flops=10**7, bytes_accessed=19 * 10**6, transcendentals=0),
        name="split",
    )(affinity, scale, p)


def block_of(ref, i):
    return ref[:, pl.ds(pl.multiple_of(i * BLK, BLK), BLK)]


def local_place(index, first, total):
    place = index - first
    place = jnp.where(place < 0, place + total, place)
    return jnp.where(place >= total, place - total, place)


def gathered(info, pat, turned, i):
    places = [local_place(pat[k, i], info[1], info[2]) for k in range(6)]
    return jnp.concatenate([turned[place] for place in places], axis=0)


def turn_all(turned, odd, triples, count):
    for part, refs in zip((2 * odd, 1, 2 - 2 * odd), triples):

        @pl.loop(0, count, unroll=UNROLL)
        def _(j):
            stack = []
            for v_ref in refs:
                v = block_of(v_ref, j)
                high = v.astype(BF16).astype(F32)
                stack += [high, v - high]
            if len(refs) == 1:
                stack.append(jnp.zeros((64, BLK), F32))
            turned[part * count + j] = jnp.concatenate(stack, axis=0).T.astype(BF16)


def first_kernel(
    info, pat, a_hbm, x_ref, xs_ref, across_odd_ref, across_even_ref, s_ref, y_ref, ys_ref, sums_ref, split_ref, turned, arrived
):
    count = s_ref.shape[0]
    copies = loads(a_hbm, split_ref, arrived)
    turn_all(turned, info[3], ((across_odd_ref,), (xs_ref,), (across_even_ref,)), count)
    xy = jnp.zeros((32, BLK), F32)
    xx = jnp.zeros((32, BLK), F32)
    for i in range(count):
        lanes = slice(i * BLK, (i + 1) * BLK)
        wait_group(copies, i, GROUP)
        weights = gathered(info, pat, turned, i)
        product = jnp.dot(split_ref[i], weights, preferred_element_type=F32)
        image = (product[:BLK] + product[BLK:]).T
        x, s = x_ref[:, lanes], s_ref[i : i + 1, :]
        y = x - s * (image[0:32] + image[32:64])
        y_ref[:, lanes] = y
        ys_ref[:, lanes] = s * y
        xy += x * y
        xx += x * x
    core = info[0]
    pair = jnp.concatenate([xy, xx], axis=0)
    stack = jnp.concatenate([jnp.where(core == 0, pair, 0.0), jnp.where(core == 1, pair, 0.0)], axis=0)
    sums_ref[...] = jnp.broadcast_to(jnp.sum(stack.T, axis=0, keepdims=True), sums_ref.shape)


def first_image(info, pattern, split, x, xs, across_odd, across_even, s, copies):
    n = s.shape[0]
    return pl.pallas_call(
        first_kernel,
        in_specs=memory(pltpu.SMEM, pltpu.SMEM, pl.ANY, *[pltpu.VMEM] * 5),
        out_shape=[
            jax.ShapeDtypeStruct(x.shape, F32),
            jax.ShapeDtypeStruct(x.shape, F32),
            jax.ShapeDtypeStruct((copies, BLK), F32),
        ],
        scratch_shapes=[
            pltpu.VMEM(split.shape, BF16),
            pltpu.VMEM((3 * n, BLK, BLK), BF16),
            pltpu.SemaphoreType.DMA((n,)),
        ],
        compiler_params=pltpu.CompilerParams(vmem_limit_bytes=VMEM_LIMIT),
        cost_estimate=pl.CostEstimate(flops=4 * 10**9, bytes_accessed=11 * 10**6, transcendentals=0),
        name="first_image",
    )(info, pattern, split, x, xs, across_odd, across_even, s)


def second_kernel(
    info, pat, a_hbm, ys_ref, ys_odd_ref, ys_even_ref, ps_ref, ps_odd_ref, ps_even_ref, s_ref, y_ref, p_ref,
    z_ref, image_ref, split_ref, turned, arrived,
):
    count = s_ref.shape[0]
    copies = loads(a_hbm, split_ref, arrived)
    turn_all(turned, info[3], ((ys_odd_ref, ps_odd_ref), (ys_ref, ps_ref), (ys_even_ref, ps_even_ref)), count)
    for i in range(count):
        lanes = slice(i * BLK, (i + 1) * BLK)
        wait_group(copies, i, GROUP)
        weights = gathered(info, pat, turned, i)
        product = jnp.dot(split_ref[i], weights, preferred_element_type=F32)
        image = (product[:BLK] + product[BLK:]).T
        s = s_ref[i : i + 1, :]
        z_ref[:, lanes] = y_ref[:, lanes] - s * (image[0:32] + image[32:64])
        image_ref[:, lanes] = p_ref[:, lanes] - s * (image[64:96] + image[96:128])


def second_image(info, pattern, split, ys, ys_odd, ys_even, ps, ps_odd, ps_even, s, y, p):
    n = s.shape[0]
    return pl.pallas_call(
        second_kernel,
        in_specs=memory(pltpu.SMEM, pltpu.SMEM, pl.ANY, *[pltpu.VMEM] * 9),
        out_shape=[jax.ShapeDtypeStruct(y.shape, F32)] * 2,
        scratch_shapes=[
            pltpu.VMEM(split.shape, BF16),
            pltpu.VMEM((3 * n, BLK, BLK), BF16),
            pltpu.SemaphoreType.DMA((n,)),
        ],
        compiler_params=pltpu.CompilerParams(vmem_limit_bytes=VMEM_LIMIT),
        cost_estimate=pl.CostEstimate(flops=4 * 10**9, bytes_accessed=14 * 10**6, transcendentals=0),
        name="second_image",
    )(info, pattern, split, ys, ys_odd, ys_even, ps, ps_odd, ps_even, s, y, p)


def products_kernel(
    info, sums_ref, x_ref, y_ref, p_ref, xo_ref, yo_ref, po_ref, z_ref, image_ref, high_ref, low_ref, out_ref, quotients, left_ref, acc
):
    core = info[0]
    own = pl.multiple_of(core * 32, 32)
    other = pl.multiple_of((1 - core) * 32, 32)
    sums = jnp.sum(sums_ref[...], axis=0, keepdims=True)
    column = jnp.broadcast_to(sums, (BLK, BLK)).T
    quotients[0:32] = column[0:32] / column[32:64]
    quotients[32:64] = column[64:96] / column[96:128]
    q_own = quotients[pl.ds(own, 32), :]
    q_other = quotients[pl.ds(other, 32), :]
    for i in range(x_ref.shape[1] // BLK):
        lanes = slice(i * BLK, (i + 1) * BLK)
        place = slice(i % CHUNK * BLK, (i % CHUNK + 1) * BLK)
        x, y = x_ref[:, lanes], y_ref[:, lanes]
        rows = (y - q_own * x, x, p_ref[:, lanes], z_ref[:, lanes] - q_own * y, y, image_ref[:, lanes])
        for at, v in enumerate(rows):
            high, low = halves(v)
            left_ref[32 * at : 32 * at + 32, place] = high
            left_ref[192 + 32 * at : 224 + 32 * at, place] = low
            if at < 3:
                high_ref[pl.ds(64 * at + own, 32), lanes] = high
                low_ref[pl.ds(64 * at + own, 32), lanes] = low
        xo = xo_ref[:, lanes]
        for at, v in enumerate((yo_ref[:, lanes] - q_other * xo, xo, po_ref[:, lanes])):
            high, low = halves(v)
            high_ref[pl.ds(64 * at + other, 32), lanes] = high
            low_ref[pl.ds(64 * at + other, 32), lanes] = low
        if i % CHUNK == CHUNK - 1:
            span = slice((i + 1 - CHUNK) * BLK, (i + 1) * BLK)
            dims = (((1,), (1,)), ((), ()))
            left = left_ref[...]
            part = lax.dot_general(left, high_ref[:, span], dims, preferred_element_type=F32)
            part = part + lax.dot_general(left, low_ref[:, span], dims, preferred_element_type=F32)
            acc[...] = part if i < CHUNK else acc[...] + part

    total = acc[0:192] + acc[192:384]
    out_ref[0:192, :] = total[:, 0:BLK]
    out_ref[192:384, :] = jnp.concatenate([total[:, BLK:192], jnp.zeros((192, 64), F32)], axis=1)


def products(info, sums, x, y, p, xo, yo, po, z, image):
    return pl.pallas_call(
        products_kernel,
        in_specs=memory(pltpu.SMEM, *[pltpu.VMEM] * 9),
        out_shape=[jax.ShapeDtypeStruct((192, x.shape[1]), BF16)] * 2 + [jax.ShapeDtypeStruct((384, BLK), F32)],
        scratch_shapes=[
            pltpu.VMEM((64, BLK), F32),
            pltpu.VMEM((384, CHUNK * BLK), BF16),
            pltpu.VMEM((384, 192), F32),
        ],
        compiler_params=pltpu.CompilerParams(vmem_limit_bytes=VMEM_LIMIT),
        cost_estimate=pl.CostEstimate(flops=2 * 10**9, bytes_accessed=6 * 10**6, transcendentals=0),
        name="products",
    )(info, sums, x, y, p, xo, yo, po, z, image)


def picked_row(groups, at):
    return jnp.broadcast_to(groups[at // 8][at % 8 : at % 8 + 1, :], (8, BLK))


def inverse_factor(block):
    lane = lax.broadcasted_iota(jnp.int32, (8, BLK), 1)
    sub = lax.broadcasted_iota(jnp.int32, (8, BLK), 0)
    tall = PIECE // 8
    a = []
    for g in range(tall):
        unit = jnp.where(lane - PIECE == sub + 8 * g, 1.0, 0.0)
        a.append(jnp.where(lane < PIECE, block[8 * g : 8 * g + 8, :], unit))
    for start in range(0, PIECE, PIVOTS):
        columns = [
            [jnp.broadcast_to(a[g][:, start + k : start + k + 1], (8, BLK)) if g >= start // 8 else None for g in range(tall)]
            for k in range(PIVOTS)
        ]
        for k in range(PIVOTS):
            at = start + k
            own = at // 8
            pivot = 1.0 / picked_row(columns[k], at)
            factor = [columns[k][g] * pivot if g >= own else None for g in range(tall)]
            factor[own] = jnp.where(sub > at % 8, factor[own], 0.0)
            for other in columns[k + 1 :]:
                e = picked_row(other, at)
                for g in range(own, tall):
                    other[g] = other[g] - factor[g] * e
            row = picked_row(a, at)
            for g in range(own, tall):
                a[g] = a[g] - factor[g] * row
    scaled = []
    for g in range(tall):
        diagonal = jnp.sum(jnp.where(lane == sub + 8 * g, a[g], 0.0), axis=1, keepdims=True)
        scaled.append(a[g] * lax.rsqrt(diagonal))
    return jnp.concatenate(scaled, axis=0)[:, PIECE : 2 * PIECE]


def exact(left, right, dims):
    return lax.dot_general(left, right, (dims, ((), ())), precision=EXACT, preferred_element_type=F32)


def inverse_cholesky(work, inverse):
    lane = lax.broadcasted_iota(jnp.int32, (PIECE, 192), 1)
    sub = lax.broadcasted_iota(jnp.int32, (PIECE, 192), 0)
    for at in range(0, 192, PIECE):
        rows = work[at : at + PIECE, :]
        if at < BLK:
            piece = rows[:, 0:BLK]
        else:
            piece = jnp.concatenate([rows[:, BLK:192], jnp.zeros((PIECE, 64), F32)], axis=1)
        if at % BLK:
            piece = pltpu.roll(piece, BLK - at % BLK, 1)
        small = inverse_factor(piece)
        unit = jnp.where(lane - at == sub, 1.0, 0.0)
        rows = jnp.where((lane >= at) & (lane < at + PIECE), unit, rows)
        new = exact(small, rows, ((1,), (0,)))
        inverse[at : at + PIECE, :] = jnp.where(lane < at + PIECE, new, 0.0)
        if at + PIECE < 192:
            update = exact(new, new, ((0,), (0,)))
            wide = lax.broadcasted_iota(jnp.int32, (192 - PIECE - at, 192), 1)
            old = jnp.where((wide >= at) & (wide < at + PIECE), 0.0, work[at + PIECE : 192, :])
            work[at + PIECE : 192, :] = old - update[at + PIECE : 192, :]


def final_kernel(
    info, summed_ref, theirs_ref, chosen_ref, high_hbm, low_hbm, vectors_ref, directions_ref, ritz_ref,
    high_ref, low_ref, work, raw, inverse, arrived, *, factor
):
    copies = [
        pltpu.make_async_copy(high_hbm, high_ref, arrived.at[0]),
        pltpu.make_async_copy(low_hbm, low_ref, arrived.at[1]),
    ]
    for copy in copies:
        copy.start()
    first = info[0] == 0
    for at in range(6):
        mine = first if at % 2 == 0 else jnp.logical_not(first)
        for base, target in ((0, work), (96, raw)):
            row = base + 32 * (at // 2)
            head, tail = slice(row, row + 32), slice(row + 192, row + 224)
            target[32 * at : 32 * at + 32, 0:BLK] = jnp.where(mine, summed_ref[head, :], theirs_ref[head, :])
            target[32 * at : 32 * at + 32, BLK:192] = jnp.where(mine, summed_ref[tail, 0:64], theirs_ref[tail, 0:64])
    inverse_cholesky(work, inverse)
    whole_inverse = inverse[...]
    half = exact(whole_inverse, raw[...], ((1,), (1,)))
    ritz_ref[...] = exact(half, whole_inverse, ((1,), (1,)))
    mix = factor * exact(chosen_ref[...], whole_inverse, ((1,), (0,)))
    left = jnp.concatenate(halves(mix), axis=0)
    for copy in copies:
        copy.wait()
    for at in range(0, high_ref.shape[1], 512):
        lanes = slice(at, at + 512)
        product = jnp.dot(left, high_ref[:, lanes], preferred_element_type=F32)
        product = product + jnp.dot(left, low_ref[:, lanes], preferred_element_type=F32)
        product = product[0:64] + product[64:128]
        vectors_ref[:, lanes] = product[0:32]
        directions_ref[:, lanes] = product[32:64]


def final(info, summed, theirs, chosen, high, low, factor):
    return pl.pallas_call(
        functools.partial(final_kernel, factor=factor),
        in_specs=memory(pltpu.SMEM, pltpu.VMEM, pltpu.VMEM, pltpu.VMEM, pl.ANY, pl.ANY),
        out_shape=[jax.ShapeDtypeStruct((32, high.shape[1]), F32)] * 2 + [jax.ShapeDtypeStruct((192, 192), F32)],
        scratch_shapes=[pltpu.VMEM(high.shape, BF16)] * 2 + [pltpu.VMEM((192, 192), F32)] * 3 + [pltpu.SemaphoreType.DMA((2,))],
        compiler_params=pltpu.CompilerParams(vmem_limit_bytes=VMEM_LIMIT),
        cost_estimate=pl.CostEstimate(flops=4 * 10**8, bytes_accessed=4 * 10**6, transcendentals=0),
        name="final",
    )(info, summed, theirs, chosen, high, low)


def other_core(x):
    return lax.ppermute(x, "cols", [(0, 1), (1, 0)])


def local(vectors, directions, affinity, pattern, rotation):
    width, rows_dev = vectors.shape
    devices = lax.axis_size("rows")
    core = lax.axis_index("cols")
    total = 2 * width
    nodes = rows_dev * devices
    local_blocks = affinity.shape[0]
    all_blocks = local_blocks * devices
    place = lax.axis_index("rows")
    first_block = (place - 1) * local_blocks
    info = jnp.stack([core, first_block, jnp.int32(all_blocks), place % 2]).astype(jnp.int32)
    columns = pattern.T
    scale, xs = degrees(affinity, vectors)
    xs_odd, xs_even = from_neighbours(xs)
    split, ps = split_affinity(affinity, scale, directions)
    ps_odd, ps_even = from_neighbours(ps)
    x_other = other_core(vectors)
    p_other = other_core(directions)
    y, ys, sums = first_image(info, columns, split, vectors, xs, xs_odd, xs_even, scale, 2 * devices)
    ys_odd, ys_even = from_neighbours(ys)
    y_other = other_core(y)
    sums = lax.all_to_all(sums.reshape(2 * devices, 1, BLK), ("rows", "cols"), 0, 0).reshape(2 * devices, BLK)
    z, image = second_image(info, columns, split, ys, ys_odd, ys_even, ps, ps_odd, ps_even, scale, y, directions)
    high, low, part = products(info, sums, vectors, y, directions, x_other, y_other, p_other, z, image)
    summed = sum_large(part.reshape(16, 24, BLK)).reshape(384, BLK)
    theirs = other_core(summed)
    mine = lambda m: lax.dynamic_slice_in_dim(m, core * width, width, 1)
    kept = jnp.concatenate([rotation[:total], jnp.zeros((total, total), F32), rotation[2 * total :]], axis=0)
    chosen = jnp.concatenate([mine(rotation), mine(kept)], axis=1).T
    new_vectors, new_directions, ritz_matrix = final(info, summed, theirs, chosen, high, low, math.sqrt(nodes))
    return new_vectors, new_directions, ritz_matrix


def solution(mesh):
    in_specs = (P("cols", "rows"), P("cols", "rows"), P("rows", None, None, None), P("rows", None), P())
    out_specs = (P("cols", "rows"), P("cols", "rows"), P())
    return jax.shard_map(local, mesh=mesh, in_specs=in_specs, out_specs=out_specs, check_vma=False)
```

```python
import functools
import math

import jax
import jax.numpy as jnp
from jax import lax
from jax.experimental import pallas as pl
from jax.experimental.pallas import tpu as pltpu
from jax.sharding import PartitionSpec as P

BLK = 128
F32 = jnp.float32
BF16 = jnp.bfloat16
UNROLL = 24
GROUP = 6
WIDE_GROUP = 12
PIECE = 64
CHUNK = 4
VMEM_LIMIT = 60 * 2**20
PIVOTS = 16
EXACT = lax.Precision.HIGHEST


def halves(v):
    high = v.astype(BF16)
    return high, (v - high.astype(F32)).astype(BF16)


def swaps(devices, first):
    return [pair for i in range(first, devices, 2) for pair in ((i, (i + 1) % devices), ((i + 1) % devices, i))]


def from_neighbours(x):
    devices = lax.axis_size("rows")
    return [lax.ppermute(x, "rows", swaps(devices, first)) for first in (1, 0)]


def row_of(z, x, y):
    return z * 16 + x * 4 + y


def plane_groups():
    return [[row_of(z, x, y) for x in range(4) for y in range(4)] for z in range(8)]


def column_groups():
    return [[row_of(z, x, y) for z in range(8)] for x in range(4) for y in range(4)]


def exchange(x, groups):
    return lax.all_to_all(x, "rows", 0, 0, axis_index_groups=groups)


def repeated(x, count):
    return jnp.broadcast_to(x[None], (count,) + x.shape)


def sum_large(x):
    part = jnp.sum(exchange(x, plane_groups()), axis=0)
    part = jnp.sum(exchange(repeated(part, 8), column_groups()), axis=0)
    return exchange(repeated(part, 16), plane_groups())


def loads(a_hbm, a_ref, arrived):
    copies = [pltpu.make_async_copy(a_hbm.at[i], a_ref.at[i], arrived.at[i]) for i in range(a_hbm.shape[0])]
    for copy in copies:
        copy.start()
    return copies


def wait_group(copies, i, group):
    if i % group == 0:
        for copy in copies[i : i + group]:
            copy.wait()


def memory(*spaces):
    return [pl.BlockSpec(memory_space=space) for space in spaces]


def degree_kernel(a_hbm, x_ref, scale_ref, xs_ref, a_ref, arrived):
    copies = loads(a_hbm, a_ref, arrived)
    for i in range(a_ref.shape[0]):
        wait_group(copies, i, GROUP)
        total = a_ref[i, 0]
        for k in range(1, 6):
            total = total + a_ref[i, k]
        scale = lax.rsqrt(jnp.sum(total.T, axis=0, keepdims=True))
        scale_ref[i : i + 1, :] = scale
        lanes = slice(i * BLK, (i + 1) * BLK)
        xs_ref[:, lanes] = x_ref[:, lanes] * scale


def degrees(affinity, x):
    n = affinity.shape[0]
    return pl.pallas_call(
        degree_kernel,
        in_specs=memory(pl.ANY, pltpu.VMEM),
        out_shape=[jax.ShapeDtypeStruct((n, BLK), F32), jax.ShapeDtypeStruct(x.shape, F32)],
        scratch_shapes=[pltpu.VMEM(affinity.shape, F32), pltpu.SemaphoreType.DMA((n,))],
        compiler_params=pltpu.CompilerParams(vmem_limit_bytes=60 * 2**20),
        cost_estimate=pl.CostEstimate(flops=10**7, bytes_accessed=10**7, transcendentals=3072),
        name="degrees",
    )(affinity, x)


def split_kernel(a_hbm, scale_ref, p_ref, split_hbm, ps_ref, a_ref, split_ref, arrived, sent):
    count = a_ref.shape[0]
    copies = loads(a_hbm, a_ref, arrived)
    sends = [pltpu.make_async_copy(split_ref.at[i], split_hbm.at[i], sent.at[i]) for i in range(count)]
    for i in range(count):
        lanes = slice(i * BLK, (i + 1) * BLK)
        ps_ref[:, lanes] = p_ref[:, lanes] * scale_ref[i : i + 1, :]
    for i in range(count):
        wait_group(copies, i, WIDE_GROUP)
        for k in range(6):
            high, low = halves(a_ref[i, k])
            split_ref[i, 0:BLK, k * BLK : (k + 1) * BLK] = high
            split_ref[i, BLK : 2 * BLK, k * BLK : (k + 1) * BLK] = low
        if i % WIDE_GROUP == WIDE_GROUP - 1:
            for copy in sends[i + 1 - WIDE_GROUP : i + 1]:
                copy.start()
    for copy in sends:
        copy.wait()


def split_affinity(affinity, scale, p):
    n = affinity.shape[0]
    split = (n, 2 * BLK, 6 * BLK)
    return pl.pallas_call(
        split_kernel,
        in_specs=memory(pl.ANY, pltpu.VMEM, pltpu.VMEM),
        out_specs=memory(pl.ANY, pltpu.VMEM),
        out_shape=[jax.ShapeDtypeStruct(split, BF16), jax.ShapeDtypeStruct(p.shape, F32)],
        scratch_shapes=[
            pltpu.VMEM((n, 6, BLK, BLK), F32),
            pltpu.VMEM(split, BF16),
            pltpu.SemaphoreType.DMA((n,)),
            pltpu.SemaphoreType.DMA((n,)),
        ],
        compiler_params=pltpu.CompilerParams(vmem_limit_bytes=60 * 2**20),
        cost_estimate=pl.CostEstimate(flops=10**7, bytes_accessed=19 * 10**6, transcendentals=0),
        name="split",
    )(affinity, scale, p)


def block_of(ref, i):
    return ref[:, pl.ds(pl.multiple_of(i * BLK, BLK), BLK)]


def local_place(index, first, total):
    place = index - first
    place = jnp.where(place < 0, place + total, place)
    return jnp.where(place >= total, place - total, place)


def gathered(info, pat, turned, i):
    places = [local_place(pat[k, i], info[1], info[2]) for k in range(6)]
    return jnp.concatenate([turned[place] for place in places], axis=0)


def turn_all(turned, odd, triples, count):
    for part, refs in zip((2 * odd, 1, 2 - 2 * odd), triples):

        @pl.loop(0, count, unroll=UNROLL)
        def _(j):
            stack = []
            for v_ref in refs:
                v = block_of(v_ref, j)
                high = v.astype(BF16).astype(F32)
                stack += [high, v - high]
            if len(refs) == 1:
                stack.append(jnp.zeros((64, BLK), F32))
            turned[part * count + j] = jnp.concatenate(stack, axis=0).T.astype(BF16)


def first_kernel(
    info, pat, a_hbm, x_ref, xs_ref, across_odd_ref, across_even_ref, s_ref, y_ref, ys_ref, sums_ref, split_ref, turned, arrived
):
    count = s_ref.shape[0]
    copies = loads(a_hbm, split_ref, arrived)
    turn_all(turned, info[3], ((across_odd_ref,), (xs_ref,), (across_even_ref,)), count)
    xy = jnp.zeros((32, BLK), F32)
    xx = jnp.zeros((32, BLK), F32)
    for i in range(count):
        lanes = slice(i * BLK, (i + 1) * BLK)
        wait_group(copies, i, GROUP)
        weights = gathered(info, pat, turned, i)
        product = jnp.dot(split_ref[i], weights, preferred_element_type=F32)
        image = (product[:BLK] + product[BLK:]).T
        x, s = x_ref[:, lanes], s_ref[i : i + 1, :]
        y = x - s * (image[0:32] + image[32:64])
        y_ref[:, lanes] = y
        ys_ref[:, lanes] = s * y
        xy += x * y
        xx += x * x
    core = info[0]
    pair = jnp.concatenate([xy, xx], axis=0)
    stack = jnp.concatenate([jnp.where(core == 0, pair, 0.0), jnp.where(core == 1, pair, 0.0)], axis=0)
    sums_ref[...] = jnp.broadcast_to(jnp.sum(stack.T, axis=0, keepdims=True), sums_ref.shape)


def first_image(info, pattern, split, x, xs, across_odd, across_even, s, copies):
    n = s.shape[0]
    return pl.pallas_call(
        first_kernel,
        in_specs=memory(pltpu.SMEM, pltpu.SMEM, pl.ANY, *[pltpu.VMEM] * 5),
        out_shape=[
            jax.ShapeDtypeStruct(x.shape, F32),
            jax.ShapeDtypeStruct(x.shape, F32),
            jax.ShapeDtypeStruct((copies, BLK), F32),
        ],
        scratch_shapes=[
            pltpu.VMEM(split.shape, BF16),
            pltpu.VMEM((3 * n, BLK, BLK), BF16),
            pltpu.SemaphoreType.DMA((n,)),
        ],
        compiler_params=pltpu.CompilerParams(vmem_limit_bytes=52 * 2**20),
        cost_estimate=pl.CostEstimate(flops=4 * 10**9, bytes_accessed=11 * 10**6, transcendentals=0),
        name="first_image",
    )(info, pattern, split, x, xs, across_odd, across_even, s)


def second_kernel(
    info, pat, a_hbm, ys_ref, ys_odd_ref, ys_even_ref, ps_ref, ps_odd_ref, ps_even_ref, s_ref, y_ref, p_ref,
    z_ref, image_ref, split_ref, turned, arrived,
):
    count = s_ref.shape[0]
    copies = loads(a_hbm, split_ref, arrived)
    turn_all(turned, info[3], ((ys_odd_ref, ps_odd_ref), (ys_ref, ps_ref), (ys_even_ref, ps_even_ref)), count)
    for i in range(count):
        lanes = slice(i * BLK, (i + 1) * BLK)
        wait_group(copies, i, GROUP)
        weights = gathered(info, pat, turned, i)
        product = jnp.dot(split_ref[i], weights, preferred_element_type=F32)
        image = (product[:BLK] + product[BLK:]).T
        s = s_ref[i : i + 1, :]
        z_ref[:, lanes] = y_ref[:, lanes] - s * (image[0:32] + image[32:64])
        image_ref[:, lanes] = p_ref[:, lanes] - s * (image[64:96] + image[96:128])


def second_image(info, pattern, split, ys, ys_odd, ys_even, ps, ps_odd, ps_even, s, y, p):
    n = s.shape[0]
    return pl.pallas_call(
        second_kernel,
        in_specs=memory(pltpu.SMEM, pltpu.SMEM, pl.ANY, *[pltpu.VMEM] * 9),
        out_shape=[jax.ShapeDtypeStruct(y.shape, F32)] * 2,
        scratch_shapes=[
            pltpu.VMEM(split.shape, BF16),
            pltpu.VMEM((3 * n, BLK, BLK), BF16),
            pltpu.SemaphoreType.DMA((n,)),
        ],
        compiler_params=pltpu.CompilerParams(vmem_limit_bytes=52 * 2**20),
        cost_estimate=pl.CostEstimate(flops=4 * 10**9, bytes_accessed=14 * 10**6, transcendentals=0),
        name="second_image",
    )(info, pattern, split, ys, ys_odd, ys_even, ps, ps_odd, ps_even, s, y, p)


def products_kernel(
    info, sums_ref, x_ref, y_ref, p_ref, xo_ref, yo_ref, po_ref, z_ref, image_ref, high_ref, low_ref, out_ref, quotients, left_ref, acc
):
    core = info[0]
    own = pl.multiple_of(core * 32, 32)
    other = pl.multiple_of((1 - core) * 32, 32)
    sums = jnp.sum(sums_ref[...], axis=0, keepdims=True)
    column = jnp.broadcast_to(sums, (BLK, BLK)).T
    quotients[0:32] = column[0:32] / column[32:64]
    quotients[32:64] = column[64:96] / column[96:128]
    q_own = quotients[pl.ds(own, 32), :]
    q_other = quotients[pl.ds(other, 32), :]
    for i in range(x_ref.shape[1] // BLK):
        lanes = slice(i * BLK, (i + 1) * BLK)
        place = slice(i % CHUNK * BLK, (i % CHUNK + 1) * BLK)
        x, y = x_ref[:, lanes], y_ref[:, lanes]
        rows = (y - q_own * x, x, p_ref[:, lanes], z_ref[:, lanes] - q_own * y, y, image_ref[:, lanes])
        for at, v in enumerate(rows):
            high, low = halves(v)
            left_ref[32 * at : 32 * at + 32, place] = high
            left_ref[192 + 32 * at : 224 + 32 * at, place] = low
            if at < 3:
                high_ref[pl.ds(64 * at + own, 32), lanes] = high
                low_ref[pl.ds(64 * at + own, 32), lanes] = low
        xo = xo_ref[:, lanes]
        for at, v in enumerate((yo_ref[:, lanes] - q_other * xo, xo, po_ref[:, lanes])):
            high, low = halves(v)
            high_ref[pl.ds(64 * at + other, 32), lanes] = high
            low_ref[pl.ds(64 * at + other, 32), lanes] = low
        if i % CHUNK == CHUNK - 1:
            span = slice((i + 1 - CHUNK) * BLK, (i + 1) * BLK)
            dims = (((1,), (1,)), ((), ()))
            left = left_ref[...]
            part = lax.dot_general(left, high_ref[:, span], dims, preferred_element_type=F32)
            part = part + lax.dot_general(left, low_ref[:, span], dims, preferred_element_type=F32)
            acc[...] = part if i < CHUNK else acc[...] + part

    total = acc[0:192] + acc[192:384]
    out_ref[0:192, :] = total[:, 0:BLK]
    out_ref[192:384, :] = jnp.concatenate([total[:, BLK:192], jnp.zeros((192, 64), F32)], axis=1)


def products(info, sums, x, y, p, xo, yo, po, z, image):
    return pl.pallas_call(
        products_kernel,
        in_specs=memory(pltpu.SMEM, *[pltpu.VMEM] * 9),
        out_shape=[jax.ShapeDtypeStruct((192, x.shape[1]), BF16)] * 2 + [jax.ShapeDtypeStruct((384, BLK), F32)],
        scratch_shapes=[
            pltpu.VMEM((64, BLK), F32),
            pltpu.VMEM((384, CHUNK * BLK), BF16),
            pltpu.VMEM((384, 192), F32),
        ],
        compiler_params=pltpu.CompilerParams(vmem_limit_bytes=24 * 2**20),
        cost_estimate=pl.CostEstimate(flops=2 * 10**9, bytes_accessed=6 * 10**6, transcendentals=0),
        name="products",
    )(info, sums, x, y, p, xo, yo, po, z, image)


def picked_row(groups, at):
    return jnp.broadcast_to(groups[at // 8][at % 8 : at % 8 + 1, :], (8, BLK))


def inverse_factor(block):
    lane = lax.broadcasted_iota(jnp.int32, (8, BLK), 1)
    sub = lax.broadcasted_iota(jnp.int32, (8, BLK), 0)
    tall = PIECE // 8
    a = []
    for g in range(tall):
        unit = jnp.where(lane - PIECE == sub + 8 * g, 1.0, 0.0)
        a.append(jnp.where(lane < PIECE, block[8 * g : 8 * g + 8, :], unit))
    for start in range(0, PIECE, PIVOTS):
        columns = [
            [jnp.broadcast_to(a[g][:, start + k : start + k + 1], (8, BLK)) if g >= start // 8 else None for g in range(tall)]
            for k in range(PIVOTS)
        ]
        for k in range(PIVOTS):
            at = start + k
            own = at // 8
            pivot = 1.0 / picked_row(columns[k], at)
            factor = [columns[k][g] * pivot if g >= own else None for g in range(tall)]
            factor[own] = jnp.where(sub > at % 8, factor[own], 0.0)
            for other in columns[k + 1 :]:
                e = picked_row(other, at)
                for g in range(own, tall):
                    other[g] = other[g] - factor[g] * e
            row = picked_row(a, at)
            for g in range(own, tall):
                a[g] = a[g] - factor[g] * row
    scaled = []
    for g in range(tall):
        diagonal = jnp.sum(jnp.where(lane == sub + 8 * g, a[g], 0.0), axis=1, keepdims=True)
        scaled.append(a[g] * lax.rsqrt(diagonal))
    return jnp.concatenate(scaled, axis=0)[:, PIECE : 2 * PIECE]


def exact(left, right, dims):
    return lax.dot_general(left, right, (dims, ((), ())), precision=EXACT, preferred_element_type=F32)


def inverse_cholesky(work, inverse):
    lane = lax.broadcasted_iota(jnp.int32, (PIECE, 192), 1)
    sub = lax.broadcasted_iota(jnp.int32, (PIECE, 192), 0)
    for at in range(0, 192, PIECE):
        rows = work[at : at + PIECE, :]
        if at < BLK:
            piece = rows[:, 0:BLK]
        else:
            piece = jnp.concatenate([rows[:, BLK:192], jnp.zeros((PIECE, 64), F32)], axis=1)
        if at % BLK:
            piece = pltpu.roll(piece, BLK - at % BLK, 1)
        small = inverse_factor(piece)
        unit = jnp.where(lane - at == sub, 1.0, 0.0)
        rows = jnp.where((lane >= at) & (lane < at + PIECE), unit, rows)
        new = exact(small, rows, ((1,), (0,)))
        inverse[at : at + PIECE, :] = jnp.where(lane < at + PIECE, new, 0.0)
        if at + PIECE < 192:
            update = exact(new, new, ((0,), (0,)))
            wide = lax.broadcasted_iota(jnp.int32, (192 - PIECE - at, 192), 1)
            old = jnp.where((wide >= at) & (wide < at + PIECE), 0.0, work[at + PIECE : 192, :])
            work[at + PIECE : 192, :] = old - update[at + PIECE : 192, :]


def final_kernel(
    info, summed_ref, theirs_ref, chosen_ref, high_hbm, low_hbm, vectors_ref, directions_ref, ritz_ref,
    high_ref, low_ref, work, raw, inverse, arrived, *, factor
):
    copies = [
        pltpu.make_async_copy(high_hbm, high_ref, arrived.at[0]),
        pltpu.make_async_copy(low_hbm, low_ref, arrived.at[1]),
    ]
    for copy in copies:
        copy.start()
    first = info[0] == 0
    for at in range(6):
        mine = first if at % 2 == 0 else jnp.logical_not(first)
        for base, target in ((0, work), (96, raw)):
            row = base + 32 * (at // 2)
            head, tail = slice(row, row + 32), slice(row + 192, row + 224)
            target[32 * at : 32 * at + 32, 0:BLK] = jnp.where(mine, summed_ref[head, :], theirs_ref[head, :])
            target[32 * at : 32 * at + 32, BLK:192] = jnp.where(mine, summed_ref[tail, 0:64], theirs_ref[tail, 0:64])
    inverse_cholesky(work, inverse)
    whole_inverse = inverse[...]
    half = exact(whole_inverse, raw[...], ((1,), (1,)))
    ritz_ref[...] = exact(half, whole_inverse, ((1,), (1,)))
    mix = factor * exact(chosen_ref[...], whole_inverse, ((1,), (0,)))
    left = jnp.concatenate(halves(mix), axis=0)
    for copy in copies:
        copy.wait()
    for at in range(0, high_ref.shape[1], 512):
        lanes = slice(at, at + 512)
        product = jnp.dot(left, high_ref[:, lanes], preferred_element_type=F32)
        product = product + jnp.dot(left, low_ref[:, lanes], preferred_element_type=F32)
        product = product[0:64] + product[64:128]
        vectors_ref[:, lanes] = product[0:32]
        directions_ref[:, lanes] = product[32:64]


def final(info, summed, theirs, chosen, high, low, factor):
    return pl.pallas_call(
        functools.partial(final_kernel, factor=factor),
        in_specs=memory(pltpu.SMEM, pltpu.VMEM, pltpu.VMEM, pltpu.VMEM, pl.ANY, pl.ANY),
        out_shape=[jax.ShapeDtypeStruct((32, high.shape[1]), F32)] * 2 + [jax.ShapeDtypeStruct((192, 192), F32)],
        scratch_shapes=[pltpu.VMEM(high.shape, BF16)] * 2 + [pltpu.VMEM((192, 192), F32)] * 3 + [pltpu.SemaphoreType.DMA((2,))],
        compiler_params=pltpu.CompilerParams(vmem_limit_bytes=24 * 2**20),
        cost_estimate=pl.CostEstimate(flops=4 * 10**8, bytes_accessed=4 * 10**6, transcendentals=0),
        name="final",
    )(info, summed, theirs, chosen, high, low)


def other_core(x):
    return lax.ppermute(x, "cols", [(0, 1), (1, 0)])


def local(vectors, directions, affinity, pattern, rotation):
    width, rows_dev = vectors.shape
    devices = lax.axis_size("rows")
    core = lax.axis_index("cols")
    total = 2 * width
    nodes = rows_dev * devices
    local_blocks = affinity.shape[0]
    all_blocks = local_blocks * devices
    place = lax.axis_index("rows")
    first_block = (place - 1) * local_blocks
    info = jnp.stack([core, first_block, jnp.int32(all_blocks), place % 2]).astype(jnp.int32)
    columns = pattern.T
    scale, xs = degrees(affinity, vectors)
    xs_odd, xs_even = from_neighbours(xs)
    split, ps = split_affinity(affinity, scale, directions)
    ps_odd, ps_even = from_neighbours(ps)
    x_other = other_core(vectors)
    p_other = other_core(directions)
    y, ys, sums = first_image(info, columns, split, vectors, xs, xs_odd, xs_even, scale, 2 * devices)
    ys_odd, ys_even = from_neighbours(ys)
    y_other = other_core(y)
    sums = lax.all_to_all(sums.reshape(2 * devices, 1, BLK), ("rows", "cols"), 0, 0).reshape(2 * devices, BLK)
    z, image = second_image(info, columns, split, ys, ys_odd, ys_even, ps, ps_odd, ps_even, scale, y, directions)
    high, low, part = products(info, sums, vectors, y, directions, x_other, y_other, p_other, z, image)
    summed = sum_large(part.reshape(16, 24, BLK)).reshape(384, BLK)
    theirs = other_core(summed)
    mine = lambda m: lax.dynamic_slice_in_dim(m, core * width, width, 1)
    kept = jnp.concatenate([rotation[:total], jnp.zeros((total, total), F32), rotation[2 * total :]], axis=0)
    chosen = jnp.concatenate([mine(rotation), mine(kept)], axis=1).T
    new_vectors, new_directions, ritz_matrix = final(info, summed, theirs, chosen, high, low, math.sqrt(nodes))
    return new_vectors, new_directions, ritz_matrix


def solution(mesh):
    in_specs = (P("cols", "rows"), P("cols", "rows"), P("rows", None, None, None), P("rows", None), P())
    out_specs = (P("cols", "rows"), P("cols", "rows"), P())
    return jax.shard_map(local, mesh=mesh, in_specs=in_specs, out_specs=out_specs, check_vma=False)
```

```python
import functools
import math

import jax
import jax.numpy as jnp
from jax import lax
from jax.experimental import pallas as pl
from jax.experimental.pallas import tpu as pltpu
from jax.sharding import PartitionSpec as P

BLK = 128
F32 = jnp.float32
BF16 = jnp.bfloat16
UNROLL = 24
GROUP = 6
WIDE_GROUP = 12
PIECE = 64
CHUNK = 4
VMEM_LIMIT = 60 * 2**20
PIVOTS = 16
EXACT = lax.Precision.HIGHEST


def halves(v):
    high = v.astype(BF16)
    return high, (v - high.astype(F32)).astype(BF16)


def swaps(devices, first):
    return [pair for i in range(first, devices, 2) for pair in ((i, (i + 1) % devices), ((i + 1) % devices, i))]


def from_neighbours(x):
    devices = lax.axis_size("rows")
    return [lax.ppermute(x, "rows", swaps(devices, first)) for first in (1, 0)]


def row_of(z, x, y):
    return z * 16 + x * 4 + y


def plane_groups():
    return [[row_of(z, x, y) for x in range(4) for y in range(4)] for z in range(8)]


def column_groups():
    return [[row_of(z, x, y) for z in range(8)] for x in range(4) for y in range(4)]


def exchange(x, groups):
    return lax.all_to_all(x, "rows", 0, 0, axis_index_groups=groups)


def repeated(x, count):
    return jnp.broadcast_to(x[None], (count,) + x.shape)


def sum_large(x):
    part = jnp.sum(exchange(x, plane_groups()), axis=0)
    part = jnp.sum(exchange(repeated(part, 8), column_groups()), axis=0)
    return exchange(repeated(part, 16), plane_groups())


def loads(a_hbm, a_ref, arrived):
    copies = [pltpu.make_async_copy(a_hbm.at[i], a_ref.at[i], arrived.at[i]) for i in range(a_hbm.shape[0])]
    for copy in copies:
        copy.start()
    return copies


def wait_group(copies, i, group):
    if i % group == 0:
        for copy in copies[i : i + group]:
            copy.wait()


def memory(*spaces):
    return [pl.BlockSpec(memory_space=space) for space in spaces]


def degree_kernel(a_hbm, x_ref, scale_ref, xs_ref, a_ref, arrived):
    copies = loads(a_hbm, a_ref, arrived)
    for i in range(a_ref.shape[0]):
        wait_group(copies, i, GROUP)
        total = a_ref[i, 0]
        for k in range(1, 6):
            total = total + a_ref[i, k]
        scale = lax.rsqrt(jnp.sum(total.T, axis=0, keepdims=True))
        scale_ref[i : i + 1, :] = scale
        lanes = slice(i * BLK, (i + 1) * BLK)
        xs_ref[:, lanes] = x_ref[:, lanes] * scale


def degrees(affinity, x):
    n = affinity.shape[0]
    return pl.pallas_call(
        degree_kernel,
        in_specs=memory(pl.ANY, pltpu.VMEM),
        out_shape=[jax.ShapeDtypeStruct((n, BLK), F32), jax.ShapeDtypeStruct(x.shape, F32)],
        scratch_shapes=[pltpu.VMEM(affinity.shape, F32), pltpu.SemaphoreType.DMA((n,))],
        compiler_params=pltpu.CompilerParams(vmem_limit_bytes=60 * 2**20),
        cost_estimate=pl.CostEstimate(flops=10**7, bytes_accessed=10**7, transcendentals=3072),
        name="degrees",
    )(affinity, x)


def split_kernel(a_hbm, scale_ref, p_ref, split_hbm, ps_ref, a_ref, split_ref, arrived, sent):
    count = a_ref.shape[0]
    copies = loads(a_hbm, a_ref, arrived)
    sends = [pltpu.make_async_copy(split_ref.at[i], split_hbm.at[i], sent.at[i]) for i in range(count)]
    for i in range(count):
        lanes = slice(i * BLK, (i + 1) * BLK)
        ps_ref[:, lanes] = p_ref[:, lanes] * scale_ref[i : i + 1, :]
    for i in range(count):
        wait_group(copies, i, WIDE_GROUP)
        for k in range(6):
            high, low = halves(a_ref[i, k])
            split_ref[i, 0:BLK, k * BLK : (k + 1) * BLK] = high
            split_ref[i, BLK : 2 * BLK, k * BLK : (k + 1) * BLK] = low
        if i % WIDE_GROUP == WIDE_GROUP - 1:
            for copy in sends[i + 1 - WIDE_GROUP : i + 1]:
                copy.start()
    for copy in sends:
        copy.wait()


def split_affinity(affinity, scale, p):
    n = affinity.shape[0]
    split = (n, 2 * BLK, 6 * BLK)
    return pl.pallas_call(
        split_kernel,
        in_specs=memory(pl.ANY, pltpu.VMEM, pltpu.VMEM),
        out_specs=memory(pl.ANY, pltpu.VMEM),
        out_shape=[jax.ShapeDtypeStruct(split, BF16), jax.ShapeDtypeStruct(p.shape, F32)],
        scratch_shapes=[
            pltpu.VMEM((n, 6, BLK, BLK), F32),
            pltpu.VMEM(split, BF16),
            pltpu.SemaphoreType.DMA((n,)),
            pltpu.SemaphoreType.DMA((n,)),
        ],
        compiler_params=pltpu.CompilerParams(vmem_limit_bytes=60 * 2**20),
        cost_estimate=pl.CostEstimate(flops=10**7, bytes_accessed=19 * 10**6, transcendentals=0),
        name="split",
    )(affinity, scale, p)


def block_of(ref, i):
    return ref[:, pl.ds(pl.multiple_of(i * BLK, BLK), BLK)]


def local_place(index, first, total):
    place = index - first
    place = jnp.where(place < 0, place + total, place)
    return jnp.where(place >= total, place - total, place)


def gathered(info, pat, turned, i):
    places = [local_place(pat[k, i], info[1], info[2]) for k in range(6)]
    return jnp.concatenate([turned[place] for place in places], axis=0)


def turn_all(turned, odd, triples, count):
    for part, refs in zip((2 * odd, 1, 2 - 2 * odd), triples):

        @pl.loop(0, count, unroll=UNROLL)
        def _(j):
            stack = []
            for v_ref in refs:
                v = block_of(v_ref, j)
                high = v.astype(BF16).astype(F32)
                stack += [high, v - high]
            if len(refs) == 1:
                stack.append(jnp.zeros((64, BLK), F32))
            turned[part * count + j] = jnp.concatenate(stack, axis=0).T.astype(BF16)


def first_kernel(
    info, pat, a_hbm, x_ref, xs_ref, across_odd_ref, across_even_ref, s_ref, y_ref, ys_ref, sums_ref, split_ref, turned, arrived
):
    count = s_ref.shape[0]
    copies = loads(a_hbm, split_ref, arrived)
    turn_all(turned, info[3], ((across_odd_ref,), (xs_ref,), (across_even_ref,)), count)
    xy = jnp.zeros((32, BLK), F32)
    xx = jnp.zeros((32, BLK), F32)
    for i in range(count):
        lanes = slice(i * BLK, (i + 1) * BLK)
        wait_group(copies, i, GROUP)
        weights = gathered(info, pat, turned, i)
        product = jnp.dot(split_ref[i], weights, preferred_element_type=F32)
        image = (product[:BLK] + product[BLK:]).T
        x, s = x_ref[:, lanes], s_ref[i : i + 1, :]
        y = x - s * (image[0:32] + image[32:64])
        y_ref[:, lanes] = y
        ys_ref[:, lanes] = s * y
        xy += x * y
        xx += x * x
    core = info[0]
    pair = jnp.concatenate([xy, xx], axis=0)
    stack = jnp.concatenate([jnp.where(core == 0, pair, 0.0), jnp.where(core == 1, pair, 0.0)], axis=0)
    sums_ref[...] = jnp.broadcast_to(jnp.sum(stack.T, axis=0, keepdims=True), sums_ref.shape)


def first_image(info, pattern, split, x, xs, across_odd, across_even, s, copies):
    n = s.shape[0]
    return pl.pallas_call(
        first_kernel,
        in_specs=memory(pltpu.SMEM, pltpu.SMEM, pl.ANY, *[pltpu.VMEM] * 5),
        out_shape=[
            jax.ShapeDtypeStruct(x.shape, F32),
            jax.ShapeDtypeStruct(x.shape, F32),
            jax.ShapeDtypeStruct((copies, BLK), F32),
        ],
        scratch_shapes=[
            pltpu.VMEM(split.shape, BF16),
            pltpu.VMEM((3 * n, BLK, BLK), BF16),
            pltpu.SemaphoreType.DMA((n,)),
        ],
        compiler_params=pltpu.CompilerParams(vmem_limit_bytes=60 * 2**20),
        cost_estimate=pl.CostEstimate(flops=4 * 10**9, bytes_accessed=11 * 10**6, transcendentals=0),
        name="first_image",
    )(info, pattern, split, x, xs, across_odd, across_even, s)


def second_kernel(
    info, pat, a_hbm, ys_ref, ys_odd_ref, ys_even_ref, ps_ref, ps_odd_ref, ps_even_ref, s_ref, y_ref, p_ref,
    z_ref, image_ref, split_ref, turned, arrived,
):
    count = s_ref.shape[0]
    copies = loads(a_hbm, split_ref, arrived)
    turn_all(turned, info[3], ((ys_odd_ref, ps_odd_ref), (ys_ref, ps_ref), (ys_even_ref, ps_even_ref)), count)
    for i in range(count):
        lanes = slice(i * BLK, (i + 1) * BLK)
        wait_group(copies, i, GROUP)
        weights = gathered(info, pat, turned, i)
        product = jnp.dot(split_ref[i], weights, preferred_element_type=F32)
        image = (product[:BLK] + product[BLK:]).T
        s = s_ref[i : i + 1, :]
        z_ref[:, lanes] = y_ref[:, lanes] - s * (image[0:32] + image[32:64])
        image_ref[:, lanes] = p_ref[:, lanes] - s * (image[64:96] + image[96:128])


def second_image(info, pattern, split, ys, ys_odd, ys_even, ps, ps_odd, ps_even, s, y, p):
    n = s.shape[0]
    return pl.pallas_call(
        second_kernel,
        in_specs=memory(pltpu.SMEM, pltpu.SMEM, pl.ANY, *[pltpu.VMEM] * 9),
        out_shape=[jax.ShapeDtypeStruct(y.shape, F32)] * 2,
        scratch_shapes=[
            pltpu.VMEM(split.shape, BF16),
            pltpu.VMEM((3 * n, BLK, BLK), BF16),
            pltpu.SemaphoreType.DMA((n,)),
        ],
        compiler_params=pltpu.CompilerParams(vmem_limit_bytes=60 * 2**20),
        cost_estimate=pl.CostEstimate(flops=4 * 10**9, bytes_accessed=14 * 10**6, transcendentals=0),
        name="second_image",
    )(info, pattern, split, ys, ys_odd, ys_even, ps, ps_odd, ps_even, s, y, p)


def products_kernel(
    info, sums_ref, x_ref, y_ref, p_ref, xo_ref, yo_ref, po_ref, z_ref, image_ref, high_ref, low_ref, out_ref, quotients, left_ref, acc
):
    core = info[0]
    own = pl.multiple_of(core * 32, 32)
    other = pl.multiple_of((1 - core) * 32, 32)
    sums = jnp.sum(sums_ref[...], axis=0, keepdims=True)
    column = jnp.broadcast_to(sums, (BLK, BLK)).T
    quotients[0:32] = column[0:32] / column[32:64]
    quotients[32:64] = column[64:96] / column[96:128]
    q_own = quotients[pl.ds(own, 32), :]
    q_other = quotients[pl.ds(other, 32), :]
    for i in range(x_ref.shape[1] // BLK):
        lanes = slice(i * BLK, (i + 1) * BLK)
        place = slice(i % CHUNK * BLK, (i % CHUNK + 1) * BLK)
        x, y = x_ref[:, lanes], y_ref[:, lanes]
        rows = (y - q_own * x, x, p_ref[:, lanes], z_ref[:, lanes] - q_own * y, y, image_ref[:, lanes])
        for at, v in enumerate(rows):
            high, low = halves(v)
            left_ref[32 * at : 32 * at + 32, place] = high
            left_ref[192 + 32 * at : 224 + 32 * at, place] = low
            if at < 3:
                high_ref[pl.ds(64 * at + own, 32), lanes] = high
                low_ref[pl.ds(64 * at + own, 32), lanes] = low
        xo = xo_ref[:, lanes]
        for at, v in enumerate((yo_ref[:, lanes] - q_other * xo, xo, po_ref[:, lanes])):
            high, low = halves(v)
            high_ref[pl.ds(64 * at + other, 32), lanes] = high
            low_ref[pl.ds(64 * at + other, 32), lanes] = low
        if i % CHUNK == CHUNK - 1:
            span = slice((i + 1 - CHUNK) * BLK, (i + 1) * BLK)
            dims = (((1,), (1,)), ((), ()))
            left = left_ref[...]
            part = lax.dot_general(left, high_ref[:, span], dims, preferred_element_type=F32)
            part = part + lax.dot_general(left, low_ref[:, span], dims, preferred_element_type=F32)
            acc[...] = part if i < CHUNK else acc[...] + part

    total = acc[0:192] + acc[192:384]
    out_ref[0:192, :] = total[:, 0:BLK]
    out_ref[192:384, :] = jnp.concatenate([total[:, BLK:192], jnp.zeros((192, 64), F32)], axis=1)


def products(info, sums, x, y, p, xo, yo, po, z, image):
    return pl.pallas_call(
        products_kernel,
        in_specs=memory(pltpu.SMEM, *[pltpu.VMEM] * 9),
        out_shape=[jax.ShapeDtypeStruct((192, x.shape[1]), BF16)] * 2 + [jax.ShapeDtypeStruct((384, BLK), F32)],
        scratch_shapes=[
            pltpu.VMEM((64, BLK), F32),
            pltpu.VMEM((384, CHUNK * BLK), BF16),
            pltpu.VMEM((384, 192), F32),
        ],
        compiler_params=pltpu.CompilerParams(vmem_limit_bytes=60 * 2**20),
        cost_estimate=pl.CostEstimate(flops=2 * 10**9, bytes_accessed=6 * 10**6, transcendentals=0),
        name="products",
    )(info, sums, x, y, p, xo, yo, po, z, image)


def picked_row(groups, at):
    return jnp.broadcast_to(groups[at // 8][at % 8 : at % 8 + 1, :], (8, BLK))


def inverse_factor(block):
    lane = lax.broadcasted_iota(jnp.int32, (8, BLK), 1)
    sub = lax.broadcasted_iota(jnp.int32, (8, BLK), 0)
    tall = PIECE // 8
    a = []
    for g in range(tall):
        unit = jnp.where(lane - PIECE == sub + 8 * g, 1.0, 0.0)
        a.append(jnp.where(lane < PIECE, block[8 * g : 8 * g + 8, :], unit))
    for start in range(0, PIECE, PIVOTS):
        columns = [
            [jnp.broadcast_to(a[g][:, start + k : start + k + 1], (8, BLK)) if g >= start // 8 else None for g in range(tall)]
            for k in range(PIVOTS)
        ]
        for k in range(PIVOTS):
            at = start + k
            own = at // 8
            pivot = 1.0 / picked_row(columns[k], at)
            factor = [columns[k][g] * pivot if g >= own else None for g in range(tall)]
            factor[own] = jnp.where(sub > at % 8, factor[own], 0.0)
            for other in columns[k + 1 :]:
                e = picked_row(other, at)
                for g in range(own, tall):
                    other[g] = other[g] - factor[g] * e
            row = picked_row(a, at)
            for g in range(own, tall):
                a[g] = a[g] - factor[g] * row
    scaled = []
    for g in range(tall):
        diagonal = jnp.sum(jnp.where(lane == sub + 8 * g, a[g], 0.0), axis=1, keepdims=True)
        scaled.append(a[g] * lax.rsqrt(diagonal))
    return jnp.concatenate(scaled, axis=0)[:, PIECE : 2 * PIECE]


def exact(left, right, dims):
    return lax.dot_general(left, right, (dims, ((), ())), precision=EXACT, preferred_element_type=F32)


def inverse_cholesky(work, inverse):
    lane = lax.broadcasted_iota(jnp.int32, (PIECE, 192), 1)
    sub = lax.broadcasted_iota(jnp.int32, (PIECE, 192), 0)
    for at in range(0, 192, PIECE):
        rows = work[at : at + PIECE, :]
        if at < BLK:
            piece = rows[:, 0:BLK]
        else:
            piece = jnp.concatenate([rows[:, BLK:192], jnp.zeros((PIECE, 64), F32)], axis=1)
        if at % BLK:
            piece = pltpu.roll(piece, BLK - at % BLK, 1)
        small = inverse_factor(piece)
        unit = jnp.where(lane - at == sub, 1.0, 0.0)
        rows = jnp.where((lane >= at) & (lane < at + PIECE), unit, rows)
        new = exact(small, rows, ((1,), (0,)))
        inverse[at : at + PIECE, :] = jnp.where(lane < at + PIECE, new, 0.0)
        if at + PIECE < 192:
            update = exact(new, new, ((0,), (0,)))
            wide = lax.broadcasted_iota(jnp.int32, (192 - PIECE - at, 192), 1)
            old = jnp.where((wide >= at) & (wide < at + PIECE), 0.0, work[at + PIECE : 192, :])
            work[at + PIECE : 192, :] = old - update[at + PIECE : 192, :]


def final_kernel(
    info, summed_ref, theirs_ref, chosen_ref, high_hbm, low_hbm, vectors_ref, directions_ref, ritz_ref,
    high_ref, low_ref, work, raw, inverse, arrived, *, factor
):
    copies = [
        pltpu.make_async_copy(high_hbm, high_ref, arrived.at[0]),
        pltpu.make_async_copy(low_hbm, low_ref, arrived.at[1]),
    ]
    for copy in copies:
        copy.start()
    first = info[0] == 0
    for at in range(6):
        mine = first if at % 2 == 0 else jnp.logical_not(first)
        for base, target in ((0, work), (96, raw)):
            row = base + 32 * (at // 2)
            head, tail = slice(row, row + 32), slice(row + 192, row + 224)
            target[32 * at : 32 * at + 32, 0:BLK] = jnp.where(mine, summed_ref[head, :], theirs_ref[head, :])
            target[32 * at : 32 * at + 32, BLK:192] = jnp.where(mine, summed_ref[tail, 0:64], theirs_ref[tail, 0:64])
    inverse_cholesky(work, inverse)
    whole_inverse = inverse[...]
    half = exact(whole_inverse, raw[...], ((1,), (1,)))
    ritz_ref[...] = exact(half, whole_inverse, ((1,), (1,)))
    mix = factor * exact(chosen_ref[...], whole_inverse, ((1,), (0,)))
    left = jnp.concatenate(halves(mix), axis=0)
    for copy in copies:
        copy.wait()
    for at in range(0, high_ref.shape[1], 512):
        lanes = slice(at, at + 512)
        product = jnp.dot(left, high_ref[:, lanes], preferred_element_type=F32)
        product = product + jnp.dot(left, low_ref[:, lanes], preferred_element_type=F32)
        product = product[0:64] + product[64:128]
        vectors_ref[:, lanes] = product[0:32]
        directions_ref[:, lanes] = product[32:64]


def final(info, summed, theirs, chosen, high, low, factor):
    return pl.pallas_call(
        functools.partial(final_kernel, factor=factor),
        in_specs=memory(pltpu.SMEM, pltpu.VMEM, pltpu.VMEM, pltpu.VMEM, pl.ANY, pl.ANY),
        out_shape=[jax.ShapeDtypeStruct((32, high.shape[1]), F32)] * 2 + [jax.ShapeDtypeStruct((192, 192), F32)],
        scratch_shapes=[pltpu.VMEM(high.shape, BF16)] * 2 + [pltpu.VMEM((192, 192), F32)] * 3 + [pltpu.SemaphoreType.DMA((2,))],
        compiler_params=pltpu.CompilerParams(vmem_limit_bytes=52 * 2**20),
        cost_estimate=pl.CostEstimate(flops=4 * 10**8, bytes_accessed=4 * 10**6, transcendentals=0),
        name="final",
    )(info, summed, theirs, chosen, high, low)


def other_core(x):
    return lax.ppermute(x, "cols", [(0, 1), (1, 0)])


def local(vectors, directions, affinity, pattern, rotation):
    width, rows_dev = vectors.shape
    devices = lax.axis_size("rows")
    core = lax.axis_index("cols")
    total = 2 * width
    nodes = rows_dev * devices
    local_blocks = affinity.shape[0]
    all_blocks = local_blocks * devices
    place = lax.axis_index("rows")
    first_block = (place - 1) * local_blocks
    info = jnp.stack([core, first_block, jnp.int32(all_blocks), place % 2]).astype(jnp.int32)
    columns = pattern.T
    scale, xs = degrees(affinity, vectors)
    xs_odd, xs_even = from_neighbours(xs)
    split, ps = split_affinity(affinity, scale, directions)
    ps_odd, ps_even = from_neighbours(ps)
    x_other = other_core(vectors)
    p_other = other_core(directions)
    y, ys, sums = first_image(info, columns, split, vectors, xs, xs_odd, xs_even, scale, 2 * devices)
    ys_odd, ys_even = from_neighbours(ys)
    y_other = other_core(y)
    sums = lax.all_to_all(sums.reshape(2 * devices, 1, BLK), ("rows", "cols"), 0, 0).reshape(2 * devices, BLK)
    z, image = second_image(info, columns, split, ys, ys_odd, ys_even, ps, ps_odd, ps_even, scale, y, directions)
    high, low, part = products(info, sums, vectors, y, directions, x_other, y_other, p_other, z, image)
    summed = sum_large(part.reshape(16, 24, BLK)).reshape(384, BLK)
    theirs = other_core(summed)
    mine = lambda m: lax.dynamic_slice_in_dim(m, core * width, width, 1)
    kept = jnp.concatenate([rotation[:total], jnp.zeros((total, total), F32), rotation[2 * total :]], axis=0)
    chosen = jnp.concatenate([mine(rotation), mine(kept)], axis=1).T
    new_vectors, new_directions, ritz_matrix = final(info, summed, theirs, chosen, high, low, math.sqrt(nodes))
    return new_vectors, new_directions, ritz_matrix


def solution(mesh):
    in_specs = (P("cols", "rows"), P("cols", "rows"), P("rows", None, None, None), P("rows", None), P())
    out_specs = (P("cols", "rows"), P("cols", "rows"), P())
    return jax.shard_map(local, mesh=mesh, in_specs=in_specs, out_specs=out_specs, check_vma=False)
```
